32 devices in a mesh: dp: 16 (over z, y, core), tensor: 2 (over x).
Axes of the slice: x: 2, y: 2, z: 4, core: 2. Of those that a mesh axis runs over, the one named last changes fastest.
Arguments:
- inputs: bfloat16 [16384, 768], P(('dp', 'tensor')), may hold values from -6 to 6
- lengths: int32 [32], P('dp'), may hold values from 128 to 512, as said below
- teacher_query_weight: bfloat16 [768, 768], P('dp', 'tensor'), may hold values from -0.21875 to 0.21875
- teacher_query_bias: bfloat16 [2, 384], P('tensor', 'dp'), may hold values from -3 to 3
- teacher_key_weight: bfloat16 [768, 768], P('dp', 'tensor'), may hold values from -0.21875 to 0.21875
- teacher_value_weight: bfloat16 [768, 768], P('dp', 'tensor'), may hold values from -0.21875 to 0.21875
- teacher_value_bias: bfloat16 [2, 384], P('tensor', 'dp'), may hold values from -0.29882812 to 0.29882812
- teacher_output_weight: bfloat16 [768, 768], P('tensor', 'dp'), may hold values from -2.5 to 2.5
- teacher_output_bias: float32 [768], P(('dp', 'tensor')), may hold values from -3 to 3
- teacher_first_gain: float32 [768], P(('dp', 'tensor')), may hold values from 0.1 to 1.9
- teacher_first_shift: float32 [768], P(('dp', 'tensor')), may hold values from -3 to 3
- teacher_up_weight: bfloat16 [768, 3072], P('dp', 'tensor'), may hold values from -0.21875 to 0.21875
- teacher_up_bias: bfloat16 [2, 1536], P('tensor', 'dp'), may hold values from -3 to 3
- teacher_down_weight: bfloat16 [3072, 768], P('tensor', 'dp'), may hold values from -0.109375 to 0.109375
- teacher_down_bias: float32 [768], P(('dp', 'tensor')), may hold values from -3 to 3
- teacher_second_gain: float32 [768], P(('dp', 'tensor')), may hold values from 0.1 to 1.9
- teacher_second_shift: float32 [768], P(('dp', 'tensor')), may hold values from -3 to 3
- student_query_weight: bfloat16 [768, 768], P('dp', 'tensor'), may hold values from -0.21875 to 0.21875
- student_query_bias: bfloat16 [2, 384], P('tensor', 'dp'), may hold values from -3 to 3
- student_key_weight: bfloat16 [768, 768], P('dp', 'tensor'), may hold values from -0.21875 to 0.21875
- student_value_weight: bfloat16 [768, 768], P('dp', 'tensor'), may hold values from -0.21875 to 0.21875
- student_value_bias: bfloat16 [2, 384], P('tensor', 'dp'), may hold values from -0.29882812 to 0.29882812
- student_output_weight: bfloat16 [768, 768], P('tensor', 'dp'), may hold values from -2.5 to 2.5
- student_output_bias: float32 [768], P(('dp', 'tensor')), may hold values from -3 to 3
- student_first_gain: float32 [768], P(('dp', 'tensor')), may hold values from 0.1 to 1.9
- student_first_shift: float32 [768], P(('dp', 'tensor')), may hold values from -3 to 3
- student_up_weight: bfloat16 [768, 3072], P('dp', 'tensor'), may hold values from -0.21875 to 0.21875
- student_up_bias: bfloat16 [2, 1536], P('tensor', 'dp'), may hold values from -3 to 3
- student_down_weight: bfloat16 [3072, 768], P('tensor', 'dp'), may hold values from -0.109375 to 0.109375
- student_down_bias: float32 [768], P(('dp', 'tensor')), may hold values from -3 to 3
- student_second_gain: float32 [768], P(('dp', 'tensor')), may hold values from 0.1 to 1.9
- student_second_shift: float32 [768], P(('dp', 'tensor')), may hold values from -3 to 3
- grad_out: bfloat16 [16384, 768], P(('dp', 'tensor')), may hold values from -6 to 6
Outputs:
- activations: bfloat16 [16384, 768], P(('dp', 'tensor'))
- input_grad: float32 [16384, 768], P(('dp', 'tensor'))
- teacher_query_weight_grad: float32 [768, 768], P('dp', 'tensor')
- teacher_query_bias_grad: float32 [2, 384], P('tensor', 'dp')
- teacher_key_weight_grad: float32 [768, 768], P('dp', 'tensor')
- teacher_value_weight_grad: float32 [768, 768], P('dp', 'tensor')
- teacher_value_bias_grad: float32 [2, 384], P('tensor', 'dp')
- teacher_output_weight_grad: float32 [768, 768], P('tensor', 'dp')
- teacher_output_bias_grad: float32 [768], P(('dp', 'tensor'))
- teacher_first_gain_grad: float32 [768], P(('dp', 'tensor'))
- teacher_first_shift_grad: float32 [768], P(('dp', 'tensor'))
- teacher_up_weight_grad: float32 [768, 3072], P('dp', 'tensor')
- teacher_up_bias_grad: float32 [2, 1536], P('tensor', 'dp')
- teacher_down_weight_grad: float32 [3072, 768], P('tensor', 'dp')
- teacher_down_bias_grad: float32 [768], P(('dp', 'tensor'))
- teacher_second_gain_grad: float32 [768], P(('dp', 'tensor'))
- teacher_second_shift_grad: float32 [768], P(('dp', 'tensor'))
- student_query_weight_grad: float32 [768, 768], P('dp', 'tensor')
- student_query_bias_grad: float32 [2, 384], P('tensor', 'dp')
- student_key_weight_grad: float32 [768, 768], P('dp', 'tensor')
- student_value_weight_grad: float32 [768, 768], P('dp', 'tensor')
- student_value_bias_grad: float32 [2, 384], P('tensor', 'dp')
- student_output_weight_grad: float32 [768, 768], P('tensor', 'dp')
- student_output_bias_grad: float32 [768], P(('dp', 'tensor'))
- student_first_gain_grad: float32 [768], P(('dp', 'tensor'))
- student_first_shift_grad: float32 [768], P(('dp', 'tensor'))
- student_up_weight_grad: float32 [768, 3072], P('dp', 'tensor')
- student_up_bias_grad: float32 [2, 1536], P('tensor', 'dp')
- student_down_weight_grad: float32 [3072, 768], P('tensor', 'dp')
- student_down_bias_grad: float32 [768], P(('dp', 'tensor'))
- student_second_gain_grad: float32 [768], P(('dp', 'tensor'))
- student_second_shift_grad: float32 [768], P(('dp', 'tensor'))
The draws below stay inside these ranges and needn't reach their ends.
Inputs may be any that keep to these rules, and one draw needn't show every extreme that they name: Sequence s holds valid tokens in its first lengths[s] of 512 slots, the rest is padding; some sequence is full and some has 128.
All inputs are finite; a program needn't handle non-finite values.
Results may differ from the reference program's by a relative error of at most 0.039.
Values may be sent and summed in bfloat16 or wider, within the bound.
A program may use at most 192 MiB of HBM per device.

```python
import math
import jax
import jax.numpy as jnp
from jax import lax

D = 768
HEADS = 12
HEAD = 64
FF = 3072
LEN = 512
SEQS = 2
SEQUENCES = 32
TOKENS = 16384
N_DP = 16
N_TENSOR = 2


def draw_lengths(key, part):
    first_key, second_key, third_key = jax.random.split(jax.random.fold_in(key, 11), 3)
    base = jax.random.randint(first_key, (SEQUENCES,), LEN // 4, LEN + 1)
    full_at = jax.random.randint(second_key, (), 0, SEQUENCES)
    short_at = (full_at + jax.random.randint(third_key, (), 1, SEQUENCES)) % SEQUENCES
    places = jnp.arange(SEQUENCES)
    base = jnp.where(places == full_at, LEN, base)
    base = jnp.where(places == short_at, LEN // 4, base)
    return base.astype(jnp.int32)


def with_spikes(values, key, source, target, parts, factor):
    owner, partner = [(jnp.arange(values.shape[axis_at]) // (values.shape[axis_at] // parts)).reshape([-1 if axis == axis_at else 1 for axis in range(values.ndim)]) for axis_at in (source, target)]
    chosen = jax.random.permutation(key, parts)[partner]
    strong = (owner == chosen) | (owner == (partner + parts // 2) % parts)
    return jnp.where(strong, factor * values, values)


def levels(key, dims, cuts, smallest, high):
    def one(axis_at, parts):
        steps = jax.random.uniform(jax.random.fold_in(jax.random.fold_in(key, 6), axis_at), (parts,), jnp.float32, smallest / len(cuts), high / len(cuts))
        return jnp.repeat(jnp.exp(steps), dims[axis_at] // parts).reshape((-1,) + (1,) * (len(dims) - axis_at - 1))

    factor_of = one(*cuts[0])
    for cut in cuts[1:]:
        factor_of = factor_of * one(*cut)
    return factor_of


def noise(stream_key, dims, width, limit, cuts=(), held_as=jnp.bfloat16):
    loudness = levels(stream_key, dims, cuts, -0.22, 0.18) if cuts else 1.0
    values = jax.random.normal(stream_key, dims, jnp.float32) * width * loudness
    return jnp.minimum(jnp.maximum(values, -limit), limit).astype(held_as)


def noise_with(stream_key, extent, scale, most, cuts, heavy, held_as=jnp.bfloat16):
    values = scale * jax.random.normal(stream_key, extent, jnp.float32)
    if cuts:
        values = values * levels(stream_key, extent, cuts, -0.22, 0.18)
    return jnp.clip(with_spikes(values, jax.random.fold_in(stream_key, 3), *heavy), -most, most).astype(held_as)


def setup_inputs(seed: int = 0) -> dict:
    key_of = jax.random.split(jax.random.key(seed), 34)
    inputs = noise(key_of[0], (TOKENS, D), 1.0, 6.0, ((0, 32),))
    lengths = draw_lengths(jax.random.fold_in(key_of[33], 71), 0)
    teacher_query_weight = noise(key_of[2], (D, D), D ** -0.5, 0.21875, ((0, 16), (1, 2)))
    teacher_query_bias = noise(key_of[3], (N_TENSOR, D // N_TENSOR), 0.5, 3.0, ((0, 2), (1, 16)))
    teacher_key_weight = noise(key_of[4], (D, D), D ** -0.5, 0.21875, ((0, 16), (1, 2)))
    teacher_value_weight = noise(key_of[5], (D, D), D ** -0.5, 0.21875, ((0, 16), (1, 2)))
    teacher_value_bias = noise(key_of[6], (N_TENSOR, D // N_TENSOR), 0.05, 0.29882812, ((0, 2), (1, 16)))
    teacher_output_weight = noise(key_of[7], (D, D), (max(D * 4 // LEN, 1)) ** -0.5, 2.5, ((0, 2), (1, 16)))
    teacher_output_bias = noise(key_of[8], (D,), 0.5, 3.0, ((0, 32),), jnp.float32)
    teacher_first_gain = jnp.clip(1.0 + 0.18 * jax.random.normal(key_of[9], (D,), jnp.float32), 0.1, 1.9)
    teacher_first_shift = noise(key_of[10], (D,), 0.5, 3.0, ((0, 32),), jnp.float32)
    teacher_up_weight = noise(key_of[11], (D, FF), D ** -0.5, 0.21875, ((0, 16), (1, 2)))
    teacher_up_bias = noise(key_of[12], (N_TENSOR, FF // N_TENSOR), 0.5, 3.0, ((0, 2), (1, 16)))
    teacher_down_weight = noise(key_of[13], (FF, D), FF ** -0.5, 0.109375, ((0, 2), (1, 16)))
    teacher_down_bias = noise(key_of[14], (D,), 0.5, 3.0, ((0, 32),), jnp.float32)
    teacher_second_gain = jnp.clip(1.0 + 0.18 * jax.random.normal(key_of[15], (D,), jnp.float32), 0.1, 1.9)
    teacher_second_shift = noise(key_of[16], (D,), 0.5, 3.0, ((0, 32),), jnp.float32)
    student_query_weight = noise(key_of[17], (D, D), D ** -0.5, 0.21875, ((0, 16), (1, 2)))
    student_query_bias = noise(key_of[18], (N_TENSOR, D // N_TENSOR), 0.5, 3.0, ((0, 2), (1, 16)))
    student_key_weight = noise(key_of[19], (D, D), D ** -0.5, 0.21875, ((0, 16), (1, 2)))
    student_value_weight = noise(key_of[20], (D, D), D ** -0.5, 0.21875, ((0, 16), (1, 2)))
    student_value_bias = noise(key_of[21], (N_TENSOR, D // N_TENSOR), 0.05, 0.29882812, ((0, 2), (1, 16)))
    student_output_weight = noise(key_of[22], (D, D), (max(D * 4 // LEN, 1)) ** -0.5, 2.5, ((0, 2), (1, 16)))
    student_output_bias = noise(key_of[23], (D,), 0.5, 3.0, ((0, 32),), jnp.float32)
    student_first_gain = jnp.clip(1.0 + 0.18 * jax.random.normal(key_of[24], (D,), jnp.float32), 0.1, 1.9)
    student_first_shift = noise(key_of[25], (D,), 0.5, 3.0, ((0, 32),), jnp.float32)
    student_up_weight = noise(key_of[26], (D, FF), D ** -0.5, 0.21875, ((0, 16), (1, 2)))
    student_up_bias = noise(key_of[27], (N_TENSOR, FF // N_TENSOR), 0.5, 3.0, ((0, 2), (1, 16)))
    student_down_weight = noise(key_of[28], (FF, D), FF ** -0.5, 0.109375, ((0, 2), (1, 16)))
    student_down_bias = noise(key_of[29], (D,), 0.5, 3.0, ((0, 32),), jnp.float32)
    student_second_gain = jnp.clip(1.0 + 0.18 * jax.random.normal(key_of[30], (D,), jnp.float32), 0.1, 1.9)
    student_second_shift = noise(key_of[31], (D,), 0.5, 3.0, ((0, 32),), jnp.float32)
    grad_out = noise_with(key_of[32], (TOKENS, D), 1.0, 6.0, ((0, 32),), (0, 1, 32, 2.75))
    return dict(inputs=inputs, lengths=lengths, teacher_query_weight=teacher_query_weight, teacher_query_bias=teacher_query_bias, teacher_key_weight=teacher_key_weight, teacher_value_weight=teacher_value_weight, teacher_value_bias=teacher_value_bias, teacher_output_weight=teacher_output_weight, teacher_output_bias=teacher_output_bias, teacher_first_gain=teacher_first_gain, teacher_first_shift=teacher_first_shift, teacher_up_weight=teacher_up_weight, teacher_up_bias=teacher_up_bias, teacher_down_weight=teacher_down_weight, teacher_down_bias=teacher_down_bias, teacher_second_gain=teacher_second_gain, teacher_second_shift=teacher_second_shift, student_query_weight=student_query_weight, student_query_bias=student_query_bias, student_key_weight=student_key_weight, student_value_weight=student_value_weight, student_value_bias=student_value_bias, student_output_weight=student_output_weight, student_output_bias=student_output_bias, student_first_gain=student_first_gain, student_first_shift=student_first_shift, student_up_weight=student_up_weight, student_up_bias=student_up_bias, student_down_weight=student_down_weight, student_down_bias=student_down_bias, student_second_gain=student_second_gain, student_second_shift=student_second_shift, grad_out=grad_out)


@jax.custom_vjp
def low(v):
    return lax.optimization_barrier(v.astype(jnp.bfloat16)).astype(jnp.float32)

@jax.custom_vjp
def low_back(v):
    return v

def low_keep(v):
    return (low(v), None)

def low_pass(kept, grad):
    return (grad,)

def back_keep(v):
    return (v, None)

def back_low(kept, grad):
    return (low(grad),)
low.defvjp(low_keep, low_pass)
low_back.defvjp(back_keep, back_low)
EPS = 1e-06
NEG = -1e+30
HIGH = lax.Precision.HIGHEST

def product(first_op, second_op):
    return jnp.dot(first_op, second_op, precision=HIGH, preferred_element_type=jnp.float32)

def layer_norm(residual, norm_gain, norm_shift):
    average = lax.optimization_barrier(jnp.mean(residual, axis=-1, keepdims=True))
    centred = residual - average
    variance = lax.optimization_barrier(jnp.mean(centred * centred, axis=-1, keepdims=True))
    return centred * lax.rsqrt(variance + EPS) * norm_gain + norm_shift

def attend_one(item):
    queries, key_rows, value_rows, valid_keys = item
    raw_scores = jnp.einsum('qhd,khd->hqk', queries, key_rows, precision=HIGH)
    scores = low_back(jnp.where(valid_keys[None, None, :], raw_scores * HEAD ** (-0.5), NEG))
    row_max = lax.optimization_barrier(jnp.max(scores, axis=-1, keepdims=True))
    exponent = jnp.exp(scores - row_max)
    attn_probs = low(exponent / lax.optimization_barrier(jnp.sum(exponent, axis=-1, keepdims=True)))
    return jnp.einsum('hqk,khd->qhd', attn_probs, value_rows, precision=HIGH)

def run_layer(layer_in, valid_keys, params):
    query_w, query_b, key_w, value_w, value_b, out_w, out_b, gain_one, shift_one, up_w, up_b, down_w, down_b, gain_two, shift_two = params
    split_shape = (valid_keys.shape[0], LEN, HEADS, HEAD)
    queries = low_back(low(product(layer_in, query_w) + query_b))
    key_rows = low_back(low(product(layer_in, key_w)))
    value_rows = low_back(low(product(layer_in, value_w) + value_b))
    attended = lax.map(jax.checkpoint(attend_one), (queries.reshape(split_shape), key_rows.reshape(split_shape), value_rows.reshape(split_shape), valid_keys))
    attended = low_back(low(attended.reshape(layer_in.shape[0], D)))
    branch = low_back(product(attended, out_w))
    hidden = low(layer_norm(layer_in + branch + out_b, gain_one, shift_one))
    upward = low_back(product(hidden, up_w) + up_b)
    active = low(jax.nn.gelu(upward, approximate=False))
    downward = low_back(product(active, down_w))
    return layer_norm(hidden + downward + down_b, gain_two, shift_two)

def forward(layer_in, valid_keys, teacher, student):
    row_mask = valid_keys.reshape(-1, 1).astype(jnp.float32)
    teacher_out = low(run_layer(layer_in, valid_keys, teacher))
    return run_layer(teacher_out, valid_keys, student) * row_mask

def prepare(arrays):
    return tuple((arrays[index].astype(jnp.float32).reshape(-1) if index in (1, 4, 10) else arrays[index].astype(jnp.float32) for index in range(15)))

def reference(inputs, lengths, teacher_query_weight, teacher_query_bias, teacher_key_weight, teacher_value_weight, teacher_value_bias, teacher_output_weight, teacher_output_bias, teacher_first_gain, teacher_first_shift, teacher_up_weight, teacher_up_bias, teacher_down_weight, teacher_down_bias, teacher_second_gain, teacher_second_shift, student_query_weight, student_query_bias, student_key_weight, student_value_weight, student_value_bias, student_output_weight, student_output_bias, student_first_gain, student_first_shift, student_up_weight, student_up_bias, student_down_weight, student_down_bias, student_second_gain, student_second_shift, grad_out):
    teacher_args = (teacher_query_weight, teacher_query_bias, teacher_key_weight, teacher_value_weight, teacher_value_bias, teacher_output_weight, teacher_output_bias, teacher_first_gain, teacher_first_shift, teacher_up_weight, teacher_up_bias, teacher_down_weight, teacher_down_bias, teacher_second_gain, teacher_second_shift)
    student_args = (student_query_weight, student_query_bias, student_key_weight, student_value_weight, student_value_bias, student_output_weight, student_output_bias, student_first_gain, student_first_shift, student_up_weight, student_up_bias, student_down_weight, student_down_bias, student_second_gain, student_second_shift)
    teacher = prepare(teacher_args)
    student = prepare(student_args)
    seq_count = SEQS * N_DP
    bundle = math.gcd(seq_count, max(1, 4096 // LEN))
    step_count = seq_count // bundle
    valid_all = (jnp.arange(LEN)[None, :] < lengths[:, None]).reshape(step_count, bundle, LEN)
    inputs_all = inputs.astype(jnp.float32).reshape(step_count, bundle * LEN, D)
    grads_all = grad_out.astype(jnp.float32).reshape(step_count, bundle * LEN, D)

    def one_step(summed, item):
        input_part, grad_part, valid_keys = item

        def apply_all(layer_in, teacher_params, student_params):
            return forward(layer_in, valid_keys, teacher_params, student_params)
        result, back_fn = jax.vjp(apply_all, input_part, teacher, student)
        d_input, d_teacher, d_student = back_fn(grad_part)
        summed = jax.tree.map(lambda first_op, second_op: first_op + second_op, summed, (d_teacher, d_student))
        return (summed, (result.astype(jnp.bfloat16), d_input))
    zeros_init = jax.tree.map(jnp.zeros_like, (teacher, student))
    (d_teacher, d_student), (results, d_inputs) = lax.scan(one_step, zeros_init, (inputs_all, grads_all, valid_all))
    every_arg = teacher_args + student_args
    every_grad = d_teacher + d_student
    shaped = [every_grad[index].reshape(every_arg[index].shape) for index in range(30)]
    return (results.reshape(-1, D), d_inputs.reshape(-1, D), shaped[0], shaped[1], shaped[2], shaped[3], shaped[4], shaped[5], shaped[6], shaped[7], shaped[8], shaped[9], shaped[10], shaped[11], shaped[12], shaped[13], shaped[14], shaped[15], shaped[16], shaped[17], shaped[18], shaped[19], shaped[20], shaped[21], shaped[22], shaped[23], shaped[24], shaped[25], shaped[26], shaped[27], shaped[28], shaped[29])
```

```python
import functools

import jax
import jax.numpy as jnp
from jax import lax
from jax.experimental import pallas as pl
from jax.experimental.pallas import tpu as pltpu
from jax.sharding import PartitionSpec as P

HEAD = 64
EPS = 1e-06
NEG = -1e30
WAVES = 6
NZ, NY, NC, NX = 4, 2, 2, 2
MESH = pl.DeviceIdType.MESH
BF = jnp.bfloat16
F32 = jnp.float32
AXES = ("dp", "tensor")


def place():
    dp = lax.axis_index("dp")
    t = lax.axis_index("tensor")
    return dp // 4, lax.rem(dp // 2, 2), lax.rem(dp, 2), t


def device(z, y, c, t):
    return {"dp": z * 4 + y * 2 + c, "tensor": t}


def greet(others):
    barrier = pltpu.get_barrier_semaphore()
    for other in others:
        pl.semaphore_signal(barrier, inc=1, device_id=other, device_id_type=MESH)
    pl.semaphore_wait(barrier, len(others))


def send(src, dst, sems, index, other):
    copy = pltpu.make_async_remote_copy(
        src_ref=src,
        dst_ref=dst,
        send_sem=sems[0].at[index],
        recv_sem=sems[1].at[index],
        device_id=other,
        device_id_type=MESH,
    )
    copy.start()
    return copy


def partners():
    z, y, c, t = place()
    core = device(z, y, 1 - c, t)
    over_x = device(z, y, c, 1 - t)
    over_y = device(z, 1 - y, c, t)
    over_z = [device(lax.rem(z + j, NZ), y, c, t) for j in range(1, NZ)]
    return core, over_x, over_y, over_z


def small_sum(src, dst, got, acc, sems):
    core, over_x, over_y, over_z = partners()
    now = src
    for step, other in enumerate((core, over_x, over_y)):
        send(now, got.at[step], sems, step, other).wait()
        acc[step] = now[...] + got[step]
        now = acc.at[step]
    copies = [send(now, got.at[3 + j], sems, 3 + j, other) for j, other in enumerate(over_z)]
    for copy in copies:
        copy.wait()
    dst[...] = now[...] + got[3] + got[4] + got[5]


def gather_kernel(shard, small, full, small_out, got, acc, s_send, s_recv, own_sem, b_send, b_recv):
    z, y, c, t = place()
    core, over_x, over_y, over_z = partners()
    greet([core, over_x, over_y] + over_z)
    half = shard.shape[2] // 2
    lo, hi = pl.ds(0, half), pl.ds(half, half)
    sems = (b_send, b_recv)
    owns, first, second, third, last = {}, {}, {}, {}, {}

    def start_first(k):
        owns[k] = pltpu.make_async_copy(shard.at[k], full.at[k, t, z, y, c], own_sem.at[k])
        owns[k].start()
        first[k] = [
            send(shard.at[k], full.at[k, t, z, y, c], sems, (k, j), other)
            for j, other in enumerate(over_z)
        ]

    def start_second(k):
        owns[k].wait()
        for copy in first[k]:
            copy.wait()
        a = full.at[k, t, :, y, c, :, lo]
        b = full.at[k, t, :, y, c, :, hi]
        second[k] = [send(a, a, sems, (k, 3), over_y), send(b, b, sems, (k, 4), over_x)]

    def start_third(k):
        for copy in second[k]:
            copy.wait()
        a = full.at[k, t, :, :, c, :, lo]
        b = full.at[k, :, :, y, c, :, hi]
        third[k] = [send(a, a, sems, (k, 5), over_x), send(b, b, sems, (k, 6), over_y)]

    def start_last(k):
        for copy in third[k]:
            copy.wait()
        a = full.at[k, :, :, :, c]
        last[k] = send(a, a, sems, (k, 7), core)

    start_first(0)
    start_first(1)
    small_sum(small, small_out, got, acc, (s_send, s_recv))
    for step in range(WAVES + 2):
        if step < WAVES:
            start_second(step)
            if step + 2 < WAVES:
                start_first(step + 2)
        if 0 <= step - 1 < WAVES:
            start_third(step - 1)
        if 0 <= step - 2 < WAVES:
            start_last(step - 2)
    for k in range(WAVES):
        last[k].wait()


def gather_all(shard, small):
    waves, rows, cols = shard.shape
    dma = pltpu.SemaphoreType.DMA
    any_spec = pl.BlockSpec(memory_space=pl.ANY)
    vmem = pl.BlockSpec(memory_space=pltpu.VMEM)
    full, small_out = pl.pallas_call(
        gather_kernel,
        out_shape=(
            jax.ShapeDtypeStruct((waves, NX, NZ, NY, NC, rows, cols), BF),
            jax.ShapeDtypeStruct(small.shape, F32),
        ),
        in_specs=[any_spec, vmem],
        out_specs=(any_spec, vmem),
        scratch_shapes=[
            pltpu.VMEM((6,) + small.shape, F32),
            pltpu.VMEM((3,) + small.shape, F32),
            dma((6,)),
            dma((6,)),
            dma((waves,)),
            dma((waves, 8)),
            dma((waves, 8)),
        ],
        name="gather_all",
        compiler_params=pltpu.CompilerParams(
            collective_id=0, has_side_effects=True, vmem_limit_bytes=32 << 20
        ),
    )(shard, small)
    return full.reshape(waves, NX, NZ * NY * NC * rows, cols), small_out


def reduce_kernel(*refs):
    parts, refs = refs[:WAVES], refs[WAVES:]
    small, out, small_out, own, rc, r2a, r2b, r3a, r3b, r4, got, acc, s_send, s_recv, own_sem, b_send, b_recv = refs
    z, y, c, t = place()
    core, over_x, over_y, over_z = partners()
    greet([core, over_x, over_y] + over_z)
    half = out.shape[2] // 2
    lo, hi = pl.ds(0, half), pl.ds(half, half)
    sems = (b_send, b_recv)
    local, first, second, third, last = {}, {}, {}, {}, {}

    def start_first(k):
        local[k] = pltpu.make_async_copy(parts[k].at[:, :, :, c], own.at[k % 2], own_sem.at[k % 2])
        local[k].start()
        first[k] = send(parts[k].at[:, :, :, 1 - c], rc.at[k], sems, (k, 0), core)

    def start_second(k):
        local[k].wait()
        first[k].wait()

        @pl.loop(0, NZ)
        def _(i):
            for a in range(NX):
                for b in range(NY):
                    rc[k, a, i, b] = rc[k, a, i, b] + own[k % 2, a, i, b]

        second[k] = [
            send(rc.at[k, 1 - t, :, :, :, lo], r2a.at[k], sems, (k, 1), over_x),
            send(rc.at[k, :, :, 1 - y, :, hi], r2b.at[k], sems, (k, 2), over_y),
        ]

    def start_third(k):
        for copy in second[k]:
            copy.wait()

        @pl.loop(0, NZ)
        def _(i):
            for b in range(2):
                rc[k, t, i, b, :, lo] = rc[k, t, i, b, :, lo] + r2a[k, i, b]
                rc[k, b, i, y, :, hi] = rc[k, b, i, y, :, hi] + r2b[k, b, i]

        third[k] = [
            send(rc.at[k, t, :, 1 - y, :, lo], r3a.at[k], sems, (k, 3), over_y),
            send(rc.at[k, 1 - t, :, y, :, hi], r3b.at[k], sems, (k, 4), over_x),
        ]

    def start_last(k):
        for copy in third[k]:
            copy.wait()

        @pl.loop(0, NZ)
        def _(i):
            rc[k, t, i, y, :, lo] = rc[k, t, i, y, :, lo] + r3a[k, i]
            rc[k, t, i, y, :, hi] = rc[k, t, i, y, :, hi] + r3b[k, i]

        last[k] = [
            send(rc.at[k, t, lax.rem(z + j + 1, NZ), y], r4.at[k, j], sems, (k, 5 + j), other)
            for j, other in enumerate(over_z)
        ]

    def finish(k):
        for copy in last[k]:
            copy.wait()
        total = rc[k, t, z, y].astype(F32)
        for j in range(3):
            total = total + r4[k, j].astype(F32)
        out[k] = total

    start_first(0)
    for step in range(WAVES + 3):
        if step < WAVES:
            if step + 1 < WAVES:
                start_first(step + 1)
            start_second(step)
        if 0 <= step - 1 < WAVES:
            start_third(step - 1)
        if 0 <= step - 2 < WAVES:
            start_last(step - 2)
        if 0 <= step - 3 < WAVES:
            finish(step - 3)
    small_sum(small, small_out, got, acc, (s_send, s_recv))


def reduce_all(parts, small):
    _, width, cols = parts[0].shape
    rows = width // (NZ * NY * NC)
    shaped = [part.reshape(NX, NZ, NY, NC, rows, cols) for part in parts]
    dma = pltpu.SemaphoreType.DMA
    any_spec = pl.BlockSpec(memory_space=pl.ANY)
    vmem = pl.BlockSpec(memory_space=pltpu.VMEM)
    return pl.pallas_call(
        reduce_kernel,
        out_shape=(
            jax.ShapeDtypeStruct((WAVES, rows, cols), F32),
            jax.ShapeDtypeStruct(small.shape, F32),
        ),
        in_specs=[any_spec] * WAVES + [vmem],
        out_specs=(vmem, vmem),
        scratch_shapes=[
            pltpu.VMEM((2, NX, NZ, NY, rows, cols), BF),
            pltpu.VMEM((WAVES, NX, NZ, NY, rows, cols), BF),
            pltpu.VMEM((WAVES, NZ, NY, rows, cols // 2), BF),
            pltpu.VMEM((WAVES, NX, NZ, rows, cols // 2), BF),
            pltpu.VMEM((WAVES, NZ, rows, cols // 2), BF),
            pltpu.VMEM((WAVES, NZ, rows, cols // 2), BF),
            pltpu.VMEM((WAVES, 3, rows, cols), BF),
            pltpu.VMEM((6,) + small.shape, F32),
            pltpu.VMEM((3,) + small.shape, F32),
            dma((6,)),
            dma((6,)),
            dma((2,)),
            dma((WAVES, 8)),
            dma((WAVES, 8)),
        ],
        name="reduce_all",
        compiler_params=pltpu.CompilerParams(
            collective_id=1, has_side_effects=True, vmem_limit_bytes=56 << 20
        ),
    )(*shaped, small)


def gather_plain(shard, small):
    rows = lax.all_gather(shard, "dp", axis=1, tiled=True)
    full = lax.all_gather(rows, "tensor", axis=1, tiled=False)
    return full, lax.psum(small, AXES)


def reduce_plain(parts, small):
    outs = []
    for part in parts:
        mine = lax.psum_scatter(part.astype(F32), "tensor", scatter_dimension=0, tiled=True)[0]
        outs.append(lax.psum_scatter(mine, "dp", scatter_dimension=0, tiled=True))
    return jnp.stack(outs), lax.psum(small, AXES)


def layer_norm(residual, gain, shift):
    average = jnp.mean(residual, axis=-1, keepdims=True)
    centred = residual - average
    variance = jnp.mean(centred * centred, axis=-1, keepdims=True)
    return centred * lax.rsqrt(variance + EPS) * gain + shift


def gelu_exact(value):
    return jax.nn.gelu(value, approximate=False)


def ein(spec, a, b):
    return jnp.einsum(spec, a, b, preferred_element_type=F32)


def heads_of(value):
    return value.reshape(value.shape[0], value.shape[1], value.shape[2] // HEAD, HEAD)


def scores_of(queries, keys, valid):
    raw = ein("tqhd,tkhd->thqk", heads_of(queries), heads_of(keys)) * (HEAD**-0.5)
    return jnp.where(valid, raw, NEG)


def layer_forward(rows, groups, small, valid):
    w_attn, w_up, w_down = groups
    width = rows.shape[1]
    half = width // 2
    bq = small[0].reshape(2, 1, half)
    bv = small[1].reshape(2, 1, half)
    bo, g1, s1, bd, g2, s2 = (small[i][None, :] for i in range(2, 8))
    bu = small[8:].reshape(2, 1, -1)
    qkv = ein("nd,tdc->tnc", rows, w_attn[:, :, : 3 * half])
    queries = (qkv[:, :, :half] + bq).astype(BF)
    keys = qkv[:, :, half : 2 * half].astype(BF)
    values = (qkv[:, :, 2 * half :] + bv).astype(BF)
    scores = scores_of(queries, keys, valid)
    row_max = jnp.max(scores, axis=-1, keepdims=True)
    exponent = jnp.exp(scores - row_max)
    total = jnp.sum(exponent, axis=-1, keepdims=True)
    probs = (exponent / total).astype(BF)
    attended = ein("thqk,tkhd->tqhd", probs, heads_of(values)).astype(BF).reshape(queries.shape)
    log_sums = row_max + jnp.log(total)
    branch = ein("tnc,tdc->nd", attended, w_attn[:, :, 3 * half :])
    resid_one = rows.astype(F32) + branch + bo
    hidden = layer_norm(resid_one, g1, s1).astype(BF)
    upward = ein("nd,tdc->tnc", hidden, w_up) + bu
    active = gelu_exact(upward).astype(BF)
    resid_two = hidden.astype(F32) + ein("tnc,tdc->nd", active, w_down) + bd
    result = layer_norm(resid_two, g2, s2)
    saved = (rows, queries, keys, values, attended, log_sums, resid_one, hidden, upward, active, resid_two)
    return result, saved


def layer_backward(d_result, groups, small, saved, valid):
    w_attn, w_up, w_down = groups
    rows, queries, keys, values, attended, log_sums, resid_one, hidden, upward, active, resid_two = saved
    half = rows.shape[1] // 2
    g1, s1, g2, s2 = (small[i] for i in (3, 4, 6, 7))
    _, norm_two_back = jax.vjp(layer_norm, resid_two, g2, s2)
    d_resid_two, d_g2, d_s2 = norm_two_back(d_result)
    d_down = d_resid_two.astype(BF)
    gw_down = ein("nd,tnc->tdc", d_down, active).astype(BF)
    _, gelu_back = jax.vjp(gelu_exact, upward)
    d_up = gelu_back(ein("nd,tdc->tnc", d_down, w_down))[0].astype(BF)
    gw_up = ein("nd,tnc->tdc", hidden, d_up).astype(BF)
    d_bu = jnp.sum(d_up, axis=1, dtype=F32).reshape(4, -1)
    d_hidden = d_resid_two + ein("tnc,tdc->nd", d_up, w_up)
    _, norm_one_back = jax.vjp(layer_norm, resid_one, g1, s1)
    d_resid_one, d_g1, d_s1 = norm_one_back(d_hidden)
    d_branch = d_resid_one.astype(BF)
    gw_out = ein("nd,tnc->tdc", d_branch, attended)
    d_attended = ein("nd,tdc->tnc", d_branch, w_attn[:, :, 3 * half :]).astype(BF)
    probs = jnp.exp(scores_of(queries, keys, valid) - log_sums)
    d_probs = ein("tqhd,tkhd->thqk", heads_of(d_attended), heads_of(values))
    d_scores = (probs * (d_probs - jnp.sum(probs * d_probs, axis=-1, keepdims=True))).astype(BF)
    scale = HEAD**-0.5
    d_queries = (ein("thqk,tkhd->tqhd", d_scores, heads_of(keys)) * scale).astype(BF).reshape(queries.shape)
    d_keys = (ein("thqk,tqhd->tkhd", d_scores, heads_of(queries)) * scale).astype(BF).reshape(queries.shape)
    d_values = ein("thqk,tqhd->tkhd", probs.astype(BF), heads_of(d_attended)).astype(BF).reshape(queries.shape)
    d_qkv = jnp.concatenate([d_queries, d_keys, d_values], axis=2)
    gw_attn = jnp.concatenate([ein("nd,tnc->tdc", rows, d_qkv), gw_out], axis=2).astype(BF)
    d_input = d_resid_one + ein("tnc,tdc->nd", d_qkv, w_attn[:, :, : 3 * half])
    d_small = jnp.concatenate(
        [
            jnp.sum(d_queries, axis=1, dtype=F32).reshape(1, -1),
            jnp.sum(d_values, axis=1, dtype=F32).reshape(1, -1),
            jnp.sum(d_resid_one, axis=0)[None],
            d_g1[None],
            d_s1[None],
            jnp.sum(d_resid_two, axis=0)[None],
            d_g2[None],
            d_s2[None],
            d_bu,
        ],
        axis=0,
    )
    return d_input, (gw_attn, gw_up, gw_down), d_small


def pack_weights(args):
    query_w, _, key_w, value_w, _, out_w, _, _, _, up_w, _, down_w = args[:12]
    return jnp.stack([jnp.concatenate([query_w, key_w, value_w, out_w.T], axis=1), up_w, down_w.T])


def spread(values, where, count):
    n, m = values.shape
    block = jnp.arange(m * count) // m
    return jnp.where(block[None, :] == where, jnp.tile(values.astype(F32), (1, count)), 0.0)


def pack_small(args, dp, n_dp, t):
    query_b, value_b, up_b = args[1], args[4], args[10]
    biases = spread(jnp.concatenate([query_b, value_b], axis=0), t * n_dp + dp, 2 * n_dp)
    norms = spread(jnp.stack([args[6], args[7], args[8], args[12], args[13], args[14]]), 2 * dp + t, 2 * n_dp)
    ups = spread(up_b, t * n_dp + dp, 2 * n_dp).reshape(4, -1)
    return jnp.concatenate([biases, norms, ups], axis=0)


def take(values, where, count):
    n, width = values.shape
    m = width // count
    return lax.dynamic_slice_in_dim(values, where * m, m, 1)


def local(n_dp, fast, *args):
    inputs, lengths, grad_out = args[0], args[1], args[-1]
    teacher, student = args[2:17], args[17:32]
    dp, t = lax.axis_index("dp"), lax.axis_index("tensor")
    seq_len = inputs.shape[0]
    width = inputs.shape[1]
    half = width // 2
    my_length = lax.dynamic_index_in_dim(lengths, t, 0, keepdims=False)
    inside = jnp.arange(seq_len) < my_length
    row_mask = inside.astype(F32)[:, None]
    valid = inside[None, None, None, :]
    shard = jnp.concatenate([pack_weights(teacher), pack_weights(student)], axis=0)
    small = jnp.concatenate([pack_small(teacher, dp, n_dp, t), pack_small(student, dp, n_dp, t)], axis=0)
    full, small = (gather_all if fast else gather_plain)(shard, small)
    groups = [tuple(full[3 * layer + i] for i in range(3)) for layer in range(2)]
    smalls = [small[:12], small[12:]]
    result, kept_t = layer_forward(inputs, groups[0], smalls[0], valid)
    result, kept_s = layer_forward(result.astype(BF), groups[1], smalls[1], valid)
    activations = (result * row_mask).astype(BF)
    d_current = grad_out.astype(F32) * row_mask
    d_current, parts_s, small_s = layer_backward(d_current, groups[1], smalls[1], kept_s, valid)
    d_current, parts_t, small_t = layer_backward(d_current, groups[0], smalls[0], kept_t, valid)
    order = (parts_s[2], parts_s[1], parts_s[0], parts_t[2], parts_t[1], parts_t[0])
    sums, small_sums = (reduce_all if fast else reduce_plain)(order, jnp.concatenate([small_t, small_s], axis=0))
    outs = [activations, d_current]
    for layer in range(2):
        base = 3 * (1 - layer)
        g_down, g_up, g_attn = sums[base], sums[base + 1], sums[base + 2]
        part = small_sums[12 * layer : 12 * layer + 12]
        biases = take(part[0:2], t * n_dp + dp, 2 * n_dp)
        norms = take(part[2:8], 2 * dp + t, 2 * n_dp)
        ups = take(part[8:12].reshape(1, -1), t * n_dp + dp, 2 * n_dp)
        outs += [
            g_attn[:, :half],
            biases[0:1],
            g_attn[:, half : 2 * half],
            g_attn[:, 2 * half : 3 * half],
            biases[1:2],
            g_attn[:, 3 * half :].T,
            norms[0],
            norms[1],
            norms[2],
            g_up,
            ups,
            g_down.T,
            norms[3],
            norms[4],
            norms[5],
        ]
    return tuple(outs)


def solution(mesh):
    n_dp = mesh.shape["dp"]
    fast = n_dp == NZ * NY * NC and mesh.shape["tensor"] == NX
    row = P(AXES, None)
    vec = P(AXES)
    cut_in, cut_out = P("dp", "tensor"), P("tensor", "dp")
    layer = (cut_in, cut_out, cut_in, cut_in, cut_out, cut_out, vec, vec, vec, cut_in, cut_out, cut_out, vec, vec, vec)
    return jax.shard_map(
        functools.partial(local, n_dp, fast),
        mesh=mesh,
        in_specs=(row, P("dp")) + layer + layer + (row,),
        out_specs=(row, row) + layer + layer,
        check_vma=False,
    )
```

```python
import functools

import jax
import jax.numpy as jnp
from jax import lax
from jax.experimental import pallas as pl
from jax.experimental.pallas import tpu as pltpu
from jax.sharding import PartitionSpec as P

HEAD = 64
EPS = 1e-06
NEG = -1e30
NZ, NY, NC, NX = 4, 2, 2, 2
MESH = pl.DeviceIdType.MESH
BF = jnp.bfloat16
F32 = jnp.float32
AXES = ("dp", "tensor")


def place():
    dp = lax.axis_index("dp")
    t = lax.axis_index("tensor")
    return dp // 4, lax.rem(dp // 2, 2), lax.rem(dp, 2), t


def device(z, y, c, t):
    return {"dp": z * 4 + y * 2 + c, "tensor": t}


def greet(others):
    barrier = pltpu.get_barrier_semaphore()
    for other in others:
        pl.semaphore_signal(barrier, inc=1, device_id=other, device_id_type=MESH)
    pl.semaphore_wait(barrier, len(others))


def send(src, dst, sems, index, other):
    copy = pltpu.make_async_remote_copy(
        src_ref=src,
        dst_ref=dst,
        send_sem=sems[0].at[index],
        recv_sem=sems[1].at[index],
        device_id=other,
        device_id_type=MESH,
    )
    copy.start()
    return copy


def partners():
    z, y, c, t = place()
    core = device(z, y, 1 - c, t)
    over_x = device(z, y, c, 1 - t)
    over_y = device(z, 1 - y, c, t)
    over_z = [device(lax.rem(z + j, NZ), y, c, t) for j in range(1, NZ)]
    return core, over_x, over_y, over_z


def small_sum(src, dst, got, acc, sems):
    core, over_x, over_y, over_z = partners()
    now = src
    for step, other in enumerate((core, over_x, over_y)):
        send(now, got.at[step], sems, step, other).wait()
        acc[step] = now[...] + got[step]
        now = acc.at[step]
    copies = [send(now, got.at[3 + j], sems, 3 + j, other) for j, other in enumerate(over_z)]
    for copy in copies:
        copy.wait()
    dst[...] = now[...] + got[3] + got[4] + got[5]


def mm(a, b):
    return jnp.dot(a, b, preferred_element_type=F32)


def mm_nt(a, b):
    return lax.dot_general(a, b, (((1,), (1,)), ((), ())), preferred_element_type=F32)


def gelu_both(u):
    bell = jnp.exp(u * u * -0.5)
    t = 1.0 / (1.0 + (0.3275911 * 0.7071067811865476) * jnp.abs(u))
    tail = 1.061405429 * 0.5 * t - 1.453152027 * 0.5
    tail = tail * t + 1.421413741 * 0.5
    tail = tail * t - 0.284496736 * 0.5
    tail = (tail * t + 0.254829592 * 0.5) * t * bell
    cdf = jnp.where(u < 0, tail, 1.0 - tail)
    return u * cdf, cdf + u * bell * 0.3989422804014327


def norm_parts(r):
    average = jnp.mean(r, axis=-1, keepdims=True)
    centred = r - average
    variance = jnp.mean(centred * centred, axis=-1, keepdims=True)
    rstd = lax.rsqrt(variance + EPS)
    return centred * rstd, rstd


def block(i, n):
    return pl.ds(pl.multiple_of(i * n, n), n)


FWAVES = 12
AHEAD = 2
SIDE = FWAVES - 1


def gather_steps(shard, full, own_sem, sems, side_sems):
    z, y, c, t = place()
    core, over_x, over_y, over_z = partners()
    half = shard.shape[2] // 2
    lo, hi = pl.ds(0, half), pl.ds(half, half)
    owns, first, second, third, last = {}, {}, {}, {}, {}

    def one(k):
        owns[k] = pltpu.make_async_copy(shard.at[k], full.at[k, t, z, y, c], own_sem.at[k])
        owns[k].start()
        first[k] = [
            send(shard.at[k], full.at[k, t, z, y, c], sems, (k, j), other)
            for j, other in enumerate(over_z)
        ]

    def two(k):
        owns[k].wait()
        for copy in first[k]:
            copy.wait()
        a = full.at[k, t, :, y, c, :, lo]
        b = full.at[k, t, :, y, c, :, hi]
        second[k] = [send(a, a, sems, (k, 3), over_y), send(b, b, sems, (k, 4), over_x)]

    def three(k):
        for copy in second[k]:
            copy.wait()
        a = full.at[k, t, :, :, c, :, lo]
        b = full.at[k, :, :, y, c, :, hi]
        third[k] = [send(a, a, sems, (k, 5), over_x), send(b, b, sems, (k, 6), over_y)]

    def four(k):
        for copy in third[k]:
            copy.wait()
        a = full.at[k, :, :, :, c]
        last[k] = send(a, a, sems, (k, 7), core)

    def five(k):
        last[k].wait()

    side = {}

    def side_one():
        owns[SIDE] = pltpu.make_async_copy(shard.at[SIDE], full.at[SIDE, t, z, y, c], own_sem.at[SIDE])
        owns[SIDE].start()
        mine = full.at[SIDE, t, z, y, c]
        side[1] = [
            send(shard.at[SIDE, :, lo], mine.at[:, lo], side_sems, 0, over_x),
            send(shard.at[SIDE, :, hi], mine.at[:, hi], side_sems, 1, over_y),
        ]

    def side_two():
        owns[SIDE].wait()
        for copy in side[1]:
            copy.wait()
        a = full.at[SIDE, :, z, y, c, :, lo]
        b = full.at[SIDE, t, z, :, c, :, hi]
        side[2] = [send(a, a, side_sems, 2, over_y), send(b, b, side_sems, 3, over_x)]

    def side_three(i):
        if i == 0:
            for copy in side[2]:
                copy.wait()
            side[3] = []
        a = full.at[SIDE, i // 2, z, i % 2, c]
        side[3] += [send(a, a, side_sems, 4 + 3 * i + j, other) for j, other in enumerate(over_z)]

    def side_four():
        for copy in side[3]:
            copy.wait()
        a = full.at[SIDE, :, :, :, c]
        last[SIDE] = send(a, a, sems, (SIDE, 7), core)

    return one, two, three, four, five, (side_one, side_two, side_three, side_four)


def sum_steps(src, dst, got, acc, sems):
    core, over_x, over_y, over_z = partners()
    flying = {}

    def begin():
        flying[0] = [send(src, got.at[0], sems, 0, core)]

    def middle(step, other):
        for copy in flying[step - 1]:
            copy.wait()
        before = src if step == 1 else acc.at[step - 2]
        acc[step - 1] = before[...] + got[step - 1]
        if step < 3:
            flying[step] = [send(acc.at[step - 1], got.at[step], sems, step, other)]
        else:
            flying[step] = [send(acc.at[2], got.at[3 + j], sems, 3 + j, o) for j, o in enumerate(over_z)]

    def end():
        for copy in flying[3]:
            copy.wait()
        dst[...] = acc[2] + got[3] + got[4] + got[5]

    return [begin, lambda: middle(1, over_x), lambda: middle(2, over_y), lambda: middle(3, None), end]


SAVED = ("x", "q", "k", "v", "probs", "o", "z1", "rstd1", "h", "g", "gp", "z2", "rstd2")


def pack_copies(raw, shard, r_bias, r_up, r_norm, sem):
    pieces = {"small": []}
    width = shard.shape[2]
    half = width // 2
    count = 0

    def copy(src, dst):
        nonlocal count
        count += 1
        return pltpu.make_async_copy(src, dst, sem.at[count - 1])

    for layer in range(2):
        wq, bq, wk, wv, bv, wo, bo, g1, s1, wu, bu, wd, bd, g2, s2 = raw[layer]
        at = 6 * layer
        pieces[f"qk{layer}"] = [copy(wq, shard.at[at, :, :half]), copy(wk, shard.at[at, :, half:])]
        pieces[f"vo{layer}"] = [copy(wv, shard.at[at + 1, :, :half]), copy(wo, shard.at[at + 1, :, half:])]
        pieces[f"u{layer}"] = [
            copy(wu.at[:, :width], shard.at[at + 2]),
            copy(wu.at[:, width:], shard.at[at + 3]),
        ]
        pieces[f"d{layer}"] = [
            copy(wd.at[:, :width], shard.at[at + 4]),
            copy(wd.at[:, width:], shard.at[at + 5]),
        ]
        pieces["small"] += [copy(bq, r_bias.at[2 * layer]), copy(bv, r_bias.at[2 * layer + 1])]
        pieces["small"] += [copy(bu, r_up.at[layer])]
        pieces["small"] += [copy(v, r_norm.at[6 * layer + i]) for i, v in enumerate((bo, g1, s1, bd, g2, s2))]
    return pieces


def one_hot(rows, columns, start, axis):
    a = lax.broadcasted_iota(jnp.int32, (rows, columns), axis)
    b = lax.broadcasted_iota(jnp.int32, (rows, columns), 1 - axis)
    return jnp.where(a == b + start, 1.0, 0.0).astype(F32)


def mm_exact(a, b):
    return jnp.dot(a, b, preferred_element_type=F32, precision=lax.Precision.HIGHEST)


def spread_small(small, r_bias, r_up, r_norm, dp, t, n_dp):
    width = small.shape[1]
    m = r_norm.shape[2]
    to_norm = one_hot(m, width, (2 * dp + t) * m, 1)
    to_bias = one_hot(m, width, (t * n_dp + dp) * m, 1)
    many = r_up.shape[2]
    biases = mm_exact(jnp.concatenate([r_bias[i].astype(F32) for i in range(4)], axis=0), to_bias)
    norms = mm_exact(jnp.concatenate([r_norm[i] for i in range(12)], axis=0), to_norm)
    ups = jnp.concatenate([r_up[i].astype(F32) for i in range(2)], axis=0)
    for layer in range(2):
        at = 12 * layer
        small[at : at + 2, :] = biases[2 * layer : 2 * layer + 2]
        small[at + 2 : at + 8, :] = norms[6 * layer : 6 * layer + 6]
    for i in range(4):
        r = mm_exact(ups, one_hot(many, width, (t * n_dp + dp) * many - i * width, 1))
        for layer in range(2):
            small[12 * layer + 8 + i : 12 * layer + 9 + i, :] = r[layer : layer + 1]


def forward_kernel(*refs):
    lengths, rows = refs[:2]
    raw = [refs[2 + 15 * i : 17 + 15 * i] for i in range(2)]
    refs = refs[32:]
    full, small_out, act_out = refs[:3]
    saves = [dict(zip(SAVED, refs[3 + 13 * i : 16 + 13 * i])) for i in range(2)]
    refs = refs[29:]
    shard, small, r_bias, r_up, r_norm, raw_sem, x_sem = refs[:7]
    refs = refs[7:]
    bufs = dict(zip(SAVED, refs[:13]))
    bias, vt, ot, r2, w_slots, got, acc, s_send, s_recv, own_sem, b_send, b_recv, c_send, c_recv, load_sem, save_sem = refs[13:]
    z, y, c, t_mine = place()
    dp = lax.axis_index("dp")
    core, over_x, over_y, over_z = partners()
    pieces = pack_copies(raw, shard, r_bias, r_up, r_norm, raw_sem)
    x_copy = pltpu.make_async_copy(rows, bufs["x"], x_sem)
    for name in ("qk0", "d1", "small", "vo0", "u0", "d0", "qk1", "vo1", "u1"):
        for copy in pieces[name]:
            copy.start()
        if name == "vo0":
            x_copy.start()
    greet([core, over_x, over_y] + over_z)
    one, two, three, four, five, side = gather_steps(
        shard, full, own_sem, (b_send, b_recv), (c_send, c_recv)
    )
    sums = sum_steps(small, small_out, got, acc, (s_send, s_recv))
    loads, stores = {}, {}
    n, width = rows.shape
    half = width // 2

    def packed(name):
        for copy in pieces[name]:
            copy.wait()

    packed("qk0")
    one(0)
    packed("d1")
    side[0]()
    packed("small")
    n_dp = lax.axis_size("dp")
    spread_small(small, r_bias, r_up, r_norm, dp, t_mine, n_dp)
    sums[0]()
    side[1]()
    packed("vo0")
    one(1)
    x_copy.wait()
    for name in ("u0", "d0", "qk1", "vo1", "u1"):
        packed(name)
    length = lengths[t_mine]
    inside = lax.broadcasted_iota(jnp.int32, (n, 1), 0) < length
    bias[...] = jnp.where(inside, 0.0, NEG)

    def bring(k):
        five(k)
        loads[k] = pltpu.make_async_copy(full.at[k], w_slots.at[k % 2], load_sem.at[k % 2])
        loads[k].start()

    def comm(step):
        if step + 1 < len(sums):
            sums[step + 1]()
        if step < SIDE:
            two(step)
            if step + AHEAD < SIDE:
                one(step + AHEAD)
        if step % 2 == 1 and step < 8:
            side[2](step // 2)
        if 0 <= step - 1 < SIDE:
            three(step - 1)
        if step == SIDE - 1:
            side[3]()
        if 0 <= step - 2 < SIDE:
            four(step - 2)
        if 0 <= step - 3 < FWAVES:
            bring(step - 3)

    def weights(k):
        loads[k].wait()
        slot = w_slots.at[k % 2]
        return lambda t, lanes: slot[t, :, :, :, :, lanes].reshape(width, -1)

    def save(layer, *names):
        for name in names:
            copy = pltpu.make_async_copy(bufs[name], saves[layer][name], save_sem.at[SAVED.index(name)])
            copy.start()
            stores[name] = copy

    def free(*names):
        for name in names:
            if name in stores:
                stores.pop(name).wait()

    def vec(layer, i):
        return small_out[12 * layer + i : 12 * layer + i + 1]

    def scores_stage(layer, k):
        w = weights(k)
        x, q, kk, probs = (bufs[i] for i in ("x", "q", "k", "probs"))
        free("q", "k", "probs")
        for t in range(2):
            here = slice(t * half, (t + 1) * half)
            r = mm(x[...], w(t, slice(0, half))) + vec(layer, 0)[:, here]
            q[:, here] = r.astype(BF) * BF(HEAD**-0.5)
            kk[:, here] = mm(x[...], w(t, slice(half, width))).astype(BF)
        save(layer, "q", "k")
        lane = lax.broadcasted_iota(jnp.int32, (1, 128), 1)

        @pl.loop(0, width // 128)
        def _(p):
            kp = kk[:, block(p, 128)]
            qp = q[:, block(p, 128)]
            for head in range(2):
                qm = jnp.where((lane >= HEAD) == (head == 1), qp, BF(0))
                s = mm_nt(kp, qm) + bias[...]
                e = jnp.exp(s - jnp.max(s, axis=0, keepdims=True))
                probs[2 * p + head] = (e * (1.0 / jnp.sum(e, axis=0, keepdims=True))).astype(BF)

        save(layer, "probs")

    def attend_stage(layer, k):
        w = weights(k)
        x, v, probs, o, z1, rstd1, h = (bufs[i] for i in ("x", "v", "probs", "o", "z1", "rstd1", "h"))
        free("v", "o", "z1", "rstd1", "h")
        for t in range(2):
            here = slice(t * half, (t + 1) * half)
            r = mm(x[...], w(t, slice(0, half))) + vec(layer, 1)[:, here]
            v[:, here] = r.astype(BF)
        save(layer, "v")
        vt[...] = v[...].T

        @pl.loop(0, width // HEAD)
        def _(i):
            ot[block(i, HEAD), :] = mm(vt[block(i, HEAD), :], probs[i]).astype(BF)

        o[...] = ot[...].T
        save(layer, "o")
        r = x[...].astype(F32) + vec(layer, 2)
        for t in range(2):
            r = r + mm_nt(o[:, t * half : (t + 1) * half], w(t, slice(half, width)))
        z, rstd = norm_parts(r)
        z1[...] = z.astype(BF)
        rstd1[...] = rstd
        h[...] = (z * vec(layer, 3) + vec(layer, 4)).astype(BF)
        save(layer, "x", "z1", "rstd1", "h")

    def up_stage(layer, k, part):
        w = weights(k)
        h, g, gp = (bufs[i] for i in ("h", "g", "gp"))
        if part == 0:
            free("g", "gp")
        step = 384
        for t in range(2):

            @pl.loop(0, width // step)
            def _(i):
                at = t * 2 * width + part * width + i * step
                here = pl.ds(pl.multiple_of(part * width + i * step, step), step)
                u = mm(h[...], w(t, block(i, step)))
                bu = bu_row(layer, t, part, i, step)
                a, b = gelu_both(u + bu)
                g[t, :, here] = a.astype(BF)
                gp[t, :, here] = b.astype(BF)

        if part == 1:
            save(layer, "g", "gp")

    def bu_row(layer, t, part, i, step):
        return small_out[pl.ds(12 * layer + 8 + 2 * t + part, 1), block(i, step)]

    def down_stage(layer, k, part):
        w = weights(k)
        h, g, z2, rstd2 = (bufs[i] for i in ("h", "g", "z2", "rstd2"))
        here = slice(part * width, (part + 1) * width)
        total = None
        for t in range(2):
            r = mm_nt(g[t, :, here], w(t, slice(0, width)))
            total = r if total is None else total + r
        if part == 0:
            r2[...] = total
            return
        free("z2", "rstd2", "x")
        r = r2[...] + total + h[...].astype(F32) + vec(layer, 5)
        z, rstd = norm_parts(r)
        z2[...] = z.astype(BF)
        rstd2[...] = rstd
        result = z * vec(layer, 6) + vec(layer, 7)
        save(layer, "z2", "rstd2")
        if layer == 0:
            bufs["x"][...] = result.astype(BF)
        else:
            act_out[...] = jnp.where(inside, result, 0.0).astype(BF)

    def compute(k):
        layer, i = k // 6, k % 6
        if i == 0:
            scores_stage(layer, k)
        elif i == 1:
            attend_stage(layer, k)
        elif i < 4:
            up_stage(layer, k, i - 2)
        else:
            down_stage(layer, k, i - 4)

    for step in range(FWAVES + 4):
        comm(step)
        if step >= 4:
            compute(step - 4)
    free(*list(stores))


def saved_kinds(n, width):
    heads = width // HEAD
    return {
        "x": ((n, width), BF),
        "q": ((n, width), BF),
        "k": ((n, width), BF),
        "v": ((n, width), BF),
        "probs": ((heads, n, n), BF),
        "o": ((n, width), BF),
        "z1": ((n, width), BF),
        "rstd1": ((n, 1), F32),
        "h": ((n, width), BF),
        "g": ((2, n, 2 * width), BF),
        "gp": ((2, n, 2 * width), BF),
        "z2": ((n, width), BF),
        "rstd2": ((n, 1), F32),
    }


def forward_all(lengths, rows, teacher, student):
    n, width = rows.shape
    part = teacher[0].shape[0]
    waves, cols = FWAVES, width
    raw = teacher + student
    few, many = raw[1].shape[1], raw[10].shape[1]
    small = jax.ShapeDtypeStruct((24, width), F32)
    kinds = saved_kinds(n, width)
    dma = pltpu.SemaphoreType.DMA
    hbm = pl.BlockSpec(memory_space=pltpu.MemorySpace.HBM)
    vmem = pl.BlockSpec(memory_space=pltpu.VMEM)
    shape = jax.ShapeDtypeStruct
    outs = pl.pallas_call(
        forward_kernel,
        out_shape=(
            shape((waves, NX, NZ, NY, NC, part, cols), BF),
            shape(small.shape, F32),
            shape((n, width), BF),
        )
        + tuple(shape(*kinds[name]) for name in SAVED) * 2,
        in_specs=[pl.BlockSpec(memory_space=pltpu.SMEM)] + [hbm] * 31,
        out_specs=(hbm, vmem, vmem) + (hbm,) * 26,
        scratch_shapes=[
            pltpu.VMEM((waves, part, cols), BF),
            pltpu.VMEM(small.shape, F32),
            pltpu.VMEM((4, 1, few), BF),
            pltpu.VMEM((2, 1, many), BF),
            pltpu.VMEM((12, 1, few), F32),
            dma((34,)),
            dma(()),
        ]
        + [pltpu.VMEM(*kinds[name]) for name in SAVED]
        + [
            pltpu.VMEM((n, 1), F32),
            pltpu.VMEM((width, n), BF),
            pltpu.VMEM((width, n), BF),
            pltpu.VMEM((n, width), F32),
            pltpu.VMEM((2, NX, NZ, NY, NC, part, cols), BF),
            pltpu.VMEM((6,) + small.shape, F32),
            pltpu.VMEM((3,) + small.shape, F32),
            dma((6,)),
            dma((6,)),
            dma((waves,)),
            dma((waves, 8)),
            dma((waves, 8)),
            dma((16,)),
            dma((16,)),
            dma((2,)),
            dma((13,)),
        ],
        name="forward_all",
        compiler_params=pltpu.CompilerParams(
            collective_id=0, has_side_effects=True, vmem_limit_bytes=60 << 20
        ),
    )(lengths, rows, *raw)
    full, small, activations = outs[:3]
    saved = [dict(zip(SAVED, outs[3 + 13 * i : 16 + 13 * i])) for i in range(2)]
    return full, small, activations, saved


ORDER = [6 + i for i in (4, 5, 2, 3, 1, 0)] + [4, 5, 2, 3, 1, 0]
RC, R2S, R3S = 7, 3, 3
TURN = 1
RESTS = 16
WAITS = (1, 5, 4, 8)
LAST = FWAVES - 1
CUTS = 3


def reduce_steps(stage, rc, r2a, r2b, r3a, r3b, r4, rz, ra, rb, out, credit, sems, t_sems):
    z, y, c, t = place()
    core, over_x, over_y, over_z = partners()
    half = out.shape[2] // 2
    lo, hi = pl.ds(0, half), pl.ds(half, half)
    flying = {}

    def rest():
        pass

    def wait(key):
        for copy in flying.pop(key):
            copy.wait()

    def give(kind, other):
        pl.semaphore_signal(credit.at[kind], inc=1, device_id=other, device_id_type=MESH)

    def add(dst, *srcs):
        total = dst[...]
        for src in srcs:
            total = total + src[...]
        dst[...] = total

    def own(s, j, lanes):
        @pl.loop(0, NZ)
        def _(i):
            for a in range(NX):
                for b in range(NY):
                    for lane in lanes:
                        add(rc.at[s, a, i, b, :, lane], stage.at[j % 2, a, i, b, c, :, lane])

    def steps(j, cut=None):
        n = j if TURN < 0 or j < TURN else j - 1
        total = FWAVES - (TURN >= 0)
        key, s, s2, s3 = (j, cut), n % RC, n % R2S, n % R3S
        row = j if cut is None else FWAVES + cut
        first = cut in (None, 0)
        width = half if cut is None else half // CUTS
        at = 0 if cut is None else cut * width
        low, high = pl.ds(at, width), pl.ds(half + at, width)
        spans = [pl.ds(0, 2 * half)] if cut is None else [low, high]

        def one():
            if n >= RC and first:
                pl.semaphore_wait(credit.at[0], 1)
            flying[key] = [
                send(stage.at[j % 2, :, :, :, 1 - c, :, lanes], rc.at[s, :, :, :, :, lanes], sems, (row, i), core)
                for i, lanes in enumerate(spans)
            ]

        def two():
            wait(key)
            own(s, j, spans)
            if n >= R2S and first:
                pl.semaphore_wait(credit.at[1], 1)
                pl.semaphore_wait(credit.at[2], 1)
            flying[key] = [
                send(rc.at[s, 1 - t, :, :, :, low], r2a.at[s2, :, :, :, low], sems, (row, 2), over_x),
                send(rc.at[s, :, :, 1 - y, :, high], r2b.at[s2, :, :, :, low], sems, (row, 3), over_y),
            ]

        def three():
            wait(key)

            @pl.loop(0, NZ)
            def _(i):
                for b in range(2):
                    add(rc.at[s, t, i, b, :, low], r2a.at[s2, i, b, :, low])
                    add(rc.at[s, b, i, y, :, high], r2b.at[s2, b, i, :, low])

            if n + R2S < total:
                give(1, over_x)
                give(2, over_y)
            if n >= R3S and first:
                pl.semaphore_wait(credit.at[3], 1)
                pl.semaphore_wait(credit.at[4], 1)
            flying[key] = [
                send(rc.at[s, t, :, 1 - y, :, low], r3a.at[s3, :, :, low], sems, (row, 4), over_y),
                send(rc.at[s, 1 - t, :, y, :, high], r3b.at[s3, :, :, low], sems, (row, 5), over_x),
            ]

        def four():
            wait(key)

            @pl.loop(0, NZ)
            def _(i):
                add(rc.at[s, t, i, y, :, low], r3a.at[s3, i, :, low])
                add(rc.at[s, t, i, y, :, high], r3b.at[s3, i, :, low])

            if n + R3S < total:
                give(3, over_y)
                give(4, over_x)
            flying[key] = [
                send(
                    rc.at[s, t, lax.rem(z + i + 1, NZ), y, :, lanes],
                    r4.at[n, i, :, lanes],
                    sems,
                    (row, 6 + 3 * k + i),
                    other,
                )
                for i, other in enumerate(over_z)
                for k, lanes in enumerate(spans)
            ]

        def five():
            wait(key)
            for lanes in spans:
                value = rc[s, t, z, y, :, lanes].astype(F32)
                for i in range(3):
                    value = value + r4[n, i, :, lanes].astype(F32)
                out[ORDER[j], :, lanes] = value
            if n + RC < total:
                give(0, core)

        return [one] + [rest] * WAITS[0] + [two] + [rest] * WAITS[1] + [three] + [rest] * WAITS[2] + [four] + [rest] * WAITS[3] + [five]

    def turned(j):
        s = RC

        def one():
            flying[j] = [send(stage.at[j % 2, :, :, :, 1 - c], rc.at[s], t_sems, 0, core)]

        def two():
            wait(j)
            own(s, j, [pl.ds(0, 2 * half)])
            flying[j] = [
                send(rc.at[s, :, lax.rem(z + i + 1, NZ)], rz.at[i], t_sems, 1 + i, other)
                for i, other in enumerate(over_z)
            ]

        def three():
            wait(j)
            for a in range(NX):
                for b in range(NY):
                    add(rc.at[s, a, z, b], rz.at[0, a, b], rz.at[1, a, b], rz.at[2, a, b])
            flying[j] = [
                send(rc.at[s, 1 - t, z, :, :, lo], ra.at[0:2], t_sems, 4, over_x),
                send(rc.at[s, :, z, 1 - y, :, hi], rb.at[0:2], t_sems, 5, over_y),
            ]

        def four():
            wait(j)
            for b in range(2):
                add(rc.at[s, t, z, b, :, lo], ra.at[b])
                add(rc.at[s, b, z, y, :, hi], rb.at[b])
            flying[j] = [
                send(rc.at[s, t, z, 1 - y, :, lo], ra.at[2], t_sems, 6, over_y),
                send(rc.at[s, 1 - t, z, y, :, hi], rb.at[2], t_sems, 7, over_x),
            ]

        def five():
            wait(j)
            out[ORDER[j], :, lo] = rc[s, t, z, y, :, lo].astype(F32) + ra[2].astype(F32)
            out[ORDER[j], :, hi] = rc[s, t, z, y, :, hi].astype(F32) + rb[2].astype(F32)

        return [one, two] + [rest] * RESTS + [three, rest, rest, four, rest, rest, five]

    return steps, turned


def back_kernel(*refs):
    lengths, grad, small, full = refs[:4]
    saves = [dict(zip(SAVED, refs[4 + 13 * i : 17 + 13 * i])) for i in range(2)]
    refs = refs[30:]
    d_input, out, small_out = refs[:3]
    refs = refs[3:]
    bufs = dict(zip(SAVED, refs[:13]))
    refs = refs[13:]
    dy, dr, dlo, lot, dlot, d_o, dq, dk, dv, kt, dqt = refs[:11]
    refs = refs[11:]
    w_slots, stage, rc, r2a, r2b, r3a, r3b, r4, rz, ra, rb, terms, got, acc = refs[:14]
    s_send, s_recv, b_send, b_recv, t_send, t_recv, credit, load_sem, w_sem = refs[14:]
    core, over_x, over_y, over_z = partners()
    n, width = grad.shape
    half = width // 2
    loads, w_loads = {}, {}

    def load(layer, *names):
        for name in names:
            copy = pltpu.make_async_copy(saves[layer][name], bufs[name], load_sem.at[SAVED.index(name)])
            copy.start()
            loads[name] = copy

    def need(*names):
        for name in names:
            if name in loads:
                loads.pop(name).wait()

    def fetch(j):
        if j < FWAVES:
            w_loads[j] = pltpu.make_async_copy(full.at[ORDER[j]], w_slots.at[j % 2], w_sem.at[j % 2])
            w_loads[j].start()

    def weights(j):
        w_loads[j].wait()
        slot = w_slots.at[j % 2]
        return lambda t, lanes: slot[t, :, :, :, :, lanes].reshape(width, -1)

    load(1, "z2", "rstd2")
    fetch(0)
    load(1, "g", "gp", "h", "z1", "rstd1")
    fetch(1)
    load(1, "o", "probs", "x", "v", "k", "q")
    greet([core, over_x, over_y] + over_z)
    steps, turned = reduce_steps(
        stage, rc, r2a, r2b, r3a, r3b, r4, rz, ra, rb, out, credit, (b_send, b_recv), (t_send, t_recv)
    )
    moving = []

    def advance():
        for item in moving:
            item.pop(0)()
        moving[:] = [item for item in moving if item]

    def comm(j, cut=None):
        advance()
        item = turned(j) if j == TURN else steps(j, cut)
        item.pop(0)()
        moving.append(item)

    def put(j, t, lanes, value):
        stage[j % 2, t, :, :, :, :, lanes] = value.astype(BF).reshape(NZ, NY, NC, -1, value.shape[1])

    def term(layer, i, value):
        terms[12 * layer + i : 12 * layer + i + 1, :] = value

    def vec(layer, i):
        return small[12 * layer + i : 12 * layer + i + 1]

    def norm_back(layer, at, d_out, z, rstd):
        zf = z[...].astype(F32)
        dz = d_out * vec(layer, at + 1)
        a = jnp.mean(dz, axis=-1, keepdims=True)
        b = jnp.mean(dz * zf, axis=-1, keepdims=True)
        d_in = rstd[...] * (dz - a - zf * b)
        term(layer, at, jnp.sum(d_in, axis=0, keepdims=True))
        term(layer, at + 1, jnp.sum(d_out * zf, axis=0, keepdims=True))
        term(layer, at + 2, jnp.sum(d_out, axis=0, keepdims=True))
        dr[...] = d_in
        low = d_in.astype(BF)
        dlo[...] = low
        dlot[...] = low.T

    def down_stage(layer, j, part):
        g, gp = bufs["g"], bufs["gp"]
        if part == 0:
            need("z2", "rstd2")
            norm_back(layer, 5, dy[...], bufs["z2"], bufs["rstd2"])
            need("g", "gp")
        w = weights(j)
        here = slice(part * width, (part + 1) * width)
        for t in range(2):
            put(j, t, slice(0, width), mm(dlot[...], g[t, :, here]))
            if t == 0:
                advance()
        comm(j)
        for t in range(2):
            if t == 1:
                advance()
            du = (mm(dlo[...], w(t, slice(0, width))) * gp[t, :, here].astype(F32)).astype(BF)
            gp[t, :, here] = du
            term(layer, 8 + 2 * t + part, jnp.sum(du.astype(F32), axis=0, keepdims=True))
        fetch(j + 2)
        if part == 1 and layer == 1:
            load(0, "z2", "rstd2", "g")

    def up_stage(layer, j, part):
        h, gp = bufs["h"], bufs["gp"]
        if part == 0:
            need("h")
            lot[...] = h[...].T
        w = weights(j)
        here = slice(part * width, (part + 1) * width)
        for t in range(2):
            put(j, t, slice(0, width), mm(lot[...], gp[t, :, here]))
            if t == 0:
                advance()
        comm(j)
        for t in range(2):
            if t == 1:
                advance()
            dr[...] = dr[...] + mm_nt(gp[t, :, here], w(t, slice(0, width)))
        fetch(j + 2)
        if part == 0:
            return
        total = dr[...]
        need("z1", "rstd1")
        norm_back(layer, 2, total, bufs["z1"], bufs["rstd1"])
        if layer == 1:
            load(0, "gp", "h", "z1", "rstd1")

    lane = lax.broadcasted_iota(jnp.int32, (1, 128), 1)

    def of_head(head, value):
        return jnp.where((lane >= HEAD) == (head == 1), value, BF(0))

    def value_stage(layer, j):
        o, probs, x = bufs["o"], bufs["probs"], bufs["x"]
        w = weights(j)
        need("o", "probs", "x")
        for t in range(2):
            here = slice(t * half, (t + 1) * half)
            put(j, t, slice(half, width), mm(dlot[...], o[:, here]))
            d_o[:, here] = mm(dlo[...], w(t, slice(half, width))).astype(BF)
        lot[...] = x[...].T
        advance()

        @pl.loop(0, width // 128)
        def _(p):
            dop = d_o[:, block(p, 128)]
            total = mm(probs[2 * p], of_head(0, dop)) + mm(probs[2 * p + 1], of_head(1, dop))
            dv[:, block(p, 128)] = total.astype(BF)

        advance()
        for t in range(2):
            put(j, t, slice(0, half), mm(lot[...], dv[:, t * half : (t + 1) * half]))
        comm(j)
        total = dr[...]
        for t in range(2):
            total = total + mm_nt(dv[:, t * half : (t + 1) * half], w(t, slice(0, half)))
        dr[...] = total
        advance()
        term(layer, 1, jnp.sum(dv[...].astype(F32), axis=0, keepdims=True))
        fetch(j + 2)
        if layer == 1:
            load(0, "o", "x")

    def score_stage(layer, j):
        probs, q, k, v = (bufs[i] for i in ("probs", "q", "k", "v"))
        w = weights(j)
        need("q", "k", "v")
        kt[...] = k[...].T

        def pair(p):
            dop = d_o[:, block(p, 128)]
            qp = q[:, block(p, 128)]
            vp = v[:, block(p, 128)]
            total = None
            for head in range(2):
                dp = mm_nt(vp, of_head(head, dop))
                pr = probs[2 * p + head].astype(F32)
                delta = jnp.sum(pr * dp, axis=0, keepdims=True)
                ds = (pr * (dp - delta)).astype(BF)
                r = mm(ds, of_head(head, qp))
                total = r if total is None else total + r
                rows = block(2 * p + head, HEAD)
                dqt[rows, :] = (mm(kt[rows, :], ds) * (HEAD**-0.5)).astype(BF)
            dk[:, block(p, 128)] = total.astype(BF)

        def stage_cols(cut, n):
            for t in range(2):
                here = slice(t * half + cut * n, t * half + (cut + 1) * n)
                put(j, t, slice(cut * n, (cut + 1) * n), mm(lot[...], dq[:, here]))
                put(j, t, slice(half + cut * n, half + (cut + 1) * n), mm(lot[...], dk[:, here]))

        if j < LAST:
            for i in range(0, width // 128, 2):
                pl.loop(i, i + 2)(pair)
                advance()
            dq[...] = dqt[...].T
            stage_cols(0, half)
            comm(j)
        else:
            n = half // CUTS
            for cut in range(CUTS):

                @pl.loop(0, 2)
                def _(t):
                    p = t * CUTS + cut
                    pair(p)
                    dq[:, block(p, n)] = dqt[block(p, n), :].T

                stage_cols(cut, n)
                comm(j, cut)
        total = dr[...]
        for t in range(2):
            here = slice(t * half, (t + 1) * half)
            total = total + mm_nt(dq[:, here], w(t, slice(0, half)))
            total = total + mm_nt(dk[:, here], w(t, slice(half, width)))
        term(layer, 0, jnp.sum(dq[...].astype(F32), axis=0, keepdims=True))
        fetch(j + 2)
        if layer == 1:
            dy[...] = total
            load(0, "probs", "q", "k", "v")
        else:
            d_input[...] = total

    inside = lax.broadcasted_iota(jnp.int32, (n, 1), 0) < lengths[lax.axis_index("tensor")]
    dy[...] = jnp.where(inside, grad[...].astype(F32), 0.0)
    for j, wave in enumerate(ORDER):
        layer, i = wave // 6, wave % 6
        if i >= 4:
            down_stage(layer, j, i - 4)
        elif i >= 2:
            up_stage(layer, j, i - 2)
        elif i == 1:
            value_stage(layer, j)
        else:
            score_stage(layer, j)
    sums = sum_steps(terms, small_out, got, acc, (s_send, s_recv))
    sums.pop(0)()
    while moving or sums:
        advance()
        if sums:
            sums.pop(0)()


def back_all(lengths, grad, full, small, saved):
    n, width = grad.shape
    heads = width // HEAD
    waves, _, _, _, _, part, cols = full.shape
    kinds = saved_kinds(n, width)
    dma = pltpu.SemaphoreType.DMA
    hbm = pl.BlockSpec(memory_space=pltpu.MemorySpace.HBM)
    vmem = pl.BlockSpec(memory_space=pltpu.VMEM)
    shape = jax.ShapeDtypeStruct
    rows = (n, width)
    return pl.pallas_call(
        back_kernel,
        out_shape=(shape(rows, F32), shape((waves, part, cols), F32), shape(small.shape, F32)),
        in_specs=[pl.BlockSpec(memory_space=pltpu.SMEM), vmem, vmem, hbm] + [hbm] * 26,
        out_specs=(vmem, vmem, vmem),
        scratch_shapes=[pltpu.VMEM(*kinds[name]) for name in SAVED]
        + [
            pltpu.VMEM(rows, F32),
            pltpu.VMEM(rows, F32),
            pltpu.VMEM(rows, BF),
            pltpu.VMEM((width, n), BF),
            pltpu.VMEM((width, n), BF),
            pltpu.VMEM(rows, BF),
            pltpu.VMEM(rows, BF),
            pltpu.VMEM(rows, BF),
            pltpu.VMEM(rows, BF),
            pltpu.VMEM((width, n), BF),
            pltpu.VMEM((width, n), BF),
            pltpu.VMEM((2, NX, NZ, NY, NC, part, cols), BF),
            pltpu.VMEM((2, NX, NZ, NY, NC, part, cols), BF),
            pltpu.VMEM((RC + 1, NX, NZ, NY, part, cols), BF),
            pltpu.VMEM((R2S, NZ, NY, part, cols // 2), BF),
            pltpu.VMEM((R2S, NX, NZ, part, cols // 2), BF),
            pltpu.VMEM((R3S, NZ, part, cols // 2), BF),
            pltpu.VMEM((R3S, NZ, part, cols // 2), BF),
            pltpu.VMEM((waves, 3, part, cols), BF),
            pltpu.VMEM((3, NX, NY, part, cols), BF),
            pltpu.VMEM((3, part, cols // 2), BF),
            pltpu.VMEM((3, part, cols // 2), BF),
            pltpu.VMEM(small.shape, F32),
            pltpu.VMEM((6,) + small.shape, F32),
            pltpu.VMEM((3,) + small.shape, F32),
            dma((6,)),
            dma((6,)),
            dma((waves + CUTS, 12)),
            dma((waves + CUTS, 12)),
            dma((8,)),
            dma((8,)),
            pltpu.SemaphoreType.REGULAR((5,)),
            dma((13,)),
            dma((2,)),
        ],
        name="back_all",
        compiler_params=pltpu.CompilerParams(
            collective_id=1, has_side_effects=True, vmem_limit_bytes=63 << 20
        ),
    )(lengths, grad, small, full, *[saved[i][name] for i in range(2) for name in SAVED])


def unpack_kernel(*refs):
    sums, small, d_input, activations = refs[:4]
    act_out, d_out = refs[4:6]
    outs = [refs[6 + 15 * i : 21 + 15 * i] for i in range(2)]
    vectors, sem = refs[36:]
    width = sums.shape[2]
    half = width // 2
    moves = [(small, vectors), (d_input, d_out), (activations, act_out)]
    for layer in range(2):
        wq, _, wk, wv, _, wo, _, _, _, wu, _, wd = outs[layer][:12]
        at = 6 * layer
        moves += [
            (sums.at[at + 2], wu.at[:, :width]),
            (sums.at[at + 3], wu.at[:, width:]),
            (sums.at[at + 4], wd.at[:, :width]),
            (sums.at[at + 5], wd.at[:, width:]),
            (sums.at[at, :, :half], wq),
            (sums.at[at, :, half:], wk),
            (sums.at[at + 1, :, :half], wv),
            (sums.at[at + 1, :, half:], wo),
        ]
    copies = [pltpu.make_async_copy(src, dst, sem.at[i]) for i, (src, dst) in enumerate(moves)]
    for copy in copies:
        copy.start()
    dp, t, n_dp = lax.axis_index("dp"), lax.axis_index("tensor"), lax.axis_size("dp")
    few, many = outs[0][1].shape[1], outs[0][10].shape[1]
    from_norm = one_hot(width, few, (2 * dp + t) * few, 0)
    from_bias = one_hot(width, few, (t * n_dp + dp) * few, 0)
    from_up = [one_hot(width, many, (t * n_dp + dp) * many - i * width, 0) for i in range(4)]
    copies[0].wait()
    biases = mm_exact(vectors[...], from_bias)
    norms = mm_exact(vectors[...], from_norm)
    for layer in range(2):
        _, bq, _, _, bv, _, bo, g1, s1, _, bu, _, bd, g2, s2 = outs[layer]
        low = 12 * layer
        for i, ref in enumerate((bq, bv)):
            ref[...] = biases[low + i : low + i + 1]
        for i, ref in enumerate((bo, g1, s1, bd, g2, s2)):
            ref[...] = norms[low + 2 + i : low + 3 + i]
    rows = [jnp.concatenate([vectors[8 + i : 9 + i, :], vectors[20 + i : 21 + i, :]], axis=0) for i in range(4)]
    total = mm_exact(rows[0], from_up[0])
    for i in range(1, 4):
        total = total + mm_exact(rows[i], from_up[i])
    for layer in range(2):
        outs[layer][10][...] = total[layer : layer + 1]
    for copy in copies[1:]:
        copy.wait()


def unpack_all(sums, small_sums, d_input, activations, teacher, student):
    hbm = pl.BlockSpec(memory_space=pltpu.MemorySpace.HBM)
    vmem = pl.BlockSpec(memory_space=pltpu.VMEM)
    shape = jax.ShapeDtypeStruct
    flat = teacher + student
    outs = pl.pallas_call(
        unpack_kernel,
        out_shape=(shape(activations.shape, BF), shape(d_input.shape, F32))
        + tuple(shape(v.shape, F32) for v in flat),
        in_specs=[hbm] * 4,
        out_specs=(vmem,) * 32,
        scratch_shapes=[pltpu.VMEM(small_sums.shape, F32), pltpu.SemaphoreType.DMA((19,))],
        name="unpack_all",
        compiler_params=pltpu.CompilerParams(vmem_limit_bytes=63 << 20),
    )(sums, small_sums, d_input, activations)
    return outs[:2], outs[2:]


def flat_params(args):
    out = [v.reshape(1, -1) if v.ndim == 1 else v for v in args]
    for i in (5, 11):
        out[i] = out[i].T
    return tuple(out)


def shaped_grads(outs, args):
    out = list(outs)
    for i in (5, 11):
        out[i] = out[i].T
    return tuple(o.reshape(v.shape) for o, v in zip(out, args))


def local_fast(n_dp, *args):
    inputs, lengths, grad_out = args[0], args[1], args[-1]
    teacher, student = args[2:17], args[17:32]
    first, second = flat_params(teacher), flat_params(student)
    full, small, activations, saved = forward_all(lengths, inputs, first, second)
    d_input, sums, small_sums = back_all(lengths, grad_out, full, small, saved)
    (activations, d_input), grads = unpack_all(sums, small_sums, d_input, activations, first, second)
    return (activations, d_input) + shaped_grads(grads[:15], teacher) + shaped_grads(grads[15:], student)


def gather_plain(shard, small):
    rows = lax.all_gather(shard, "dp", axis=1, tiled=True)
    full = lax.all_gather(rows, "tensor", axis=1, tiled=False)
    return full, lax.psum(small, AXES)


def reduce_plain(parts, small):
    outs = []
    for part in parts:
        mine = lax.psum_scatter(part.astype(F32), "tensor", scatter_dimension=0, tiled=True)[0]
        outs.append(lax.psum_scatter(mine, "dp", scatter_dimension=0, tiled=True))
    return jnp.stack(outs), lax.psum(small, AXES)


def layer_norm(residual, gain, shift):
    average = jnp.mean(residual, axis=-1, keepdims=True)
    centred = residual - average
    variance = jnp.mean(centred * centred, axis=-1, keepdims=True)
    return centred * lax.rsqrt(variance + EPS) * gain + shift


def gelu_exact(value):
    return jax.nn.gelu(value, approximate=False)


def ein(spec, a, b):
    return jnp.einsum(spec, a, b, preferred_element_type=F32)


def heads_of(value):
    return value.reshape(value.shape[0], value.shape[1], value.shape[2] // HEAD, HEAD)


def scores_of(queries, keys, valid):
    raw = ein("tqhd,tkhd->thqk", heads_of(queries), heads_of(keys)) * (HEAD**-0.5)
    return jnp.where(valid, raw, NEG)


def layer_forward(rows, groups, small, valid):
    w_attn, w_up, w_down = groups
    width = rows.shape[1]
    half = width // 2
    bq = small[0].reshape(2, 1, half)
    bv = small[1].reshape(2, 1, half)
    bo, g1, s1, bd, g2, s2 = (small[i][None, :] for i in range(2, 8))
    bu = small[8:].reshape(2, 1, -1)
    qkv = ein("nd,tdc->tnc", rows, w_attn[:, :, : 3 * half])
    queries = (qkv[:, :, :half] + bq).astype(BF)
    keys = qkv[:, :, half : 2 * half].astype(BF)
    values = (qkv[:, :, 2 * half :] + bv).astype(BF)
    scores = scores_of(queries, keys, valid)
    row_max = jnp.max(scores, axis=-1, keepdims=True)
    exponent = jnp.exp(scores - row_max)
    total = jnp.sum(exponent, axis=-1, keepdims=True)
    probs = (exponent / total).astype(BF)
    attended = ein("thqk,tkhd->tqhd", probs, heads_of(values)).astype(BF).reshape(queries.shape)
    log_sums = row_max + jnp.log(total)
    branch = ein("tnc,tdc->nd", attended, w_attn[:, :, 3 * half :])
    resid_one = rows.astype(F32) + branch + bo
    hidden = layer_norm(resid_one, g1, s1).astype(BF)
    upward = ein("nd,tdc->tnc", hidden, w_up) + bu
    active = gelu_exact(upward).astype(BF)
    resid_two = hidden.astype(F32) + ein("tnc,tdc->nd", active, w_down) + bd
    result = layer_norm(resid_two, g2, s2)
    saved = (rows, queries, keys, values, attended, log_sums, resid_one, hidden, upward, active, resid_two)
    return result, saved


def layer_backward(d_result, groups, small, saved, valid):
    w_attn, w_up, w_down = groups
    rows, queries, keys, values, attended, log_sums, resid_one, hidden, upward, active, resid_two = saved
    half = rows.shape[1] // 2
    g1, s1, g2, s2 = (small[i] for i in (3, 4, 6, 7))
    _, norm_two_back = jax.vjp(layer_norm, resid_two, g2, s2)
    d_resid_two, d_g2, d_s2 = norm_two_back(d_result)
    d_down = d_resid_two.astype(BF)
    gw_down = ein("nd,tnc->tdc", d_down, active).astype(BF)
    _, gelu_back = jax.vjp(gelu_exact, upward)
    d_up = gelu_back(ein("nd,tdc->tnc", d_down, w_down))[0].astype(BF)
    gw_up = ein("nd,tnc->tdc", hidden, d_up).astype(BF)
    d_bu = jnp.sum(d_up, axis=1, dtype=F32).reshape(4, -1)
    d_hidden = d_resid_two + ein("tnc,tdc->nd", d_up, w_up)
    _, norm_one_back = jax.vjp(layer_norm, resid_one, g1, s1)
    d_resid_one, d_g1, d_s1 = norm_one_back(d_hidden)
    d_branch = d_resid_one.astype(BF)
    gw_out = ein("nd,tnc->tdc", d_branch, attended)
    d_attended = ein("nd,tdc->tnc", d_branch, w_attn[:, :, 3 * half :]).astype(BF)
    probs = jnp.exp(scores_of(queries, keys, valid) - log_sums)
    d_probs = ein("tqhd,tkhd->thqk", heads_of(d_attended), heads_of(values))
    d_scores = (probs * (d_probs - jnp.sum(probs * d_probs, axis=-1, keepdims=True))).astype(BF)
    scale = HEAD**-0.5
    d_queries = (ein("thqk,tkhd->tqhd", d_scores, heads_of(keys)) * scale).astype(BF).reshape(queries.shape)
    d_keys = (ein("thqk,tqhd->tkhd", d_scores, heads_of(queries)) * scale).astype(BF).reshape(queries.shape)
    d_values = ein("thqk,tqhd->tkhd", probs.astype(BF), heads_of(d_attended)).astype(BF).reshape(queries.shape)
    d_qkv = jnp.concatenate([d_queries, d_keys, d_values], axis=2)
    gw_attn = jnp.concatenate([ein("nd,tnc->tdc", rows, d_qkv), gw_out], axis=2).astype(BF)
    d_input = d_resid_one + ein("tnc,tdc->nd", d_qkv, w_attn[:, :, : 3 * half])
    d_small = jnp.concatenate(
        [
            jnp.sum(d_queries, axis=1, dtype=F32).reshape(1, -1),
            jnp.sum(d_values, axis=1, dtype=F32).reshape(1, -1),
            jnp.sum(d_resid_one, axis=0)[None],
            d_g1[None],
            d_s1[None],
            jnp.sum(d_resid_two, axis=0)[None],
            d_g2[None],
            d_s2[None],
            d_bu,
        ],
        axis=0,
    )
    return d_input, (gw_attn, gw_up, gw_down), d_small


def pack_weights(args):
    query_w, _, key_w, value_w, _, out_w, _, _, _, up_w, _, down_w = args[:12]
    return jnp.stack([jnp.concatenate([query_w, key_w, value_w, out_w.T], axis=1), up_w, down_w.T])


def spread(values, where, count):
    n, m = values.shape
    block = jnp.arange(m * count) // m
    return jnp.where(block[None, :] == where, jnp.tile(values.astype(F32), (1, count)), 0.0)


def pack_small(args, dp, n_dp, t):
    query_b, value_b, up_b = args[1], args[4], args[10]
    biases = spread(jnp.concatenate([query_b, value_b], axis=0), t * n_dp + dp, 2 * n_dp)
    norms = spread(jnp.stack([args[6], args[7], args[8], args[12], args[13], args[14]]), 2 * dp + t, 2 * n_dp)
    ups = spread(up_b, t * n_dp + dp, 2 * n_dp).reshape(4, -1)
    return jnp.concatenate([biases, norms, ups], axis=0)


def take(values, where, count):
    n, width = values.shape
    m = width // count
    return lax.dynamic_slice_in_dim(values, where * m, m, 1)


def local_plain(n_dp, *args):
    inputs, lengths, grad_out = args[0], args[1], args[-1]
    teacher, student = args[2:17], args[17:32]
    dp, t = lax.axis_index("dp"), lax.axis_index("tensor")
    seq_len = inputs.shape[0]
    width = inputs.shape[1]
    half = width // 2
    my_length = lax.dynamic_index_in_dim(lengths, t, 0, keepdims=False)
    inside = jnp.arange(seq_len) < my_length
    row_mask = inside.astype(F32)[:, None]
    valid = inside[None, None, None, :]
    shard = jnp.concatenate([pack_weights(teacher), pack_weights(student)], axis=0)
    small = jnp.concatenate([pack_small(teacher, dp, n_dp, t), pack_small(student, dp, n_dp, t)], axis=0)
    full, small = gather_plain(shard, small)
    groups = [tuple(full[3 * layer + i] for i in range(3)) for layer in range(2)]
    smalls = [small[:12], small[12:]]
    result, kept_t = layer_forward(inputs, groups[0], smalls[0], valid)
    result, kept_s = layer_forward(result.astype(BF), groups[1], smalls[1], valid)
    activations = (result * row_mask).astype(BF)
    d_current = grad_out.astype(F32) * row_mask
    d_current, parts_s, small_s = layer_backward(d_current, groups[1], smalls[1], kept_s, valid)
    d_current, parts_t, small_t = layer_backward(d_current, groups[0], smalls[0], kept_t, valid)
    order = (parts_s[2], parts_s[1], parts_s[0], parts_t[2], parts_t[1], parts_t[0])
    sums, small_sums = reduce_plain(order, jnp.concatenate([small_t, small_s], axis=0))
    outs = [activations, d_current]
    for layer in range(2):
        base = 3 * (1 - layer)
        g_down, g_up, g_attn = sums[base], sums[base + 1], sums[base + 2]
        part = small_sums[12 * layer : 12 * layer + 12]
        biases = take(part[0:2], t * n_dp + dp, 2 * n_dp)
        norms = take(part[2:8], 2 * dp + t, 2 * n_dp)
        ups = take(part[8:12].reshape(1, -1), t * n_dp + dp, 2 * n_dp)
        outs += [
            g_attn[:, :half],
            biases[0:1],
            g_attn[:, half : 2 * half],
            g_attn[:, 2 * half : 3 * half],
            biases[1:2],
            g_attn[:, 3 * half :].T,
            norms[0],
            norms[1],
            norms[2],
            g_up,
            ups,
            g_down.T,
            norms[3],
            norms[4],
            norms[5],
        ]
    return tuple(outs)


def solution(mesh):
    n_dp = mesh.shape["dp"]
    fast = n_dp == NZ * NY * NC and mesh.shape["tensor"] == NX
    row = P(AXES, None)
    vec = P(AXES)
    cut_in, cut_out = P("dp", "tensor"), P("tensor", "dp")
    layer = (cut_in, cut_out, cut_in, cut_in, cut_out, cut_out, vec, vec, vec, cut_in, cut_out, cut_out, vec, vec, vec)
    return jax.shard_map(
        functools.partial(local_fast if fast else local_plain, n_dp),
        mesh=mesh,
        in_specs=(row, P("dp")) + layer + layer + (row,),
        out_specs=(row, row) + layer + layer,
        check_vma=False,
    )
```

```python
import functools

import jax
import jax.numpy as jnp
from jax import lax
from jax.experimental import pallas as pl
from jax.experimental.pallas import tpu as pltpu
from jax.sharding import PartitionSpec as P

HEAD = 64
EPS = 1e-06
NEG = -1e30
NZ, NY, NC, NX = 4, 2, 2, 2
MESH = pl.DeviceIdType.MESH
BF = jnp.bfloat16
F32 = jnp.float32
AXES = ("dp", "tensor")


def place():
    dp = lax.axis_index("dp")
    t = lax.axis_index("tensor")
    return dp // 4, lax.rem(dp // 2, 2), lax.rem(dp, 2), t


def device(z, y, c, t):
    return {"dp": z * 4 + y * 2 + c, "tensor": t}


def greet(others):
    barrier = pltpu.get_barrier_semaphore()
    for other in others:
        pl.semaphore_signal(barrier, inc=1, device_id=other, device_id_type=MESH)
    pl.semaphore_wait(barrier, len(others))


def send(src, dst, sems, index, other):
    copy = pltpu.make_async_remote_copy(
        src_ref=src,
        dst_ref=dst,
        send_sem=sems[0].at[index],
        recv_sem=sems[1].at[index],
        device_id=other,
        device_id_type=MESH,
    )
    copy.start()
    return copy


def partners():
    z, y, c, t = place()
    core = device(z, y, 1 - c, t)
    over_x = device(z, y, c, 1 - t)
    over_y = device(z, 1 - y, c, t)
    over_z = [device(lax.rem(z + j, NZ), y, c, t) for j in range(1, NZ)]
    return core, over_x, over_y, over_z


def small_sum(src, dst, got, acc, sems):
    core, over_x, over_y, over_z = partners()
    now = src
    for step, other in enumerate((core, over_x, over_y)):
        send(now, got.at[step], sems, step, other).wait()
        acc[step] = now[...] + got[step]
        now = acc.at[step]
    copies = [send(now, got.at[3 + j], sems, 3 + j, other) for j, other in enumerate(over_z)]
    for copy in copies:
        copy.wait()
    dst[...] = now[...] + got[3] + got[4] + got[5]


def mm(a, b):
    return jnp.dot(a, b, preferred_element_type=F32)


def mm_nt(a, b):
    return lax.dot_general(a, b, (((1,), (1,)), ((), ())), preferred_element_type=F32)


def gelu_both(u):
    bell = jnp.exp(u * u * -0.5)
    t = 1.0 / (1.0 + (0.3275911 * 0.7071067811865476) * jnp.abs(u))
    tail = 1.061405429 * 0.5 * t - 1.453152027 * 0.5
    tail = tail * t + 1.421413741 * 0.5
    tail = tail * t - 0.284496736 * 0.5
    tail = (tail * t + 0.254829592 * 0.5) * t * bell
    cdf = jnp.where(u < 0, tail, 1.0 - tail)
    return u * cdf, cdf + u * bell * 0.3989422804014327


def norm_parts(r):
    average = jnp.mean(r, axis=-1, keepdims=True)
    centred = r - average
    variance = jnp.mean(centred * centred, axis=-1, keepdims=True)
    rstd = lax.rsqrt(variance + EPS)
    return centred * rstd, rstd


def block(i, n):
    return pl.ds(pl.multiple_of(i * n, n), n)


FWAVES = 12
AHEAD = 2
BULK = (5, 7, 9, 10)
SIDE = FWAVES - 1


def gather_steps(shard, full, own_sem, sems, side_sems):
    z, y, c, t = place()
    core, over_x, over_y, over_z = partners()
    half = shard.shape[2] // 2
    lo, hi = pl.ds(0, half), pl.ds(half, half)
    owns, first, second, third, last = {}, {}, {}, {}, {}

    def one(k):
        owns[k] = pltpu.make_async_copy(shard.at[k], full.at[k, t, z, y, c], own_sem.at[k])
        owns[k].start()
        first[k] = [
            send(shard.at[k], full.at[k, t, z, y, c], sems, (k, j), other)
            for j, other in enumerate(over_z)
        ]

    def two(k):
        owns[k].wait()
        for copy in first[k]:
            copy.wait()
        a = full.at[k, t, :, y, c, :, lo]
        b = full.at[k, t, :, y, c, :, hi]
        second[k] = [send(a, a, sems, (k, 3), over_y), send(b, b, sems, (k, 4), over_x)]

    def three(k):
        for copy in second[k]:
            copy.wait()
        a = full.at[k, t, :, :, c, :, lo]
        b = full.at[k, :, :, y, c, :, hi]
        third[k] = [send(a, a, sems, (k, 5), over_x), send(b, b, sems, (k, 6), over_y)]

    def four(k):
        for copy in third[k]:
            copy.wait()
        a = full.at[k, :, :, :, c]
        last[k] = send(a, a, sems, (k, 7), core)

    def five(k):
        last[k].wait()

    side = {}

    def side_one():
        owns[SIDE] = pltpu.make_async_copy(shard.at[SIDE], full.at[SIDE, t, z, y, c], own_sem.at[SIDE])
        owns[SIDE].start()
        mine = full.at[SIDE, t, z, y, c]
        side[1] = [
            send(shard.at[SIDE, :, lo], mine.at[:, lo], side_sems, 0, over_x),
            send(shard.at[SIDE, :, hi], mine.at[:, hi], side_sems, 1, over_y),
        ]

    def side_two():
        owns[SIDE].wait()
        for copy in side[1]:
            copy.wait()
        a = full.at[SIDE, :, z, y, c, :, lo]
        b = full.at[SIDE, t, z, :, c, :, hi]
        side[2] = [send(a, a, side_sems, 2, over_y), send(b, b, side_sems, 3, over_x)]

    def side_three(i):
        if i == 0:
            for copy in side[2]:
                copy.wait()
            side[3] = []
        a = full.at[SIDE, i // 2, z, i % 2, c]
        side[3] += [send(a, a, side_sems, 4 + 3 * i + j, other) for j, other in enumerate(over_z)]

    def side_four():
        for copy in side[3]:
            copy.wait()
        a = full.at[SIDE, :, :, :, c]
        last[SIDE] = send(a, a, sems, (SIDE, 7), core)

    return one, two, three, four, five, (side_one, side_two, side_three, side_four)


def sum_steps(src, dst, got, acc, sems):
    core, over_x, over_y, over_z = partners()
    flying = {}

    def begin():
        flying[0] = [send(src, got.at[0], sems, 0, core)]

    def middle(step, other):
        for copy in flying[step - 1]:
            copy.wait()
        before = src if step == 1 else acc.at[step - 2]
        acc[step - 1] = before[...] + got[step - 1]
        if step < 3:
            flying[step] = [send(acc.at[step - 1], got.at[step], sems, step, other)]
        else:
            flying[step] = [send(acc.at[2], got.at[3 + j], sems, 3 + j, o) for j, o in enumerate(over_z)]

    def end():
        for copy in flying[3]:
            copy.wait()
        dst[...] = acc[2] + got[3] + got[4] + got[5]

    return [begin, lambda: middle(1, over_x), lambda: middle(2, over_y), lambda: middle(3, None), end]


SAVED = ("x", "q", "k", "v", "probs", "o", "z1", "rstd1", "h", "g", "gp", "z2", "rstd2")


def pack_copies(raw, shard, r_bias, r_up, r_norm, sem):
    pieces = {"small": []}
    width = shard.shape[2]
    half = width // 2
    count = 0

    def copy(src, dst):
        nonlocal count
        count += 1
        return pltpu.make_async_copy(src, dst, sem.at[count - 1])

    for layer in range(2):
        wq, bq, wk, wv, bv, wo, bo, g1, s1, wu, bu, wd, bd, g2, s2 = raw[layer]
        at = 6 * layer
        pieces[f"qk{layer}"] = [copy(wq, shard.at[at, :, :half]), copy(wk, shard.at[at, :, half:])]
        pieces[f"vo{layer}"] = [copy(wv, shard.at[at + 1, :, :half]), copy(wo, shard.at[at + 1, :, half:])]
        pieces[f"u{layer}"] = [
            copy(wu.at[:, :width], shard.at[at + 2]),
            copy(wu.at[:, width:], shard.at[at + 3]),
        ]
        pieces[f"d{layer}"] = [
            copy(wd.at[:, :width], shard.at[at + 4]),
            copy(wd.at[:, width:], shard.at[at + 5]),
        ]
        pieces["small"] += [copy(bq, r_bias.at[2 * layer]), copy(bv, r_bias.at[2 * layer + 1])]
        pieces["small"] += [copy(bu, r_up.at[layer])]
        pieces["small"] += [copy(v, r_norm.at[6 * layer + i]) for i, v in enumerate((bo, g1, s1, bd, g2, s2))]
    return pieces


def one_hot(rows, columns, start, axis):
    a = lax.broadcasted_iota(jnp.int32, (rows, columns), axis)
    b = lax.broadcasted_iota(jnp.int32, (rows, columns), 1 - axis)
    return jnp.where(a == b + start, 1.0, 0.0).astype(F32)


def mm_exact(a, b):
    return jnp.dot(a, b, preferred_element_type=F32, precision=lax.Precision.HIGHEST)


def spread_small(small, r_bias, r_up, r_norm, dp, t, n_dp):
    width = small.shape[1]
    m = r_norm.shape[2]
    to_norm = one_hot(m, width, (2 * dp + t) * m, 1)
    to_bias = one_hot(m, width, (t * n_dp + dp) * m, 1)
    many = r_up.shape[2]
    biases = mm_exact(jnp.concatenate([r_bias[i].astype(F32) for i in range(4)], axis=0), to_bias)
    norms = mm_exact(jnp.concatenate([r_norm[i] for i in range(12)], axis=0), to_norm)
    ups = jnp.concatenate([r_up[i].astype(F32) for i in range(2)], axis=0)
    for layer in range(2):
        at = 12 * layer
        small[at : at + 2, :] = biases[2 * layer : 2 * layer + 2]
        small[at + 2 : at + 8, :] = norms[6 * layer : 6 * layer + 6]
    for i in range(4):
        r = mm_exact(ups, one_hot(many, width, (t * n_dp + dp) * many - i * width, 1))
        for layer in range(2):
            small[12 * layer + 8 + i : 12 * layer + 9 + i, :] = r[layer : layer + 1]


def forward_kernel(*refs):
    lengths, rows = refs[:2]
    raw = [refs[2 + 15 * i : 17 + 15 * i] for i in range(2)]
    refs = refs[32:]
    full, small_out, act_out = refs[:3]
    saves = [dict(zip(SAVED, refs[3 + 13 * i : 16 + 13 * i])) for i in range(2)]
    refs = refs[29:]
    shard, small, r_bias, r_up, r_norm, raw_sem, x_sem = refs[:7]
    refs = refs[7:]
    bufs = dict(zip(SAVED, refs[:13]))
    bias, vt, ot, r2, w_slots, got, acc, s_send, s_recv, own_sem, b_send, b_recv, c_send, c_recv, load_sem, save_sem = refs[13:]
    z, y, c, t_mine = place()
    dp = lax.axis_index("dp")
    core, over_x, over_y, over_z = partners()
    pieces = pack_copies(raw, shard, r_bias, r_up, r_norm, raw_sem)
    x_copy = pltpu.make_async_copy(rows, bufs["x"], x_sem)
    for name in ("qk0", "d1", "small", "vo0", "u0", "d0", "qk1", "vo1", "u1"):
        for copy in pieces[name]:
            copy.start()
        if name == "vo0":
            x_copy.start()
    greet([core, over_x, over_y] + over_z)
    one, two, three, four, five, side = gather_steps(
        shard, full, own_sem, (b_send, b_recv), (c_send, c_recv)
    )
    sums = sum_steps(small, small_out, got, acc, (s_send, s_recv))
    loads, stores = {}, {}
    n, width = rows.shape
    half = width // 2

    def packed(name):
        for copy in pieces[name]:
            copy.wait()

    packed("qk0")
    one(0)
    packed("d1")
    side[0]()
    packed("small")
    n_dp = lax.axis_size("dp")
    spread_small(small, r_bias, r_up, r_norm, dp, t_mine, n_dp)
    sums[0]()
    side[1]()
    packed("vo0")
    one(1)
    x_copy.wait()
    for name in ("u0", "d0", "qk1", "vo1", "u1"):
        packed(name)
    length = lengths[t_mine]
    inside = lax.broadcasted_iota(jnp.int32, (n, 1), 0) < length
    bias[...] = jnp.where(inside, 0.0, NEG)

    def bring(k):
        five(k)
        loads[k] = pltpu.make_async_copy(full.at[k], w_slots.at[k % 2], load_sem.at[k % 2])
        loads[k].start()

    def comm(step):
        if step + 1 < len(sums):
            sums[step + 1]()
        if step < SIDE:
            two(step)
            if step + AHEAD < SIDE:
                one(step + AHEAD)
        if step in BULK:
            side[2](BULK.index(step))
        if 0 <= step - 1 < SIDE:
            three(step - 1)
        if step == SIDE:
            side[3]()
        if 0 <= step - 2 < SIDE:
            four(step - 2)
        if 0 <= step - 3 < SIDE - 1:
            bring(step - 3)

    def weights(k):
        loads[k].wait()
        slot = w_slots.at[k % 2]
        return lambda t, lanes: slot[t, :, :, :, :, lanes].reshape(width, -1)

    def save(layer, *names):
        for name in names:
            copy = pltpu.make_async_copy(bufs[name], saves[layer][name], save_sem.at[SAVED.index(name)])
            copy.start()
            stores[name] = copy

    def free(*names):
        for name in names:
            if name in stores:
                stores.pop(name).wait()

    def vec(layer, i):
        return small_out[12 * layer + i : 12 * layer + i + 1]

    def scores_stage(layer, k):
        w = weights(k)
        x, q, kk, probs = (bufs[i] for i in ("x", "q", "k", "probs"))
        free("q", "k", "probs")
        for t in range(2):
            here = slice(t * half, (t + 1) * half)
            r = mm(x[...], w(t, slice(0, half))) + vec(layer, 0)[:, here]
            q[:, here] = r.astype(BF) * BF(HEAD**-0.5)
            kk[:, here] = mm(x[...], w(t, slice(half, width))).astype(BF)
        save(layer, "q", "k")
        lane = lax.broadcasted_iota(jnp.int32, (1, 128), 1)

        @pl.loop(0, width // 128)
        def _(p):
            kp = kk[:, block(p, 128)]
            qp = q[:, block(p, 128)]
            for head in range(2):
                qm = jnp.where((lane >= HEAD) == (head == 1), qp, BF(0))
                s = mm_nt(kp, qm) + bias[...]
                e = jnp.exp(s - jnp.max(s, axis=0, keepdims=True))
                probs[2 * p + head] = (e * (1.0 / jnp.sum(e, axis=0, keepdims=True))).astype(BF)

        save(layer, "probs")

    def attend_stage(layer, k):
        w = weights(k)
        x, v, probs, o, z1, rstd1, h = (bufs[i] for i in ("x", "v", "probs", "o", "z1", "rstd1", "h"))
        free("v", "o", "z1", "rstd1", "h")
        for t in range(2):
            here = slice(t * half, (t + 1) * half)
            r = mm(x[...], w(t, slice(0, half))) + vec(layer, 1)[:, here]
            v[:, here] = r.astype(BF)
        save(layer, "v")
        vt[...] = v[...].T

        @pl.loop(0, width // HEAD)
        def _(i):
            ot[block(i, HEAD), :] = mm(vt[block(i, HEAD), :], probs[i]).astype(BF)

        o[...] = ot[...].T
        save(layer, "o")
        r = x[...].astype(F32) + vec(layer, 2)
        for t in range(2):
            r = r + mm_nt(o[:, t * half : (t + 1) * half], w(t, slice(half, width)))
        z, rstd = norm_parts(r)
        z1[...] = z.astype(BF)
        rstd1[...] = rstd
        h[...] = (z * vec(layer, 3) + vec(layer, 4)).astype(BF)
        save(layer, "x", "z1", "rstd1", "h")

    def up_stage(layer, k, part):
        w = weights(k)
        h, g, gp = (bufs[i] for i in ("h", "g", "gp"))
        if part == 0:
            free("g", "gp")
        step = 384
        for t in range(2):

            @pl.loop(0, width // step)
            def _(i):
                at = t * 2 * width + part * width + i * step
                here = pl.ds(pl.multiple_of(part * width + i * step, step), step)
                u = mm(h[...], w(t, block(i, step)))
                bu = bu_row(layer, t, part, i, step)
                a, b = gelu_both(u + bu)
                g[t, :, here] = a.astype(BF)
                gp[t, :, here] = b.astype(BF)

        if part == 1:
            save(layer, "g", "gp")

    def bu_row(layer, t, part, i, step):
        return small_out[pl.ds(12 * layer + 8 + 2 * t + part, 1), block(i, step)]

    def down_stage(layer, k, part):
        w = weights(k)
        h, g, z2, rstd2 = (bufs[i] for i in ("h", "g", "z2", "rstd2"))
        here = slice(part * width, (part + 1) * width)
        total = None
        for t in range(2):
            r = mm_nt(g[t, :, here], w(t, slice(0, width)))
            total = r if total is None else total + r
        if part == layer:
            r2[...] = total
            return
        free("z2", "rstd2", "x")
        r = r2[...] + total + h[...].astype(F32) + vec(layer, 5)
        z, rstd = norm_parts(r)
        z2[...] = z.astype(BF)
        rstd2[...] = rstd
        result = z * vec(layer, 6) + vec(layer, 7)
        save(layer, "z2", "rstd2")
        if layer == 0:
            bufs["x"][...] = result.astype(BF)
        else:
            act_out[...] = jnp.where(inside, result, 0.0).astype(BF)

    def compute(k):
        layer, i = k // 6, k % 6
        if i == 0:
            scores_stage(layer, k)
        elif i == 1:
            attend_stage(layer, k)
        elif i < 4:
            up_stage(layer, k, i - 2)
        else:
            down_stage(layer, k, i - 4)

    for step in range(SIDE + 3):
        comm(step)
        if step >= 4:
            compute(step - 4)
    for k in (SIDE, SIDE - 1):
        bring(k)
        compute(k)
    free(*list(stores))


def saved_kinds(n, width):
    heads = width // HEAD
    return {
        "x": ((n, width), BF),
        "q": ((n, width), BF),
        "k": ((n, width), BF),
        "v": ((n, width), BF),
        "probs": ((heads, n, n), BF),
        "o": ((n, width), BF),
        "z1": ((n, width), BF),
        "rstd1": ((n, 1), F32),
        "h": ((n, width), BF),
        "g": ((2, n, 2 * width), BF),
        "gp": ((2, n, 2 * width), BF),
        "z2": ((n, width), BF),
        "rstd2": ((n, 1), F32),
    }


def forward_all(lengths, rows, teacher, student):
    n, width = rows.shape
    part = teacher[0].shape[0]
    waves, cols = FWAVES, width
    raw = teacher + student
    few, many = raw[1].shape[1], raw[10].shape[1]
    small = jax.ShapeDtypeStruct((24, width), F32)
    kinds = saved_kinds(n, width)
    dma = pltpu.SemaphoreType.DMA
    hbm = pl.BlockSpec(memory_space=pltpu.MemorySpace.HBM)
    vmem = pl.BlockSpec(memory_space=pltpu.VMEM)
    shape = jax.ShapeDtypeStruct
    outs = pl.pallas_call(
        forward_kernel,
        out_shape=(
            shape((waves, NX, NZ, NY, NC, part, cols), BF),
            shape(small.shape, F32),
            shape((n, width), BF),
        )
        + tuple(shape(*kinds[name]) for name in SAVED) * 2,
        in_specs=[pl.BlockSpec(memory_space=pltpu.SMEM)] + [hbm] * 31,
        out_specs=(hbm, vmem, vmem) + (hbm,) * 26,
        scratch_shapes=[
            pltpu.VMEM((waves, part, cols), BF),
            pltpu.VMEM(small.shape, F32),
            pltpu.VMEM((4, 1, few), BF),
            pltpu.VMEM((2, 1, many), BF),
            pltpu.VMEM((12, 1, few), F32),
            dma((34,)),
            dma(()),
        ]
        + [pltpu.VMEM(*kinds[name]) for name in SAVED]
        + [
            pltpu.VMEM((n, 1), F32),
            pltpu.VMEM((width, n), BF),
            pltpu.VMEM((width, n), BF),
            pltpu.VMEM((n, width), F32),
            pltpu.VMEM((2, NX, NZ, NY, NC, part, cols), BF),
            pltpu.VMEM((6,) + small.shape, F32),
            pltpu.VMEM((3,) + small.shape, F32),
            dma((6,)),
            dma((6,)),
            dma((waves,)),
            dma((waves, 8)),
            dma((waves, 8)),
            dma((16,)),
            dma((16,)),
            dma((2,)),
            dma((13,)),
        ],
        name="forward_all",
        compiler_params=pltpu.CompilerParams(
            collective_id=0, has_side_effects=True, vmem_limit_bytes=60 << 20
        ),
    )(lengths, rows, *raw)
    full, small, activations = outs[:3]
    saved = [dict(zip(SAVED, outs[3 + 13 * i : 16 + 13 * i])) for i in range(2)]
    return full, small, activations, saved


ORDER = [6 + i for i in (4, 5, 2, 3, 1, 0)] + [4, 5, 2, 3, 1, 0]
RC, R2S, R3S = 7, 3, 3
TURN = 1
RESTS = 16
WAITS = (1, 5, 4, 8)
LAST = FWAVES - 1
CUTS = 3


def reduce_steps(stage, rc, r2a, r2b, r3a, r3b, r4, rz, ra, rb, out, credit, sems, t_sems):
    z, y, c, t = place()
    core, over_x, over_y, over_z = partners()
    half = out.shape[2] // 2
    lo, hi = pl.ds(0, half), pl.ds(half, half)
    flying = {}

    def rest():
        pass

    def wait(key):
        for copy in flying.pop(key):
            copy.wait()

    def give(kind, other):
        pl.semaphore_signal(credit.at[kind], inc=1, device_id=other, device_id_type=MESH)

    def add(dst, *srcs):
        total = dst[...]
        for src in srcs:
            total = total + src[...]
        dst[...] = total

    def own(s, j, lanes):
        @pl.loop(0, NZ)
        def _(i):
            for a in range(NX):
                for b in range(NY):
                    for lane in lanes:
                        add(rc.at[s, a, i, b, :, lane], stage.at[j % 2, a, i, b, c, :, lane])

    def steps(j, cut=None):
        n = j if TURN < 0 or j < TURN else j - 1
        total = FWAVES - (TURN >= 0)
        key, s, s2, s3 = (j, cut), n % RC, n % R2S, n % R3S
        row = j if cut is None else FWAVES + cut
        first = cut in (None, 0)
        width = half if cut is None else half // CUTS
        at = 0 if cut is None else cut * width
        low, high = pl.ds(at, width), pl.ds(half + at, width)
        spans = [pl.ds(0, 2 * half)] if cut is None else [low, high]

        def one():
            if n >= RC and first:
                pl.semaphore_wait(credit.at[0], 1)
            flying[key] = [
                send(stage.at[j % 2, :, :, :, 1 - c, :, lanes], rc.at[s, :, :, :, :, lanes], sems, (row, i), core)
                for i, lanes in enumerate(spans)
            ]

        def two():
            wait(key)
            own(s, j, spans)
            if n >= R2S and first:
                pl.semaphore_wait(credit.at[1], 1)
                pl.semaphore_wait(credit.at[2], 1)
            flying[key] = [
                send(rc.at[s, 1 - t, :, :, :, low], r2a.at[s2, :, :, :, low], sems, (row, 2), over_x),
                send(rc.at[s, :, :, 1 - y, :, high], r2b.at[s2, :, :, :, low], sems, (row, 3), over_y),
            ]

        def three():
            wait(key)

            @pl.loop(0, NZ)
            def _(i):
                for b in range(2):
                    add(rc.at[s, t, i, b, :, low], r2a.at[s2, i, b, :, low])
                    add(rc.at[s, b, i, y, :, high], r2b.at[s2, b, i, :, low])

            if n + R2S < total:
                give(1, over_x)
                give(2, over_y)
            if n >= R3S and first:
                pl.semaphore_wait(credit.at[3], 1)
                pl.semaphore_wait(credit.at[4], 1)
            flying[key] = [
                send(rc.at[s, t, :, 1 - y, :, low], r3a.at[s3, :, :, low], sems, (row, 4), over_y),
                send(rc.at[s, 1 - t, :, y, :, high], r3b.at[s3, :, :, low], sems, (row, 5), over_x),
            ]

        def four():
            wait(key)

            @pl.loop(0, NZ)
            def _(i):
                add(rc.at[s, t, i, y, :, low], r3a.at[s3, i, :, low])
                add(rc.at[s, t, i, y, :, high], r3b.at[s3, i, :, low])

            if n + R3S < total:
                give(3, over_y)
                give(4, over_x)
            flying[key] = [
                send(
                    rc.at[s, t, lax.rem(z + i + 1, NZ), y, :, lanes],
                    r4.at[n, i, :, lanes],
                    sems,
                    (row, 6 + 3 * k + i),
                    other,
                )
                for i, other in enumerate(over_z)
                for k, lanes in enumerate(spans)
            ]

        def five():
            wait(key)
            for lanes in spans:
                value = rc[s, t, z, y, :, lanes].astype(F32)
                for i in range(3):
                    value = value + r4[n, i, :, lanes].astype(F32)
                out[ORDER[j], :, lanes] = value
            if n + RC < total:
                give(0, core)

        return [one] + [rest] * WAITS[0] + [two] + [rest] * WAITS[1] + [three] + [rest] * WAITS[2] + [four] + [rest] * WAITS[3] + [five]

    def turned(j):
        s = RC

        def one():
            flying[j] = [send(stage.at[j % 2, :, :, :, 1 - c], rc.at[s], t_sems, 0, core)]

        def two():
            wait(j)
            own(s, j, [pl.ds(0, 2 * half)])
            flying[j] = [
                send(rc.at[s, :, lax.rem(z + i + 1, NZ)], rz.at[i], t_sems, 1 + i, other)
                for i, other in enumerate(over_z)
            ]

        def three():
            wait(j)
            for a in range(NX):
                for b in range(NY):
                    add(rc.at[s, a, z, b], rz.at[0, a, b], rz.at[1, a, b], rz.at[2, a, b])
            flying[j] = [
                send(rc.at[s, 1 - t, z, :, :, lo], ra.at[0:2], t_sems, 4, over_x),
                send(rc.at[s, :, z, 1 - y, :, hi], rb.at[0:2], t_sems, 5, over_y),
            ]

        def four():
            wait(j)
            for b in range(2):
                add(rc.at[s, t, z, b, :, lo], ra.at[b])
                add(rc.at[s, b, z, y, :, hi], rb.at[b])
            flying[j] = [
                send(rc.at[s, t, z, 1 - y, :, lo], ra.at[2], t_sems, 6, over_y),
                send(rc.at[s, 1 - t, z, y, :, hi], rb.at[2], t_sems, 7, over_x),
            ]

        def five():
            wait(j)
            out[ORDER[j], :, lo] = rc[s, t, z, y, :, lo].astype(F32) + ra[2].astype(F32)
            out[ORDER[j], :, hi] = rc[s, t, z, y, :, hi].astype(F32) + rb[2].astype(F32)

        return [one, two] + [rest] * RESTS + [three, rest, rest, four, rest, rest, five]

    return steps, turned, rest


def back_kernel(*refs):
    lengths, grad, small, full = refs[:4]
    saves = [dict(zip(SAVED, refs[4 + 13 * i : 17 + 13 * i])) for i in range(2)]
    refs = refs[30:]
    d_input, out, small_out = refs[:3]
    refs = refs[3:]
    bufs = dict(zip(SAVED, refs[:13]))
    refs = refs[13:]
    dy, dr, dlo, lot, dlot, d_o, dq, dk, dv, kt, dqt = refs[:11]
    refs = refs[11:]
    w_slots, stage, rc, r2a, r2b, r3a, r3b, r4, rz, ra, rb, terms, got, acc = refs[:14]
    s_send, s_recv, b_send, b_recv, t_send, t_recv, credit, load_sem, w_sem = refs[14:]
    core, over_x, over_y, over_z = partners()
    n, width = grad.shape
    half = width // 2
    loads, w_loads = {}, {}

    def load(layer, *names):
        for name in names:
            copy = pltpu.make_async_copy(saves[layer][name], bufs[name], load_sem.at[SAVED.index(name)])
            copy.start()
            loads[name] = copy

    def need(*names):
        for name in names:
            if name in loads:
                loads.pop(name).wait()

    def fetch(j):
        if j < FWAVES:
            w_loads[j] = pltpu.make_async_copy(full.at[ORDER[j]], w_slots.at[j % 2], w_sem.at[j % 2])
            w_loads[j].start()

    def weights(j):
        w_loads[j].wait()
        slot = w_slots.at[j % 2]
        return lambda t, lanes: slot[t, :, :, :, :, lanes].reshape(width, -1)

    load(1, "z2", "rstd2")
    fetch(0)
    load(1, "g", "gp", "h", "z1", "rstd1")
    fetch(1)
    load(1, "o", "probs", "x", "v", "k", "q")
    greet([core, over_x, over_y] + over_z)
    steps, turned, rest = reduce_steps(
        stage, rc, r2a, r2b, r3a, r3b, r4, rz, ra, rb, out, credit, (b_send, b_recv), (t_send, t_recv)
    )
    moving = []

    def advance():
        for item in moving:
            item.pop(0)()
        moving[:] = [item for item in moving if item]

    def comm(j, cut=None):
        advance()
        item = turned(j) if j == TURN else steps(j, cut)
        item.pop(0)()
        moving.append(item)

    def put(j, t, lanes, value):
        stage[j % 2, t, :, :, :, :, lanes] = value.astype(BF).reshape(NZ, NY, NC, -1, value.shape[1])

    def term(layer, i, value):
        terms[12 * layer + i : 12 * layer + i + 1, :] = value

    def vec(layer, i):
        return small[12 * layer + i : 12 * layer + i + 1]

    def norm_back(layer, at, d_out, z, rstd):
        zf = z[...].astype(F32)
        dz = d_out * vec(layer, at + 1)
        a = jnp.mean(dz, axis=-1, keepdims=True)
        b = jnp.mean(dz * zf, axis=-1, keepdims=True)
        d_in = rstd[...] * (dz - a - zf * b)
        term(layer, at, jnp.sum(d_in, axis=0, keepdims=True))
        term(layer, at + 1, jnp.sum(d_out * zf, axis=0, keepdims=True))
        term(layer, at + 2, jnp.sum(d_out, axis=0, keepdims=True))
        dr[...] = d_in
        low = d_in.astype(BF)
        dlo[...] = low
        dlot[...] = low.T

    def down_stage(layer, j, part):
        g, gp = bufs["g"], bufs["gp"]
        if part == 0:
            need("z2", "rstd2")
            norm_back(layer, 5, dy[...], bufs["z2"], bufs["rstd2"])
            need("g", "gp")
        w = weights(j)
        here = slice(part * width, (part + 1) * width)
        for t in range(2):
            put(j, t, slice(0, width), mm(dlot[...], g[t, :, here]))
            if t == 0:
                advance()
        comm(j)
        for t in range(2):
            if t == 1:
                advance()
            du = (mm(dlo[...], w(t, slice(0, width))) * gp[t, :, here].astype(F32)).astype(BF)
            gp[t, :, here] = du
            term(layer, 8 + 2 * t + part, jnp.sum(du.astype(F32), axis=0, keepdims=True))
        fetch(j + 2)
        if part == 1 and layer == 1:
            load(0, "z2", "rstd2", "g")

    def up_stage(layer, j, part):
        h, gp = bufs["h"], bufs["gp"]
        if part == 0:
            need("h")
            lot[...] = h[...].T
        w = weights(j)
        here = slice(part * width, (part + 1) * width)
        for t in range(2):
            put(j, t, slice(0, width), mm(lot[...], gp[t, :, here]))
            if t == 0:
                advance()
        comm(j)
        for t in range(2):
            if t == 1:
                advance()
            dr[...] = dr[...] + mm_nt(gp[t, :, here], w(t, slice(0, width)))
        fetch(j + 2)
        if part == 0:
            return
        total = dr[...]
        need("z1", "rstd1")
        norm_back(layer, 2, total, bufs["z1"], bufs["rstd1"])
        if layer == 1:
            load(0, "gp", "h", "z1", "rstd1")

    lane = lax.broadcasted_iota(jnp.int32, (1, 128), 1)

    def of_head(head, value):
        return jnp.where((lane >= HEAD) == (head == 1), value, BF(0))

    def value_stage(layer, j):
        o, probs, x = bufs["o"], bufs["probs"], bufs["x"]
        w = weights(j)
        need("o", "probs", "x")
        for t in range(2):
            here = slice(t * half, (t + 1) * half)
            put(j, t, slice(half, width), mm(dlot[...], o[:, here]))
            d_o[:, here] = mm(dlo[...], w(t, slice(half, width))).astype(BF)
        lot[...] = x[...].T
        advance()

        @pl.loop(0, width // 128)
        def _(p):
            dop = d_o[:, block(p, 128)]
            total = mm(probs[2 * p], of_head(0, dop)) + mm(probs[2 * p + 1], of_head(1, dop))
            dv[:, block(p, 128)] = total.astype(BF)

        advance()
        for t in range(2):
            put(j, t, slice(0, half), mm(lot[...], dv[:, t * half : (t + 1) * half]))
        comm(j)
        total = dr[...]
        for t in range(2):
            total = total + mm_nt(dv[:, t * half : (t + 1) * half], w(t, slice(0, half)))
        dr[...] = total
        advance()
        term(layer, 1, jnp.sum(dv[...].astype(F32), axis=0, keepdims=True))
        fetch(j + 2)
        if layer == 1:
            load(0, "o", "x")

    def score_stage(layer, j):
        probs, q, k, v = (bufs[i] for i in ("probs", "q", "k", "v"))
        w = weights(j)
        need("q", "k", "v")
        kt[...] = k[...].T

        def pair(p):
            dop = d_o[:, block(p, 128)]
            qp = q[:, block(p, 128)]
            vp = v[:, block(p, 128)]
            total = None
            for head in range(2):
                dp = mm_nt(vp, of_head(head, dop))
                pr = probs[2 * p + head].astype(F32)
                delta = jnp.sum(pr * dp, axis=0, keepdims=True)
                ds = (pr * (dp - delta)).astype(BF)
                r = mm(ds, of_head(head, qp))
                total = r if total is None else total + r
                rows = block(2 * p + head, HEAD)
                dqt[rows, :] = (mm(kt[rows, :], ds) * (HEAD**-0.5)).astype(BF)
            dk[:, block(p, 128)] = total.astype(BF)

        def stage_cols(cut, n):
            for t in range(2):
                here = slice(t * half + cut * n, t * half + (cut + 1) * n)
                put(j, t, slice(cut * n, (cut + 1) * n), mm(lot[...], dq[:, here]))
                put(j, t, slice(half + cut * n, half + (cut + 1) * n), mm(lot[...], dk[:, here]))

        if j < LAST:
            for i in range(0, width // 128, 2):
                pl.loop(i, i + 2)(pair)
                advance()
            dq[...] = dqt[...].T
            stage_cols(0, half)
            comm(j)
        else:
            n = half // CUTS
            for cut in range(CUTS):

                @pl.loop(0, 2)
                def _(t):
                    p = t * CUTS + cut
                    pair(p)
                    dq[:, block(p, n)] = dqt[block(p, n), :].T

                stage_cols(cut, n)
                comm(j, cut)
        total = dr[...]
        for t in range(2):
            here = slice(t * half, (t + 1) * half)
            total = total + mm_nt(dq[:, here], w(t, slice(0, half)))
            total = total + mm_nt(dk[:, here], w(t, slice(half, width)))
        term(layer, 0, jnp.sum(dq[...].astype(F32), axis=0, keepdims=True))
        fetch(j + 2)
        if layer == 1:
            dy[...] = total
            load(0, "probs", "q", "k", "v")
        else:
            d_input[...] = total

    inside = lax.broadcasted_iota(jnp.int32, (n, 1), 0) < lengths[lax.axis_index("tensor")]
    dy[...] = jnp.where(inside, grad[...].astype(F32), 0.0)
    for j, wave in enumerate(ORDER):
        layer, i = wave // 6, wave % 6
        if i >= 4:
            down_stage(layer, j, i - 4)
        elif i >= 2:
            up_stage(layer, j, i - 2)
        elif i == 1:
            value_stage(layer, j)
        else:
            score_stage(layer, j)
    sums = sum_steps(terms, small_out, got, acc, (s_send, s_recv))
    sums.pop(0)()
    moving = [[step for step in item if step is not rest] for item in moving]
    while any(len(item) > 1 for item in moving):
        for item in moving:
            if len(item) > 1:
                item.pop(0)()
        if sums:
            sums.pop(0)()
    for step in [item[0] for item in moving] + sums:
        step()


def back_all(lengths, grad, full, small, saved):
    n, width = grad.shape
    heads = width // HEAD
    waves, _, _, _, _, part, cols = full.shape
    kinds = saved_kinds(n, width)
    dma = pltpu.SemaphoreType.DMA
    hbm = pl.BlockSpec(memory_space=pltpu.MemorySpace.HBM)
    vmem = pl.BlockSpec(memory_space=pltpu.VMEM)
    shape = jax.ShapeDtypeStruct
    rows = (n, width)
    return pl.pallas_call(
        back_kernel,
        out_shape=(shape(rows, F32), shape((waves, part, cols), F32), shape(small.shape, F32)),
        in_specs=[pl.BlockSpec(memory_space=pltpu.SMEM), vmem, vmem, hbm] + [hbm] * 26,
        out_specs=(vmem, vmem, vmem),
        scratch_shapes=[pltpu.VMEM(*kinds[name]) for name in SAVED]
        + [
            pltpu.VMEM(rows, F32),
            pltpu.VMEM(rows, F32),
            pltpu.VMEM(rows, BF),
            pltpu.VMEM((width, n), BF),
            pltpu.VMEM((width, n), BF),
            pltpu.VMEM(rows, BF),
            pltpu.VMEM(rows, BF),
            pltpu.VMEM(rows, BF),
            pltpu.VMEM(rows, BF),
            pltpu.VMEM((width, n), BF),
            pltpu.VMEM((width, n), BF),
            pltpu.VMEM((2, NX, NZ, NY, NC, part, cols), BF),
            pltpu.VMEM((2, NX, NZ, NY, NC, part, cols), BF),
            pltpu.VMEM((RC + 1, NX, NZ, NY, part, cols), BF),
            pltpu.VMEM((R2S, NZ, NY, part, cols // 2), BF),
            pltpu.VMEM((R2S, NX, NZ, part, cols // 2), BF),
            pltpu.VMEM((R3S, NZ, part, cols // 2), BF),
            pltpu.VMEM((R3S, NZ, part, cols // 2), BF),
            pltpu.VMEM((waves, 3, part, cols), BF),
            pltpu.VMEM((3, NX, NY, part, cols), BF),
            pltpu.VMEM((3, part, cols // 2), BF),
            pltpu.VMEM((3, part, cols // 2), BF),
            pltpu.VMEM(small.shape, F32),
            pltpu.VMEM((6,) + small.shape, F32),
            pltpu.VMEM((3,) + small.shape, F32),
            dma((6,)),
            dma((6,)),
            dma((waves + CUTS, 12)),
            dma((waves + CUTS, 12)),
            dma((8,)),
            dma((8,)),
            pltpu.SemaphoreType.REGULAR((5,)),
            dma((13,)),
            dma((2,)),
        ],
        name="back_all",
        compiler_params=pltpu.CompilerParams(
            collective_id=1, has_side_effects=True, vmem_limit_bytes=63 << 20
        ),
    )(lengths, grad, small, full, *[saved[i][name] for i in range(2) for name in SAVED])


def unpack_kernel(*refs):
    sums, small, d_input, activations = refs[:4]
    act_out, d_out = refs[4:6]
    outs = [refs[6 + 15 * i : 21 + 15 * i] for i in range(2)]
    vectors, sem = refs[36:]
    width = sums.shape[2]
    half = width // 2
    moves = [(small, vectors), (d_input, d_out), (activations, act_out)]
    for layer in range(2):
        wq, _, wk, wv, _, wo, _, _, _, wu, _, wd = outs[layer][:12]
        at = 6 * layer
        moves += [
            (sums.at[at + 2], wu.at[:, :width]),
            (sums.at[at + 3], wu.at[:, width:]),
            (sums.at[at + 4], wd.at[:, :width]),
            (sums.at[at + 5], wd.at[:, width:]),
            (sums.at[at, :, :half], wq),
            (sums.at[at, :, half:], wk),
            (sums.at[at + 1, :, :half], wv),
            (sums.at[at + 1, :, half:], wo),
        ]
    copies = [pltpu.make_async_copy(src, dst, sem.at[i]) for i, (src, dst) in enumerate(moves)]
    for copy in copies:
        copy.start()
    dp, t, n_dp = lax.axis_index("dp"), lax.axis_index("tensor"), lax.axis_size("dp")
    few, many = outs[0][1].shape[1], outs[0][10].shape[1]
    from_norm = one_hot(width, few, (2 * dp + t) * few, 0)
    from_bias = one_hot(width, few, (t * n_dp + dp) * few, 0)
    from_up = [one_hot(width, many, (t * n_dp + dp) * many - i * width, 0) for i in range(4)]
    copies[0].wait()
    biases = mm_exact(vectors[...], from_bias)
    norms = mm_exact(vectors[...], from_norm)
    for layer in range(2):
        _, bq, _, _, bv, _, bo, g1, s1, _, bu, _, bd, g2, s2 = outs[layer]
        low = 12 * layer
        for i, ref in enumerate((bq, bv)):
            ref[...] = biases[low + i : low + i + 1]
        for i, ref in enumerate((bo, g1, s1, bd, g2, s2)):
            ref[...] = norms[low + 2 + i : low + 3 + i]
    rows = [jnp.concatenate([vectors[8 + i : 9 + i, :], vectors[20 + i : 21 + i, :]], axis=0) for i in range(4)]
    total = mm_exact(rows[0], from_up[0])
    for i in range(1, 4):
        total = total + mm_exact(rows[i], from_up[i])
    for layer in range(2):
        outs[layer][10][...] = total[layer : layer + 1]
    for copy in copies[1:]:
        copy.wait()


def unpack_all(sums, small_sums, d_input, activations, teacher, student):
    hbm = pl.BlockSpec(memory_space=pltpu.MemorySpace.HBM)
    vmem = pl.BlockSpec(memory_space=pltpu.VMEM)
    shape = jax.ShapeDtypeStruct
    flat = teacher + student
    outs = pl.pallas_call(
        unpack_kernel,
        out_shape=(shape(activations.shape, BF), shape(d_input.shape, F32))
        + tuple(shape(v.shape, F32) for v in flat),
        in_specs=[hbm] * 4,
        out_specs=(vmem,) * 32,
        scratch_shapes=[pltpu.VMEM(small_sums.shape, F32), pltpu.SemaphoreType.DMA((19,))],
        name="unpack_all",
        compiler_params=pltpu.CompilerParams(vmem_limit_bytes=63 << 20),
    )(sums, small_sums, d_input, activations)
    return outs[:2], outs[2:]


def flat_params(args):
    out = [v.reshape(1, -1) if v.ndim == 1 else v for v in args]
    for i in (5, 11):
        out[i] = out[i].T
    return tuple(out)


def shaped_grads(outs, args):
    out = list(outs)
    for i in (5, 11):
        out[i] = out[i].T
    return tuple(o.reshape(v.shape) for o, v in zip(out, args))


def local_fast(n_dp, *args):
    inputs, lengths, grad_out = args[0], args[1], args[-1]
    teacher, student = args[2:17], args[17:32]
    first, second = flat_params(teacher), flat_params(student)
    full, small, activations, saved = forward_all(lengths, inputs, first, second)
    d_input, sums, small_sums = back_all(lengths, grad_out, full, small, saved)
    (activations, d_input), grads = unpack_all(sums, small_sums, d_input, activations, first, second)
    return (activations, d_input) + shaped_grads(grads[:15], teacher) + shaped_grads(grads[15:], student)


def gather_plain(shard, small):
    rows = lax.all_gather(shard, "dp", axis=1, tiled=True)
    full = lax.all_gather(rows, "tensor", axis=1, tiled=False)
    return full, lax.psum(small, AXES)


def reduce_plain(parts, small):
    outs = []
    for part in parts:
        mine = lax.psum_scatter(part.astype(F32), "tensor", scatter_dimension=0, tiled=True)[0]
        outs.append(lax.psum_scatter(mine, "dp", scatter_dimension=0, tiled=True))
    return jnp.stack(outs), lax.psum(small, AXES)


def layer_norm(residual, gain, shift):
    average = jnp.mean(residual, axis=-1, keepdims=True)
    centred = residual - average
    variance = jnp.mean(centred * centred, axis=-1, keepdims=True)
    return centred * lax.rsqrt(variance + EPS) * gain + shift


def gelu_exact(value):
    return jax.nn.gelu(value, approximate=False)


def ein(spec, a, b):
    return jnp.einsum(spec, a, b, preferred_element_type=F32)


def heads_of(value):
    return value.reshape(value.shape[0], value.shape[1], value.shape[2] // HEAD, HEAD)


def scores_of(queries, keys, valid):
    raw = ein("tqhd,tkhd->thqk", heads_of(queries), heads_of(keys)) * (HEAD**-0.5)
    return jnp.where(valid, raw, NEG)


def layer_forward(rows, groups, small, valid):
    w_attn, w_up, w_down = groups
    width = rows.shape[1]
    half = width // 2
    bq = small[0].reshape(2, 1, half)
    bv = small[1].reshape(2, 1, half)
    bo, g1, s1, bd, g2, s2 = (small[i][None, :] for i in range(2, 8))
    bu = small[8:].reshape(2, 1, -1)
    qkv = ein("nd,tdc->tnc", rows, w_attn[:, :, : 3 * half])
    queries = (qkv[:, :, :half] + bq).astype(BF)
    keys = qkv[:, :, half : 2 * half].astype(BF)
    values = (qkv[:, :, 2 * half :] + bv).astype(BF)
    scores = scores_of(queries, keys, valid)
    row_max = jnp.max(scores, axis=-1, keepdims=True)
    exponent = jnp.exp(scores - row_max)
    total = jnp.sum(exponent, axis=-1, keepdims=True)
    probs = (exponent / total).astype(BF)
    attended = ein("thqk,tkhd->tqhd", probs, heads_of(values)).astype(BF).reshape(queries.shape)
    log_sums = row_max + jnp.log(total)
    branch = ein("tnc,tdc->nd", attended, w_attn[:, :, 3 * half :])
    resid_one = rows.astype(F32) + branch + bo
    hidden = layer_norm(resid_one, g1, s1).astype(BF)
    upward = ein("nd,tdc->tnc", hidden, w_up) + bu
    active = gelu_exact(upward).astype(BF)
    resid_two = hidden.astype(F32) + ein("tnc,tdc->nd", active, w_down) + bd
    result = layer_norm(resid_two, g2, s2)
    saved = (rows, queries, keys, values, attended, log_sums, resid_one, hidden, upward, active, resid_two)
    return result, saved


def layer_backward(d_result, groups, small, saved, valid):
    w_attn, w_up, w_down = groups
    rows, queries, keys, values, attended, log_sums, resid_one, hidden, upward, active, resid_two = saved
    half = rows.shape[1] // 2
    g1, s1, g2, s2 = (small[i] for i in (3, 4, 6, 7))
    _, norm_two_back = jax.vjp(layer_norm, resid_two, g2, s2)
    d_resid_two, d_g2, d_s2 = norm_two_back(d_result)
    d_down = d_resid_two.astype(BF)
    gw_down = ein("nd,tnc->tdc", d_down, active).astype(BF)
    _, gelu_back = jax.vjp(gelu_exact, upward)
    d_up = gelu_back(ein("nd,tdc->tnc", d_down, w_down))[0].astype(BF)
    gw_up = ein("nd,tnc->tdc", hidden, d_up).astype(BF)
    d_bu = jnp.sum(d_up, axis=1, dtype=F32).reshape(4, -1)
    d_hidden = d_resid_two + ein("tnc,tdc->nd", d_up, w_up)
    _, norm_one_back = jax.vjp(layer_norm, resid_one, g1, s1)
    d_resid_one, d_g1, d_s1 = norm_one_back(d_hidden)
    d_branch = d_resid_one.astype(BF)
    gw_out = ein("nd,tnc->tdc", d_branch, attended)
    d_attended = ein("nd,tdc->tnc", d_branch, w_attn[:, :, 3 * half :]).astype(BF)
    probs = jnp.exp(scores_of(queries, keys, valid) - log_sums)
    d_probs = ein("tqhd,tkhd->thqk", heads_of(d_attended), heads_of(values))
    d_scores = (probs * (d_probs - jnp.sum(probs * d_probs, axis=-1, keepdims=True))).astype(BF)
    scale = HEAD**-0.5
    d_queries = (ein("thqk,tkhd->tqhd", d_scores, heads_of(keys)) * scale).astype(BF).reshape(queries.shape)
    d_keys = (ein("thqk,tqhd->tkhd", d_scores, heads_of(queries)) * scale).astype(BF).reshape(queries.shape)
    d_values = ein("thqk,tqhd->tkhd", probs.astype(BF), heads_of(d_attended)).astype(BF).reshape(queries.shape)
    d_qkv = jnp.concatenate([d_queries, d_keys, d_values], axis=2)
    gw_attn = jnp.concatenate([ein("nd,tnc->tdc", rows, d_qkv), gw_out], axis=2).astype(BF)
    d_input = d_resid_one + ein("tnc,tdc->nd", d_qkv, w_attn[:, :, : 3 * half])
    d_small = jnp.concatenate(
        [
            jnp.sum(d_queries, axis=1, dtype=F32).reshape(1, -1),
            jnp.sum(d_values, axis=1, dtype=F32).reshape(1, -1),
            jnp.sum(d_resid_one, axis=0)[None],
            d_g1[None],
            d_s1[None],
            jnp.sum(d_resid_two, axis=0)[None],
            d_g2[None],
            d_s2[None],
            d_bu,
        ],
        axis=0,
    )
    return d_input, (gw_attn, gw_up, gw_down), d_small


def pack_weights(args):
    query_w, _, key_w, value_w, _, out_w, _, _, _, up_w, _, down_w = args[:12]
    return jnp.stack([jnp.concatenate([query_w, key_w, value_w, out_w.T], axis=1), up_w, down_w.T])


def spread(values, where, count):
    n, m = values.shape
    block = jnp.arange(m * count) // m
    return jnp.where(block[None, :] == where, jnp.tile(values.astype(F32), (1, count)), 0.0)


def pack_small(args, dp, n_dp, t):
    query_b, value_b, up_b = args[1], args[4], args[10]
    biases = spread(jnp.concatenate([query_b, value_b], axis=0), t * n_dp + dp, 2 * n_dp)
    norms = spread(jnp.stack([args[6], args[7], args[8], args[12], args[13], args[14]]), 2 * dp + t, 2 * n_dp)
    ups = spread(up_b, t * n_dp + dp, 2 * n_dp).reshape(4, -1)
    return jnp.concatenate([biases, norms, ups], axis=0)


def take(values, where, count):
    n, width = values.shape
    m = width // count
    return lax.dynamic_slice_in_dim(values, where * m, m, 1)


def local_plain(n_dp, *args):
    inputs, lengths, grad_out = args[0], args[1], args[-1]
    teacher, student = args[2:17], args[17:32]
    dp, t = lax.axis_index("dp"), lax.axis_index("tensor")
    seq_len = inputs.shape[0]
    width = inputs.shape[1]
    half = width // 2
    my_length = lax.dynamic_index_in_dim(lengths, t, 0, keepdims=False)
    inside = jnp.arange(seq_len) < my_length
    row_mask = inside.astype(F32)[:, None]
    valid = inside[None, None, None, :]
    shard = jnp.concatenate([pack_weights(teacher), pack_weights(student)], axis=0)
    small = jnp.concatenate([pack_small(teacher, dp, n_dp, t), pack_small(student, dp, n_dp, t)], axis=0)
    full, small = gather_plain(shard, small)
    groups = [tuple(full[3 * layer + i] for i in range(3)) for layer in range(2)]
    smalls = [small[:12], small[12:]]
    result, kept_t = layer_forward(inputs, groups[0], smalls[0], valid)
    result, kept_s = layer_forward(result.astype(BF), groups[1], smalls[1], valid)
    activations = (result * row_mask).astype(BF)
    d_current = grad_out.astype(F32) * row_mask
    d_current, parts_s, small_s = layer_backward(d_current, groups[1], smalls[1], kept_s, valid)
    d_current, parts_t, small_t = layer_backward(d_current, groups[0], smalls[0], kept_t, valid)
    order = (parts_s[2], parts_s[1], parts_s[0], parts_t[2], parts_t[1], parts_t[0])
    sums, small_sums = reduce_plain(order, jnp.concatenate([small_t, small_s], axis=0))
    outs = [activations, d_current]
    for layer in range(2):
        base = 3 * (1 - layer)
        g_down, g_up, g_attn = sums[base], sums[base + 1], sums[base + 2]
        part = small_sums[12 * layer : 12 * layer + 12]
        biases = take(part[0:2], t * n_dp + dp, 2 * n_dp)
        norms = take(part[2:8], 2 * dp + t, 2 * n_dp)
        ups = take(part[8:12].reshape(1, -1), t * n_dp + dp, 2 * n_dp)
        outs += [
            g_attn[:, :half],
            biases[0:1],
            g_attn[:, half : 2 * half],
            g_attn[:, 2 * half : 3 * half],
            biases[1:2],
            g_attn[:, 3 * half :].T,
            norms[0],
            norms[1],
            norms[2],
            g_up,
            ups,
            g_down.T,
            norms[3],
            norms[4],
            norms[5],
        ]
    return tuple(outs)


def solution(mesh):
    n_dp = mesh.shape["dp"]
    fast = n_dp == NZ * NY * NC and mesh.shape["tensor"] == NX
    row = P(AXES, None)
    vec = P(AXES)
    cut_in, cut_out = P("dp", "tensor"), P("tensor", "dp")
    layer = (cut_in, cut_out, cut_in, cut_in, cut_out, cut_out, vec, vec, vec, cut_in, cut_out, cut_out, vec, vec, vec)
    return jax.shard_map(
        functools.partial(local_fast if fast else local_plain, n_dp),
        mesh=mesh,
        in_specs=(row, P("dp")) + layer + layer + (row,),
        out_specs=(row, row) + layer + layer,
        check_vma=False,
    )
```

```python
import functools

import jax
import jax.numpy as jnp
from jax import lax
from jax.experimental import pallas as pl
from jax.experimental.pallas import tpu as pltpu
from jax.sharding import PartitionSpec as P

HEAD = 64
EPS = 1e-06
NEG = -1e30
NZ, NY, NC, NX = 4, 2, 2, 2
MESH = pl.DeviceIdType.MESH
BF = jnp.bfloat16
F32 = jnp.float32
AXES = ("dp", "tensor")


def place():
    dp = lax.axis_index("dp")
    t = lax.axis_index("tensor")
    return dp // 4, lax.rem(dp // 2, 2), lax.rem(dp, 2), t


def device(z, y, c, t):
    return {"dp": z * 4 + y * 2 + c, "tensor": t}


def greet(others):
    barrier = pltpu.get_barrier_semaphore()
    for other in others:
        pl.semaphore_signal(barrier, inc=1, device_id=other, device_id_type=MESH)
    return lambda: pl.semaphore_wait(barrier, len(others))


def send(src, dst, sems, index, other):
    copy = pltpu.make_async_remote_copy(
        src_ref=src,
        dst_ref=dst,
        send_sem=sems[0].at[index],
        recv_sem=sems[1].at[index],
        device_id=other,
        device_id_type=MESH,
    )
    copy.start()
    return copy


def partners():
    z, y, c, t = place()
    core = device(z, y, 1 - c, t)
    over_x = device(z, y, c, 1 - t)
    over_y = device(z, 1 - y, c, t)
    over_z = [device(lax.rem(z + j, NZ), y, c, t) for j in range(1, NZ)]
    return core, over_x, over_y, over_z


def small_sum(src, dst, got, acc, sems):
    core, over_x, over_y, over_z = partners()
    now = src
    for step, other in enumerate((core, over_x, over_y)):
        send(now, got.at[step], sems, step, other).wait()
        acc[step] = now[...] + got[step]
        now = acc.at[step]
    copies = [send(now, got.at[3 + j], sems, 3 + j, other) for j, other in enumerate(over_z)]
    for copy in copies:
        copy.wait()
    dst[...] = now[...] + got[3] + got[4] + got[5]


def mm(a, b):
    return jnp.dot(a, b, preferred_element_type=F32)


def mm_nt(a, b):
    return lax.dot_general(a, b, (((1,), (1,)), ((), ())), preferred_element_type=F32)


def gelu_both(u):
    bell = jnp.exp(u * u * -0.5)
    t = 1.0 / (1.0 + (0.3275911 * 0.7071067811865476) * jnp.abs(u))
    tail = 1.061405429 * 0.5 * t - 1.453152027 * 0.5
    tail = tail * t + 1.421413741 * 0.5
    tail = tail * t - 0.284496736 * 0.5
    tail = (tail * t + 0.254829592 * 0.5) * t * bell
    cdf = jnp.where(u < 0, tail, 1.0 - tail)
    return u * cdf, cdf + u * bell * 0.3989422804014327


def norm_parts(r):
    average = jnp.mean(r, axis=-1, keepdims=True)
    centred = r - average
    variance = jnp.mean(centred * centred, axis=-1, keepdims=True)
    rstd = lax.rsqrt(variance + EPS)
    return centred * rstd, rstd


def block(i, n):
    return pl.ds(pl.multiple_of(i * n, n), n)


FWAVES = 12
AHEAD = 2
BULK = (5, 7, 9, 10)
SIDE = FWAVES - 1


def gather_steps(shard, full, own_sem, sems, side_sems):
    z, y, c, t = place()
    core, over_x, over_y, over_z = partners()
    half = shard.shape[2] // 2
    lo, hi = pl.ds(0, half), pl.ds(half, half)
    owns, first, second, third, last = {}, {}, {}, {}, {}

    def one(k):
        owns[k] = pltpu.make_async_copy(shard.at[k], full.at[k, t, z, y, c], own_sem.at[k])
        owns[k].start()
        first[k] = [
            send(shard.at[k], full.at[k, t, z, y, c], sems, (k, j), other)
            for j, other in enumerate(over_z)
        ]

    def two(k):
        owns[k].wait()
        for copy in first[k]:
            copy.wait()
        a = full.at[k, t, :, y, c, :, lo]
        b = full.at[k, t, :, y, c, :, hi]
        second[k] = [send(a, a, sems, (k, 3), over_y), send(b, b, sems, (k, 4), over_x)]

    def three(k):
        for copy in second[k]:
            copy.wait()
        a = full.at[k, t, :, :, c, :, lo]
        b = full.at[k, :, :, y, c, :, hi]
        third[k] = [send(a, a, sems, (k, 5), over_x), send(b, b, sems, (k, 6), over_y)]

    def four(k):
        for copy in third[k]:
            copy.wait()
        a = full.at[k, :, :, :, c]
        last[k] = send(a, a, sems, (k, 7), core)

    def five(k):
        last[k].wait()

    side = {}

    def side_one():
        owns[SIDE] = pltpu.make_async_copy(shard.at[SIDE], full.at[SIDE, t, z, y, c], own_sem.at[SIDE])
        owns[SIDE].start()
        mine = full.at[SIDE, t, z, y, c]
        side[1] = [
            send(shard.at[SIDE, :, lo], mine.at[:, lo], side_sems, 0, over_x),
            send(shard.at[SIDE, :, hi], mine.at[:, hi], side_sems, 1, over_y),
        ]

    def side_two():
        owns[SIDE].wait()
        for copy in side[1]:
            copy.wait()
        a = full.at[SIDE, :, z, y, c, :, lo]
        b = full.at[SIDE, t, z, :, c, :, hi]
        side[2] = [send(a, a, side_sems, 2, over_y), send(b, b, side_sems, 3, over_x)]

    def side_three(i):
        if i == 0:
            for copy in side[2]:
                copy.wait()
            side[3] = []
        a = full.at[SIDE, i // 2, z, i % 2, c]
        side[3] += [send(a, a, side_sems, 4 + 3 * i + j, other) for j, other in enumerate(over_z)]

    def side_four():
        for copy in side[3]:
            copy.wait()
        a = full.at[SIDE, :, :, :, c]
        last[SIDE] = send(a, a, sems, (SIDE, 7), core)

    return one, two, three, four, five, (side_one, side_two, side_three, side_four)


def sum_steps(src, dst, got, acc, sems):
    core, over_x, over_y, over_z = partners()
    flying = {}

    def begin():
        flying[0] = [send(src, got.at[0], sems, 0, core)]

    def middle(step, other):
        for copy in flying[step - 1]:
            copy.wait()
        before = src if step == 1 else acc.at[step - 2]
        acc[step - 1] = before[...] + got[step - 1]
        if step < 3:
            flying[step] = [send(acc.at[step - 1], got.at[step], sems, step, other)]
        else:
            flying[step] = [send(acc.at[2], got.at[3 + j], sems, 3 + j, o) for j, o in enumerate(over_z)]

    def end():
        for copy in flying[3]:
            copy.wait()
        dst[...] = acc[2] + got[3] + got[4] + got[5]

    return [begin, lambda: middle(1, over_x), lambda: middle(2, over_y), lambda: middle(3, None), end]


SAVED = ("x", "q", "k", "v", "probs", "o", "z1", "rstd1", "h", "g", "gp", "z2", "rstd2")


def pack_copies(raw, shard, r_bias, r_up, r_norm, sem):
    pieces = {"small": []}
    width = shard.shape[2]
    half = width // 2
    count = 0

    def copy(src, dst):
        nonlocal count
        count += 1
        return pltpu.make_async_copy(src, dst, sem.at[count - 1])

    for layer in range(2):
        wq, bq, wk, wv, bv, wo, bo, g1, s1, wu, bu, wd, bd, g2, s2 = raw[layer]
        at = 6 * layer
        pieces[f"qk{layer}"] = [copy(wq, shard.at[at, :, :half]), copy(wk, shard.at[at, :, half:])]
        pieces[f"vo{layer}"] = [copy(wv, shard.at[at + 1, :, :half]), copy(wo, shard.at[at + 1, :, half:])]
        pieces[f"u{layer}"] = [
            copy(wu.at[:, :width], shard.at[at + 2]),
            copy(wu.at[:, width:], shard.at[at + 3]),
        ]
        pieces[f"d{layer}"] = [
            copy(wd.at[:, :width], shard.at[at + 4]),
            copy(wd.at[:, width:], shard.at[at + 5]),
        ]
        pieces["small"] += [copy(bq, r_bias.at[2 * layer]), copy(bv, r_bias.at[2 * layer + 1])]
        pieces["small"] += [copy(bu, r_up.at[layer])]
        pieces["small"] += [copy(v, r_norm.at[6 * layer + i]) for i, v in enumerate((bo, g1, s1, bd, g2, s2))]
    return pieces


def one_hot(rows, columns, start, axis):
    a = lax.broadcasted_iota(jnp.int32, (rows, columns), axis)
    b = lax.broadcasted_iota(jnp.int32, (rows, columns), 1 - axis)
    return jnp.where(a == b + start, 1.0, 0.0).astype(F32)


def mm_exact(a, b):
    return jnp.dot(a, b, preferred_element_type=F32, precision=lax.Precision.HIGHEST)


def spread_small(small, r_bias, r_up, r_norm, dp, t, n_dp):
    width = small.shape[1]
    m = r_norm.shape[2]
    to_norm = one_hot(m, width, (2 * dp + t) * m, 1)
    to_bias = one_hot(m, width, (t * n_dp + dp) * m, 1)
    many = r_up.shape[2]
    biases = mm_exact(jnp.concatenate([r_bias[i].astype(F32) for i in range(4)], axis=0), to_bias)
    norms = mm_exact(jnp.concatenate([r_norm[i] for i in range(12)], axis=0), to_norm)
    ups = jnp.concatenate([r_up[i].astype(F32) for i in range(2)], axis=0)
    for layer in range(2):
        at = 12 * layer
        small[at : at + 2, :] = biases[2 * layer : 2 * layer + 2]
        small[at + 2 : at + 8, :] = norms[6 * layer : 6 * layer + 6]
    for i in range(4):
        r = mm_exact(ups, one_hot(many, width, (t * n_dp + dp) * many - i * width, 1))
        for layer in range(2):
            small[12 * layer + 8 + i : 12 * layer + 9 + i, :] = r[layer : layer + 1]


def forward_kernel(*refs):
    lengths, rows = refs[:2]
    raw = [refs[2 + 15 * i : 17 + 15 * i] for i in range(2)]
    refs = refs[32:]
    full, small_out, act_out = refs[:3]
    saves = [dict(zip(SAVED, refs[3 + 13 * i : 16 + 13 * i])) for i in range(2)]
    refs = refs[29:]
    shard, small, r_bias, r_up, r_norm, raw_sem, x_sem = refs[:7]
    refs = refs[7:]
    bufs = dict(zip(SAVED, refs[:13]))
    bias, vt, ot, r2, w_slots, got, acc, s_send, s_recv, own_sem, b_send, b_recv, c_send, c_recv, load_sem, save_sem = refs[13:]
    z, y, c, t_mine = place()
    dp = lax.axis_index("dp")
    core, over_x, over_y, over_z = partners()
    arrived = greet([core, over_x, over_y] + over_z)
    pieces = pack_copies(raw, shard, r_bias, r_up, r_norm, raw_sem)
    x_copy = pltpu.make_async_copy(rows, bufs["x"], x_sem)
    for name in ("qk0", "d1", "small", "vo0", "u0", "d0", "qk1", "vo1", "u1"):
        for copy in pieces[name]:
            copy.start()
        if name == "vo0":
            x_copy.start()
    arrived()
    one, two, three, four, five, side = gather_steps(
        shard, full, own_sem, (b_send, b_recv), (c_send, c_recv)
    )
    sums = sum_steps(small, small_out, got, acc, (s_send, s_recv))
    loads, stores = {}, {}
    n, width = rows.shape
    half = width // 2

    def packed(name):
        for copy in pieces[name]:
            copy.wait()

    packed("qk0")
    one(0)
    packed("d1")
    side[0]()
    packed("small")
    n_dp = lax.axis_size("dp")
    spread_small(small, r_bias, r_up, r_norm, dp, t_mine, n_dp)
    sums[0]()
    side[1]()
    packed("vo0")
    one(1)
    x_copy.wait()
    for name in ("u0", "d0", "qk1", "vo1", "u1"):
        packed(name)
    length = lengths[t_mine]
    inside = lax.broadcasted_iota(jnp.int32, (n, 1), 0) < length
    bias[...] = jnp.where(inside, 0.0, NEG)

    def bring(k):
        five(k)
        loads[k] = pltpu.make_async_copy(full.at[k], w_slots.at[k % 2], load_sem.at[k % 2])
        loads[k].start()

    def comm(step):
        if step + 1 < len(sums):
            sums[step + 1]()
        if step < SIDE:
            two(step)
            if step + AHEAD < SIDE:
                one(step + AHEAD)
        if step in BULK:
            side[2](BULK.index(step))
        if 0 <= step - 1 < SIDE:
            three(step - 1)
        if step == SIDE:
            side[3]()
        if 0 <= step - 2 < SIDE:
            four(step - 2)
        if 0 <= step - 3 < SIDE - 1:
            bring(step - 3)

    def weights(k):
        loads[k].wait()
        slot = w_slots.at[k % 2]
        return lambda t, lanes: slot[t, :, :, :, :, lanes].reshape(width, -1)

    def save(layer, *names):
        for name in names:
            copy = pltpu.make_async_copy(bufs[name], saves[layer][name], save_sem.at[SAVED.index(name)])
            copy.start()
            stores[name] = copy

    def free(*names):
        for name in names:
            if name in stores:
                stores.pop(name).wait()

    def vec(layer, i):
        return small_out[12 * layer + i : 12 * layer + i + 1]

    def scores_stage(layer, k):
        w = weights(k)
        x, q, kk, probs = (bufs[i] for i in ("x", "q", "k", "probs"))
        free("q", "k", "probs")
        for t in range(2):
            here = slice(t * half, (t + 1) * half)
            r = mm(x[...], w(t, slice(0, half))) + vec(layer, 0)[:, here]
            q[:, here] = r.astype(BF) * BF(HEAD**-0.5)
            kk[:, here] = mm(x[...], w(t, slice(half, width))).astype(BF)
        save(layer, "q", "k")
        lane = lax.broadcasted_iota(jnp.int32, (1, 128), 1)

        @pl.loop(0, width // 128)
        def _(p):
            kp = kk[:, block(p, 128)]
            qp = q[:, block(p, 128)]
            for head in range(2):
                qm = jnp.where((lane >= HEAD) == (head == 1), qp, BF(0))
                s = mm_nt(kp, qm) + bias[...]
                e = jnp.exp(s - jnp.max(s, axis=0, keepdims=True))
                probs[2 * p + head] = (e * (1.0 / jnp.sum(e, axis=0, keepdims=True))).astype(BF)

        save(layer, "probs")

    def attend_stage(layer, k):
        w = weights(k)
        x, v, probs, o, z1, rstd1, h = (bufs[i] for i in ("x", "v", "probs", "o", "z1", "rstd1", "h"))
        free("v", "o", "z1", "rstd1", "h")
        for t in range(2):
            here = slice(t * half, (t + 1) * half)
            r = mm(x[...], w(t, slice(0, half))) + vec(layer, 1)[:, here]
            v[:, here] = r.astype(BF)
        save(layer, "v")
        vt[...] = v[...].T

        @pl.loop(0, width // HEAD)
        def _(i):
            ot[block(i, HEAD), :] = mm(vt[block(i, HEAD), :], probs[i]).astype(BF)

        o[...] = ot[...].T
        save(layer, "o")
        r = x[...].astype(F32) + vec(layer, 2)
        for t in range(2):
            r = r + mm_nt(o[:, t * half : (t + 1) * half], w(t, slice(half, width)))
        z, rstd = norm_parts(r)
        z1[...] = z.astype(BF)
        rstd1[...] = rstd
        h[...] = (z * vec(layer, 3) + vec(layer, 4)).astype(BF)
        save(layer, "x", "z1", "rstd1", "h")

    def up_stage(layer, k, part):
        w = weights(k)
        h, g, gp = (bufs[i] for i in ("h", "g", "gp"))
        if part == 0:
            free("g", "gp")
        step = 384
        for t in range(2):

            @pl.loop(0, width // step)
            def _(i):
                at = t * 2 * width + part * width + i * step
                here = pl.ds(pl.multiple_of(part * width + i * step, step), step)
                u = mm(h[...], w(t, block(i, step)))
                bu = bu_row(layer, t, part, i, step)
                a, b = gelu_both(u + bu)
                g[t, :, here] = a.astype(BF)
                gp[t, :, here] = b.astype(BF)

        if part == 1:
            save(layer, "g", "gp")

    def bu_row(layer, t, part, i, step):
        return small_out[pl.ds(12 * layer + 8 + 2 * t + part, 1), block(i, step)]

    def down_stage(layer, k, part):
        w = weights(k)
        h, g, z2, rstd2 = (bufs[i] for i in ("h", "g", "z2", "rstd2"))
        here = slice(part * width, (part + 1) * width)
        total = None
        for t in range(2):
            r = mm_nt(g[t, :, here], w(t, slice(0, width)))
            total = r if total is None else total + r
        if part == layer:
            r2[...] = total
            return
        free("z2", "rstd2", "x")
        r = r2[...] + total + h[...].astype(F32) + vec(layer, 5)
        z, rstd = norm_parts(r)
        z2[...] = z.astype(BF)
        rstd2[...] = rstd
        result = z * vec(layer, 6) + vec(layer, 7)
        save(layer, "z2", "rstd2")
        if layer == 0:
            bufs["x"][...] = result.astype(BF)
        else:
            act_out[...] = jnp.where(inside, result, 0.0).astype(BF)

    def compute(k):
        layer, i = k // 6, k % 6
        if i == 0:
            scores_stage(layer, k)
        elif i == 1:
            attend_stage(layer, k)
        elif i < 4:
            up_stage(layer, k, i - 2)
        else:
            down_stage(layer, k, i - 4)

    for step in range(SIDE + 3):
        comm(step)
        if step >= 4:
            compute(step - 4)
    for k in (SIDE, SIDE - 1):
        bring(k)
        compute(k)
    free(*list(stores))


def saved_kinds(n, width):
    heads = width // HEAD
    return {
        "x": ((n, width), BF),
        "q": ((n, width), BF),
        "k": ((n, width), BF),
        "v": ((n, width), BF),
        "probs": ((heads, n, n), BF),
        "o": ((n, width), BF),
        "z1": ((n, width), BF),
        "rstd1": ((n, 1), F32),
        "h": ((n, width), BF),
        "g": ((2, n, 2 * width), BF),
        "gp": ((2, n, 2 * width), BF),
        "z2": ((n, width), BF),
        "rstd2": ((n, 1), F32),
    }


def forward_all(lengths, rows, teacher, student):
    n, width = rows.shape
    part = teacher[0].shape[0]
    waves, cols = FWAVES, width
    raw = teacher + student
    few, many = raw[1].shape[1], raw[10].shape[1]
    small = jax.ShapeDtypeStruct((24, width), F32)
    kinds = saved_kinds(n, width)
    dma = pltpu.SemaphoreType.DMA
    hbm = pl.BlockSpec(memory_space=pltpu.MemorySpace.HBM)
    vmem = pl.BlockSpec(memory_space=pltpu.VMEM)
    shape = jax.ShapeDtypeStruct
    outs = pl.pallas_call(
        forward_kernel,
        out_shape=(
            shape((waves, NX, NZ, NY, NC, part, cols), BF),
            shape(small.shape, F32),
            shape((n, width), BF),
        )
        + tuple(shape(*kinds[name]) for name in SAVED) * 2,
        in_specs=[pl.BlockSpec(memory_space=pltpu.SMEM)] + [hbm] * 31,
        out_specs=(hbm, vmem, vmem) + (hbm,) * 26,
        scratch_shapes=[
            pltpu.VMEM((waves, part, cols), BF),
            pltpu.VMEM(small.shape, F32),
            pltpu.VMEM((4, 1, few), BF),
            pltpu.VMEM((2, 1, many), BF),
            pltpu.VMEM((12, 1, few), F32),
            dma((34,)),
            dma(()),
        ]
        + [pltpu.VMEM(*kinds[name]) for name in SAVED]
        + [
            pltpu.VMEM((n, 1), F32),
            pltpu.VMEM((width, n), BF),
            pltpu.VMEM((width, n), BF),
            pltpu.VMEM((n, width), F32),
            pltpu.VMEM((2, NX, NZ, NY, NC, part, cols), BF),
            pltpu.VMEM((6,) + small.shape, F32),
            pltpu.VMEM((3,) + small.shape, F32),
            dma((6,)),
            dma((6,)),
            dma((waves,)),
            dma((waves, 8)),
            dma((waves, 8)),
            dma((16,)),
            dma((16,)),
            dma((2,)),
            dma((13,)),
        ],
        name="forward_all",
        compiler_params=pltpu.CompilerParams(
            collective_id=0, has_side_effects=True, vmem_limit_bytes=60 << 20
        ),
    )(lengths, rows, *raw)
    full, small, activations = outs[:3]
    saved = [dict(zip(SAVED, outs[3 + 13 * i : 16 + 13 * i])) for i in range(2)]
    return full, small, activations, saved


ORDER = [6 + i for i in (4, 5, 2, 3, 1, 0)] + [4, 5, 2, 3, 1, 0]
RC, R2S, R3S = 7, 3, 3
TURN = 1
RESTS = 16
WAITS = (1, 5, 4, 8)
LAST = FWAVES - 1
CUTS = 3


def reduce_steps(stage, rc, r2a, r2b, r3a, r3b, r4, rz, ra, rb, out, credit, sems, t_sems):
    z, y, c, t = place()
    core, over_x, over_y, over_z = partners()
    half = out.shape[2] // 2
    lo, hi = pl.ds(0, half), pl.ds(half, half)
    flying = {}

    def rest():
        pass

    def wait(key):
        for copy in flying.pop(key):
            copy.wait()

    def give(kind, other):
        pl.semaphore_signal(credit.at[kind], inc=1, device_id=other, device_id_type=MESH)

    def add(dst, *srcs):
        total = dst[...]
        for src in srcs:
            total = total + src[...]
        dst[...] = total

    def own(s, j, lanes):
        @pl.loop(0, NZ)
        def _(i):
            for a in range(NX):
                for b in range(NY):
                    for lane in lanes:
                        add(rc.at[s, a, i, b, :, lane], stage.at[j % 2, a, i, b, c, :, lane])

    def steps(j, cut=None):
        n = j if TURN < 0 or j < TURN else j - 1
        total = FWAVES - (TURN >= 0)
        key, s, s2, s3 = (j, cut), n % RC, n % R2S, n % R3S
        row = j if cut is None else FWAVES + cut
        first = cut in (None, 0)
        width = half if cut is None else half // CUTS
        at = 0 if cut is None else cut * width
        low, high = pl.ds(at, width), pl.ds(half + at, width)
        spans = [pl.ds(0, 2 * half)] if cut is None else [low, high]

        def one():
            if n >= RC and first:
                pl.semaphore_wait(credit.at[0], 1)
            flying[key] = [
                send(stage.at[j % 2, :, :, :, 1 - c, :, lanes], rc.at[s, :, :, :, :, lanes], sems, (row, i), core)
                for i, lanes in enumerate(spans)
            ]

        def two():
            wait(key)
            own(s, j, spans)
            if n >= R2S and first:
                pl.semaphore_wait(credit.at[1], 1)
                pl.semaphore_wait(credit.at[2], 1)
            flying[key] = [
                send(rc.at[s, 1 - t, :, :, :, low], r2a.at[s2, :, :, :, low], sems, (row, 2), over_x),
                send(rc.at[s, :, :, 1 - y, :, high], r2b.at[s2, :, :, :, low], sems, (row, 3), over_y),
            ]

        def three():
            wait(key)

            @pl.loop(0, NZ)
            def _(i):
                for b in range(2):
                    add(rc.at[s, t, i, b, :, low], r2a.at[s2, i, b, :, low])
                    add(rc.at[s, b, i, y, :, high], r2b.at[s2, b, i, :, low])

            if n + R2S < total:
                give(1, over_x)
                give(2, over_y)
            if n >= R3S and first:
                pl.semaphore_wait(credit.at[3], 1)
                pl.semaphore_wait(credit.at[4], 1)
            flying[key] = [
                send(rc.at[s, t, :, 1 - y, :, low], r3a.at[s3, :, :, low], sems, (row, 4), over_y),
                send(rc.at[s, 1 - t, :, y, :, high], r3b.at[s3, :, :, low], sems, (row, 5), over_x),
            ]

        def four():
            wait(key)

            @pl.loop(0, NZ)
            def _(i):
                add(rc.at[s, t, i, y, :, low], r3a.at[s3, i, :, low])
                add(rc.at[s, t, i, y, :, high], r3b.at[s3, i, :, low])

            if n + R3S < total:
                give(3, over_y)
                give(4, over_x)
            flying[key] = [
                send(
                    rc.at[s, t, lax.rem(z + i + 1, NZ), y, :, lanes],
                    r4.at[n, i, :, lanes],
                    sems,
                    (row, 6 + 3 * k + i),
                    other,
                )
                for i, other in enumerate(over_z)
                for k, lanes in enumerate(spans)
            ]

        def five():
            wait(key)
            for lanes in spans:
                value = rc[s, t, z, y, :, lanes].astype(F32)
                for i in range(3):
                    value = value + r4[n, i, :, lanes].astype(F32)
                out[ORDER[j], :, lanes] = value
            if n + RC < total:
                give(0, core)

        return [one] + [rest] * WAITS[0] + [two] + [rest] * WAITS[1] + [three] + [rest] * WAITS[2] + [four] + [rest] * WAITS[3] + [five]

    def turned(j):
        s = RC

        def one():
            flying[j] = [send(stage.at[j % 2, :, :, :, 1 - c], rc.at[s], t_sems, 0, core)]

        def two():
            wait(j)
            own(s, j, [pl.ds(0, 2 * half)])
            flying[j] = [
                send(rc.at[s, :, lax.rem(z + i + 1, NZ)], rz.at[i], t_sems, 1 + i, other)
                for i, other in enumerate(over_z)
            ]

        def three():
            wait(j)
            for a in range(NX):
                for b in range(NY):
                    add(rc.at[s, a, z, b], rz.at[0, a, b], rz.at[1, a, b], rz.at[2, a, b])
            flying[j] = [
                send(rc.at[s, 1 - t, z, :, :, lo], ra.at[0:2], t_sems, 4, over_x),
                send(rc.at[s, :, z, 1 - y, :, hi], rb.at[0:2], t_sems, 5, over_y),
            ]

        def four():
            wait(j)
            for b in range(2):
                add(rc.at[s, t, z, b, :, lo], ra.at[b])
                add(rc.at[s, b, z, y, :, hi], rb.at[b])
            flying[j] = [
                send(rc.at[s, t, z, 1 - y, :, lo], ra.at[2], t_sems, 6, over_y),
                send(rc.at[s, 1 - t, z, y, :, hi], rb.at[2], t_sems, 7, over_x),
            ]

        def five():
            wait(j)
            out[ORDER[j], :, lo] = rc[s, t, z, y, :, lo].astype(F32) + ra[2].astype(F32)
            out[ORDER[j], :, hi] = rc[s, t, z, y, :, hi].astype(F32) + rb[2].astype(F32)

        return [one, two] + [rest] * RESTS + [three, rest, rest, four, rest, rest, five]

    return steps, turned, rest


def back_kernel(*refs):
    lengths, grad, small, full = refs[:4]
    saves = [dict(zip(SAVED, refs[4 + 13 * i : 17 + 13 * i])) for i in range(2)]
    refs = refs[30:]
    d_input, out, small_out = refs[:3]
    refs = refs[3:]
    bufs = dict(zip(SAVED, refs[:13]))
    refs = refs[13:]
    dy, dr, dlo, lot, dlot, d_o, dq, dk, dv, kt, dqt = refs[:11]
    refs = refs[11:]
    w_slots, stage, rc, r2a, r2b, r3a, r3b, r4, rz, ra, rb, terms, got, acc = refs[:14]
    s_send, s_recv, b_send, b_recv, t_send, t_recv, credit, load_sem, w_sem = refs[14:]
    core, over_x, over_y, over_z = partners()
    n, width = grad.shape
    half = width // 2
    loads, w_loads = {}, {}

    def load(layer, *names):
        for name in names:
            copy = pltpu.make_async_copy(saves[layer][name], bufs[name], load_sem.at[SAVED.index(name)])
            copy.start()
            loads[name] = copy

    def need(*names):
        for name in names:
            if name in loads:
                loads.pop(name).wait()

    def fetch(j):
        if j < FWAVES:
            w_loads[j] = pltpu.make_async_copy(full.at[ORDER[j]], w_slots.at[j % 2], w_sem.at[j % 2])
            w_loads[j].start()

    def weights(j):
        w_loads[j].wait()
        slot = w_slots.at[j % 2]
        return lambda t, lanes: slot[t, :, :, :, :, lanes].reshape(width, -1)

    arrived = greet([core, over_x, over_y] + over_z)
    load(1, "z2", "rstd2")
    fetch(0)
    load(1, "g", "gp", "h", "z1", "rstd1")
    fetch(1)
    load(1, "o", "probs", "x", "v", "k", "q")
    steps, turned, rest = reduce_steps(
        stage, rc, r2a, r2b, r3a, r3b, r4, rz, ra, rb, out, credit, (b_send, b_recv), (t_send, t_recv)
    )
    moving = []

    def advance():
        for item in moving:
            item.pop(0)()
        moving[:] = [item for item in moving if item]

    def comm(j, cut=None):
        advance()
        item = turned(j) if j == TURN else steps(j, cut)
        item.pop(0)()
        moving.append(item)

    def put(j, t, lanes, value):
        stage[j % 2, t, :, :, :, :, lanes] = value.astype(BF).reshape(NZ, NY, NC, -1, value.shape[1])

    def term(layer, i, value):
        terms[12 * layer + i : 12 * layer + i + 1, :] = value

    def vec(layer, i):
        return small[12 * layer + i : 12 * layer + i + 1]

    def norm_back(layer, at, d_out, z, rstd):
        zf = z[...].astype(F32)
        dz = d_out * vec(layer, at + 1)
        a = jnp.mean(dz, axis=-1, keepdims=True)
        b = jnp.mean(dz * zf, axis=-1, keepdims=True)
        d_in = rstd[...] * (dz - a - zf * b)
        term(layer, at, jnp.sum(d_in, axis=0, keepdims=True))
        term(layer, at + 1, jnp.sum(d_out * zf, axis=0, keepdims=True))
        term(layer, at + 2, jnp.sum(d_out, axis=0, keepdims=True))
        dr[...] = d_in
        low = d_in.astype(BF)
        dlo[...] = low
        dlot[...] = low.T

    def down_stage(layer, j, part):
        g, gp = bufs["g"], bufs["gp"]
        if part == 0:
            need("z2", "rstd2")
            norm_back(layer, 5, dy[...], bufs["z2"], bufs["rstd2"])
            need("g", "gp")
            if j == 0:
                arrived()
        w = weights(j)
        here = slice(part * width, (part + 1) * width)
        for t in range(2):
            put(j, t, slice(0, width), mm(dlot[...], g[t, :, here]))
            if t == 0:
                advance()
        comm(j)
        for t in range(2):
            if t == 1:
                advance()
            du = (mm(dlo[...], w(t, slice(0, width))) * gp[t, :, here].astype(F32)).astype(BF)
            gp[t, :, here] = du
            term(layer, 8 + 2 * t + part, jnp.sum(du.astype(F32), axis=0, keepdims=True))
        fetch(j + 2)
        if part == 1 and layer == 1:
            load(0, "z2", "rstd2", "g")

    def up_stage(layer, j, part):
        h, gp = bufs["h"], bufs["gp"]
        if part == 0:
            need("h")
            lot[...] = h[...].T
        w = weights(j)
        here = slice(part * width, (part + 1) * width)
        for t in range(2):
            put(j, t, slice(0, width), mm(lot[...], gp[t, :, here]))
            if t == 0:
                advance()
        comm(j)
        for t in range(2):
            if t == 1:
                advance()
            dr[...] = dr[...] + mm_nt(gp[t, :, here], w(t, slice(0, width)))
        fetch(j + 2)
        if part == 0:
            return
        total = dr[...]
        need("z1", "rstd1")
        norm_back(layer, 2, total, bufs["z1"], bufs["rstd1"])
        if layer == 1:
            load(0, "gp", "h", "z1", "rstd1")

    lane = lax.broadcasted_iota(jnp.int32, (1, 128), 1)

    def of_head(head, value):
        return jnp.where((lane >= HEAD) == (head == 1), value, BF(0))

    def value_stage(layer, j):
        o, probs, x = bufs["o"], bufs["probs"], bufs["x"]
        w = weights(j)
        need("o", "probs", "x")
        for t in range(2):
            here = slice(t * half, (t + 1) * half)
            put(j, t, slice(half, width), mm(dlot[...], o[:, here]))
            d_o[:, here] = mm(dlo[...], w(t, slice(half, width))).astype(BF)
        lot[...] = x[...].T
        advance()

        @pl.loop(0, width // 128)
        def _(p):
            dop = d_o[:, block(p, 128)]
            total = mm(probs[2 * p], of_head(0, dop)) + mm(probs[2 * p + 1], of_head(1, dop))
            dv[:, block(p, 128)] = total.astype(BF)

        advance()
        for t in range(2):
            put(j, t, slice(0, half), mm(lot[...], dv[:, t * half : (t + 1) * half]))
        comm(j)
        total = dr[...]
        for t in range(2):
            total = total + mm_nt(dv[:, t * half : (t + 1) * half], w(t, slice(0, half)))
        dr[...] = total
        advance()
        term(layer, 1, jnp.sum(dv[...].astype(F32), axis=0, keepdims=True))
        fetch(j + 2)
        if layer == 1:
            load(0, "o", "x")

    def score_stage(layer, j):
        probs, q, k, v = (bufs[i] for i in ("probs", "q", "k", "v"))
        w = weights(j)
        need("q", "k", "v")
        kt[...] = k[...].T

        def pair(p):
            dop = d_o[:, block(p, 128)]
            qp = q[:, block(p, 128)]
            vp = v[:, block(p, 128)]
            total = None
            for head in range(2):
                dp = mm_nt(vp, of_head(head, dop))
                pr = probs[2 * p + head].astype(F32)
                delta = jnp.sum(pr * dp, axis=0, keepdims=True)
                ds = (pr * (dp - delta)).astype(BF)
                r = mm(ds, of_head(head, qp))
                total = r if total is None else total + r
                rows = block(2 * p + head, HEAD)
                dqt[rows, :] = (mm(kt[rows, :], ds) * (HEAD**-0.5)).astype(BF)
            dk[:, block(p, 128)] = total.astype(BF)

        def stage_cols(cut, n):
            for t in range(2):
                here = slice(t * half + cut * n, t * half + (cut + 1) * n)
                put(j, t, slice(cut * n, (cut + 1) * n), mm(lot[...], dq[:, here]))
                put(j, t, slice(half + cut * n, half + (cut + 1) * n), mm(lot[...], dk[:, here]))

        if j < LAST:
            for i in range(0, width // 128, 2):
                pl.loop(i, i + 2)(pair)
                advance()
            dq[...] = dqt[...].T
            stage_cols(0, half)
            comm(j)
        else:
            n = half // CUTS
            for cut in range(CUTS):

                @pl.loop(0, 2)
                def _(t):
                    p = t * CUTS + cut
                    pair(p)
                    dq[:, block(p, n)] = dqt[block(p, n), :].T

                stage_cols(cut, n)
                comm(j, cut)
        total = dr[...]
        for t in range(2):
            here = slice(t * half, (t + 1) * half)
            total = total + mm_nt(dq[:, here], w(t, slice(0, half)))
            total = total + mm_nt(dk[:, here], w(t, slice(half, width)))
        term(layer, 0, jnp.sum(dq[...].astype(F32), axis=0, keepdims=True))
        fetch(j + 2)
        if layer == 1:
            dy[...] = total
            load(0, "probs", "q", "k", "v")
        else:
            d_input[...] = total

    inside = lax.broadcasted_iota(jnp.int32, (n, 1), 0) < lengths[lax.axis_index("tensor")]
    dy[...] = jnp.where(inside, grad[...].astype(F32), 0.0)
    for j, wave in enumerate(ORDER):
        layer, i = wave // 6, wave % 6
        if i >= 4:
            down_stage(layer, j, i - 4)
        elif i >= 2:
            up_stage(layer, j, i - 2)
        elif i == 1:
            value_stage(layer, j)
        else:
            score_stage(layer, j)
    sums = sum_steps(terms, small_out, got, acc, (s_send, s_recv))
    sums.pop(0)()
    moving = [[step for step in item if step is not rest] for item in moving]
    while any(len(item) > 1 for item in moving):
        for item in moving:
            if len(item) > 1:
                item.pop(0)()
        if sums:
            sums.pop(0)()
    for step in [item[0] for item in moving] + sums:
        step()


def back_all(lengths, grad, full, small, saved):
    n, width = grad.shape
    heads = width // HEAD
    waves, _, _, _, _, part, cols = full.shape
    kinds = saved_kinds(n, width)
    dma = pltpu.SemaphoreType.DMA
    hbm = pl.BlockSpec(memory_space=pltpu.MemorySpace.HBM)
    vmem = pl.BlockSpec(memory_space=pltpu.VMEM)
    shape = jax.ShapeDtypeStruct
    rows = (n, width)
    return pl.pallas_call(
        back_kernel,
        out_shape=(shape(rows, F32), shape((waves, part, cols), F32), shape(small.shape, F32)),
        in_specs=[pl.BlockSpec(memory_space=pltpu.SMEM), vmem, vmem, hbm] + [hbm] * 26,
        out_specs=(vmem, vmem, vmem),
        scratch_shapes=[pltpu.VMEM(*kinds[name]) for name in SAVED]
        + [
            pltpu.VMEM(rows, F32),
            pltpu.VMEM(rows, F32),
            pltpu.VMEM(rows, BF),
            pltpu.VMEM((width, n), BF),
            pltpu.VMEM((width, n), BF),
            pltpu.VMEM(rows, BF),
            pltpu.VMEM(rows, BF),
            pltpu.VMEM(rows, BF),
            pltpu.VMEM(rows, BF),
            pltpu.VMEM((width, n), BF),
            pltpu.VMEM((width, n), BF),
            pltpu.VMEM((2, NX, NZ, NY, NC, part, cols), BF),
            pltpu.VMEM((2, NX, NZ, NY, NC, part, cols), BF),
            pltpu.VMEM((RC + 1, NX, NZ, NY, part, cols), BF),
            pltpu.VMEM((R2S, NZ, NY, part, cols // 2), BF),
            pltpu.VMEM((R2S, NX, NZ, part, cols // 2), BF),
            pltpu.VMEM((R3S, NZ, part, cols // 2), BF),
            pltpu.VMEM((R3S, NZ, part, cols // 2), BF),
            pltpu.VMEM((waves, 3, part, cols), BF),
            pltpu.VMEM((3, NX, NY, part, cols), BF),
            pltpu.VMEM((3, part, cols // 2), BF),
            pltpu.VMEM((3, part, cols // 2), BF),
            pltpu.VMEM(small.shape, F32),
            pltpu.VMEM((6,) + small.shape, F32),
            pltpu.VMEM((3,) + small.shape, F32),
            dma((6,)),
            dma((6,)),
            dma((waves + CUTS, 12)),
            dma((waves + CUTS, 12)),
            dma((8,)),
            dma((8,)),
            pltpu.SemaphoreType.REGULAR((5,)),
            dma((13,)),
            dma((2,)),
        ],
        name="back_all",
        compiler_params=pltpu.CompilerParams(
            collective_id=1, has_side_effects=True, vmem_limit_bytes=63 << 20
        ),
    )(lengths, grad, small, full, *[saved[i][name] for i in range(2) for name in SAVED])


def unpack_kernel(*refs):
    sums, small, d_input, activations = refs[:4]
    act_out, d_out = refs[4:6]
    outs = [refs[6 + 15 * i : 21 + 15 * i] for i in range(2)]
    vectors, sem = refs[36:]
    width = sums.shape[2]
    half = width // 2
    moves = [(small, vectors), (d_input, d_out), (activations, act_out)]
    for layer in range(2):
        wq, _, wk, wv, _, wo, _, _, _, wu, _, wd = outs[layer][:12]
        at = 6 * layer
        moves += [
            (sums.at[at + 2], wu.at[:, :width]),
            (sums.at[at + 3], wu.at[:, width:]),
            (sums.at[at + 4], wd.at[:, :width]),
            (sums.at[at + 5], wd.at[:, width:]),
            (sums.at[at, :, :half], wq),
            (sums.at[at, :, half:], wk),
            (sums.at[at + 1, :, :half], wv),
            (sums.at[at + 1, :, half:], wo),
        ]
    copies = [pltpu.make_async_copy(src, dst, sem.at[i]) for i, (src, dst) in enumerate(moves)]
    for copy in copies:
        copy.start()
    dp, t, n_dp = lax.axis_index("dp"), lax.axis_index("tensor"), lax.axis_size("dp")
    few, many = outs[0][1].shape[1], outs[0][10].shape[1]
    from_norm = one_hot(width, few, (2 * dp + t) * few, 0)
    from_bias = one_hot(width, few, (t * n_dp + dp) * few, 0)
    from_up = [one_hot(width, many, (t * n_dp + dp) * many - i * width, 0) for i in range(4)]
    copies[0].wait()
    biases = mm_exact(vectors[...], from_bias)
    norms = mm_exact(vectors[...], from_norm)
    for layer in range(2):
        _, bq, _, _, bv, _, bo, g1, s1, _, bu, _, bd, g2, s2 = outs[layer]
        low = 12 * layer
        for i, ref in enumerate((bq, bv)):
            ref[...] = biases[low + i : low + i + 1]
        for i, ref in enumerate((bo, g1, s1, bd, g2, s2)):
            ref[...] = norms[low + 2 + i : low + 3 + i]
    rows = [jnp.concatenate([vectors[8 + i : 9 + i, :], vectors[20 + i : 21 + i, :]], axis=0) for i in range(4)]
    total = mm_exact(rows[0], from_up[0])
    for i in range(1, 4):
        total = total + mm_exact(rows[i], from_up[i])
    for layer in range(2):
        outs[layer][10][...] = total[layer : layer + 1]
    for copy in copies[1:]:
        copy.wait()


def unpack_all(sums, small_sums, d_input, activations, teacher, student):
    hbm = pl.BlockSpec(memory_space=pltpu.MemorySpace.HBM)
    vmem = pl.BlockSpec(memory_space=pltpu.VMEM)
    shape = jax.ShapeDtypeStruct
    flat = teacher + student
    outs = pl.pallas_call(
        unpack_kernel,
        out_shape=(shape(activations.shape, BF), shape(d_input.shape, F32))
        + tuple(shape(v.shape, F32) for v in flat),
        in_specs=[hbm] * 4,
        out_specs=(vmem,) * 32,
        scratch_shapes=[pltpu.VMEM(small_sums.shape, F32), pltpu.SemaphoreType.DMA((19,))],
        name="unpack_all",
        compiler_params=pltpu.CompilerParams(vmem_limit_bytes=63 << 20),
    )(sums, small_sums, d_input, activations)
    return outs[:2], outs[2:]


def flat_params(args):
    out = [v.reshape(1, -1) if v.ndim == 1 else v for v in args]
    for i in (5, 11):
        out[i] = out[i].T
    return tuple(out)


def shaped_grads(outs, args):
    out = list(outs)
    for i in (5, 11):
        out[i] = out[i].T
    return tuple(o.reshape(v.shape) for o, v in zip(out, args))


def local_fast(n_dp, *args):
    inputs, lengths, grad_out = args[0], args[1], args[-1]
    teacher, student = args[2:17], args[17:32]
    first, second = flat_params(teacher), flat_params(student)
    full, small, activations, saved = forward_all(lengths, inputs, first, second)
    d_input, sums, small_sums = back_all(lengths, grad_out, full, small, saved)
    (activations, d_input), grads = unpack_all(sums, small_sums, d_input, activations, first, second)
    return (activations, d_input) + shaped_grads(grads[:15], teacher) + shaped_grads(grads[15:], student)


def gather_plain(shard, small):
    rows = lax.all_gather(shard, "dp", axis=1, tiled=True)
    full = lax.all_gather(rows, "tensor", axis=1, tiled=False)
    return full, lax.psum(small, AXES)


def reduce_plain(parts, small):
    outs = []
    for part in parts:
        mine = lax.psum_scatter(part.astype(F32), "tensor", scatter_dimension=0, tiled=True)[0]
        outs.append(lax.psum_scatter(mine, "dp", scatter_dimension=0, tiled=True))
    return jnp.stack(outs), lax.psum(small, AXES)


def layer_norm(residual, gain, shift):
    average = jnp.mean(residual, axis=-1, keepdims=True)
    centred = residual - average
    variance = jnp.mean(centred * centred, axis=-1, keepdims=True)
    return centred * lax.rsqrt(variance + EPS) * gain + shift


def gelu_exact(value):
    return jax.nn.gelu(value, approximate=False)


def ein(spec, a, b):
    return jnp.einsum(spec, a, b, preferred_element_type=F32)


def heads_of(value):
    return value.reshape(value.shape[0], value.shape[1], value.shape[2] // HEAD, HEAD)


def scores_of(queries, keys, valid):
    raw = ein("tqhd,tkhd->thqk", heads_of(queries), heads_of(keys)) * (HEAD**-0.5)
    return jnp.where(valid, raw, NEG)


def layer_forward(rows, groups, small, valid):
    w_attn, w_up, w_down = groups
    width = rows.shape[1]
    half = width // 2
    bq = small[0].reshape(2, 1, half)
    bv = small[1].reshape(2, 1, half)
    bo, g1, s1, bd, g2, s2 = (small[i][None, :] for i in range(2, 8))
    bu = small[8:].reshape(2, 1, -1)
    qkv = ein("nd,tdc->tnc", rows, w_attn[:, :, : 3 * half])
    queries = (qkv[:, :, :half] + bq).astype(BF)
    keys = qkv[:, :, half : 2 * half].astype(BF)
    values = (qkv[:, :, 2 * half :] + bv).astype(BF)
    scores = scores_of(queries, keys, valid)
    row_max = jnp.max(scores, axis=-1, keepdims=True)
    exponent = jnp.exp(scores - row_max)
    total = jnp.sum(exponent, axis=-1, keepdims=True)
    probs = (exponent / total).astype(BF)
    attended = ein("thqk,tkhd->tqhd", probs, heads_of(values)).astype(BF).reshape(queries.shape)
    log_sums = row_max + jnp.log(total)
    branch = ein("tnc,tdc->nd", attended, w_attn[:, :, 3 * half :])
    resid_one = rows.astype(F32) + branch + bo
    hidden = layer_norm(resid_one, g1, s1).astype(BF)
    upward = ein("nd,tdc->tnc", hidden, w_up) + bu
    active = gelu_exact(upward).astype(BF)
    resid_two = hidden.astype(F32) + ein("tnc,tdc->nd", active, w_down) + bd
    result = layer_norm(resid_two, g2, s2)
    saved = (rows, queries, keys, values, attended, log_sums, resid_one, hidden, upward, active, resid_two)
    return result, saved


def layer_backward(d_result, groups, small, saved, valid):
    w_attn, w_up, w_down = groups
    rows, queries, keys, values, attended, log_sums, resid_one, hidden, upward, active, resid_two = saved
    half = rows.shape[1] // 2
    g1, s1, g2, s2 = (small[i] for i in (3, 4, 6, 7))
    _, norm_two_back = jax.vjp(layer_norm, resid_two, g2, s2)
    d_resid_two, d_g2, d_s2 = norm_two_back(d_result)
    d_down = d_resid_two.astype(BF)
    gw_down = ein("nd,tnc->tdc", d_down, active).astype(BF)
    _, gelu_back = jax.vjp(gelu_exact, upward)
    d_up = gelu_back(ein("nd,tdc->tnc", d_down, w_down))[0].astype(BF)
    gw_up = ein("nd,tnc->tdc", hidden, d_up).astype(BF)
    d_bu = jnp.sum(d_up, axis=1, dtype=F32).reshape(4, -1)
    d_hidden = d_resid_two + ein("tnc,tdc->nd", d_up, w_up)
    _, norm_one_back = jax.vjp(layer_norm, resid_one, g1, s1)
    d_resid_one, d_g1, d_s1 = norm_one_back(d_hidden)
    d_branch = d_resid_one.astype(BF)
    gw_out = ein("nd,tnc->tdc", d_branch, attended)
    d_attended = ein("nd,tdc->tnc", d_branch, w_attn[:, :, 3 * half :]).astype(BF)
    probs = jnp.exp(scores_of(queries, keys, valid) - log_sums)
    d_probs = ein("tqhd,tkhd->thqk", heads_of(d_attended), heads_of(values))
    d_scores = (probs * (d_probs - jnp.sum(probs * d_probs, axis=-1, keepdims=True))).astype(BF)
    scale = HEAD**-0.5
    d_queries = (ein("thqk,tkhd->tqhd", d_scores, heads_of(keys)) * scale).astype(BF).reshape(queries.shape)
    d_keys = (ein("thqk,tqhd->tkhd", d_scores, heads_of(queries)) * scale).astype(BF).reshape(queries.shape)
    d_values = ein("thqk,tqhd->tkhd", probs.astype(BF), heads_of(d_attended)).astype(BF).reshape(queries.shape)
    d_qkv = jnp.concatenate([d_queries, d_keys, d_values], axis=2)
    gw_attn = jnp.concatenate([ein("nd,tnc->tdc", rows, d_qkv), gw_out], axis=2).astype(BF)
    d_input = d_resid_one + ein("tnc,tdc->nd", d_qkv, w_attn[:, :, : 3 * half])
    d_small = jnp.concatenate(
        [
            jnp.sum(d_queries, axis=1, dtype=F32).reshape(1, -1),
            jnp.sum(d_values, axis=1, dtype=F32).reshape(1, -1),
            jnp.sum(d_resid_one, axis=0)[None],
            d_g1[None],
            d_s1[None],
            jnp.sum(d_resid_two, axis=0)[None],
            d_g2[None],
            d_s2[None],
            d_bu,
        ],
        axis=0,
    )
    return d_input, (gw_attn, gw_up, gw_down), d_small


def pack_weights(args):
    query_w, _, key_w, value_w, _, out_w, _, _, _, up_w, _, down_w = args[:12]
    return jnp.stack([jnp.concatenate([query_w, key_w, value_w, out_w.T], axis=1), up_w, down_w.T])


def spread(values, where, count):
    n, m = values.shape
    block = jnp.arange(m * count) // m
    return jnp.where(block[None, :] == where, jnp.tile(values.astype(F32), (1, count)), 0.0)


def pack_small(args, dp, n_dp, t):
    query_b, value_b, up_b = args[1], args[4], args[10]
    biases = spread(jnp.concatenate([query_b, value_b], axis=0), t * n_dp + dp, 2 * n_dp)
    norms = spread(jnp.stack([args[6], args[7], args[8], args[12], args[13], args[14]]), 2 * dp + t, 2 * n_dp)
    ups = spread(up_b, t * n_dp + dp, 2 * n_dp).reshape(4, -1)
    return jnp.concatenate([biases, norms, ups], axis=0)


def take(values, where, count):
    n, width = values.shape
    m = width // count
    return lax.dynamic_slice_in_dim(values, where * m, m, 1)


def local_plain(n_dp, *args):
    inputs, lengths, grad_out = args[0], args[1], args[-1]
    teacher, student = args[2:17], args[17:32]
    dp, t = lax.axis_index("dp"), lax.axis_index("tensor")
    seq_len = inputs.shape[0]
    width = inputs.shape[1]
    half = width // 2
    my_length = lax.dynamic_index_in_dim(lengths, t, 0, keepdims=False)
    inside = jnp.arange(seq_len) < my_length
    row_mask = inside.astype(F32)[:, None]
    valid = inside[None, None, None, :]
    shard = jnp.concatenate([pack_weights(teacher), pack_weights(student)], axis=0)
    small = jnp.concatenate([pack_small(teacher, dp, n_dp, t), pack_small(student, dp, n_dp, t)], axis=0)
    full, small = gather_plain(shard, small)
    groups = [tuple(full[3 * layer + i] for i in range(3)) for layer in range(2)]
    smalls = [small[:12], small[12:]]
    result, kept_t = layer_forward(inputs, groups[0], smalls[0], valid)
    result, kept_s = layer_forward(result.astype(BF), groups[1], smalls[1], valid)
    activations = (result * row_mask).astype(BF)
    d_current = grad_out.astype(F32) * row_mask
    d_current, parts_s, small_s = layer_backward(d_current, groups[1], smalls[1], kept_s, valid)
    d_current, parts_t, small_t = layer_backward(d_current, groups[0], smalls[0], kept_t, valid)
    order = (parts_s[2], parts_s[1], parts_s[0], parts_t[2], parts_t[1], parts_t[0])
    sums, small_sums = reduce_plain(order, jnp.concatenate([small_t, small_s], axis=0))
    outs = [activations, d_current]
    for layer in range(2):
        base = 3 * (1 - layer)
        g_down, g_up, g_attn = sums[base], sums[base + 1], sums[base + 2]
        part = small_sums[12 * layer : 12 * layer + 12]
        biases = take(part[0:2], t * n_dp + dp, 2 * n_dp)
        norms = take(part[2:8], 2 * dp + t, 2 * n_dp)
        ups = take(part[8:12].reshape(1, -1), t * n_dp + dp, 2 * n_dp)
        outs += [
            g_attn[:, :half],
            biases[0:1],
            g_attn[:, half : 2 * half],
            g_attn[:, 2 * half : 3 * half],
            biases[1:2],
            g_attn[:, 3 * half :].T,
            norms[0],
            norms[1],
            norms[2],
            g_up,
            ups,
            g_down.T,
            norms[3],
            norms[4],
            norms[5],
        ]
    return tuple(outs)


def solution(mesh):
    n_dp = mesh.shape["dp"]
    fast = n_dp == NZ * NY * NC and mesh.shape["tensor"] == NX
    row = P(AXES, None)
    vec = P(AXES)
    cut_in, cut_out = P("dp", "tensor"), P("tensor", "dp")
    layer = (cut_in, cut_out, cut_in, cut_in, cut_out, cut_out, vec, vec, vec, cut_in, cut_out, cut_out, vec, vec, vec)
    return jax.shard_map(
        functools.partial(local_fast if fast else local_plain, n_dp),
        mesh=mesh,
        in_specs=(row, P("dp")) + layer + layer + (row,),
        out_specs=(row, row) + layer + layer,
        check_vma=False,
    )
```
